768 devices in a mesh: lat: 64 (over x, z_hi, y), lon: 12 (over z_lo, core).
Axes of the slice: x: 4, y: 8, z: 12 (z_hi: 2, z_lo: 6; z = z_hi * 6 + z_lo), core: 2. Of those that a mesh axis runs over, the one named last changes fastest.
Arguments:
- tracers: float32 [5, 16, 576, 1440], P(None, None, 'lat', 'lon'), may hold values from -6 to 6
- zonal_wind: float32 [16, 576, 1440], P(None, 'lat', 'lon'), may hold values from -0.45 to 0.45
- meridional_wind: float32 [16, 576, 1440], P(None, 'lat', 'lon'), may hold values from -0.45 to 0.45
- cutoff: int32 [576], P('lat'), may hold values from 1 to 720, as said below
Outputs:
- filtered: float32 [5, 16, 576, 1440], P(None, None, 'lat', 'lon')
The draws below stay inside these ranges and needn't reach their ends.
Inputs may be any that keep to these rules, and one draw needn't show every extreme that they name: cutoff is 720 on every row at least 96 rows from both poles and below it on the rows nearer a pole; it is 1 on row 0 and row 575.
All inputs are finite; a program needn't handle non-finite values.
Results may differ from the reference program's by a relative error of at most 0.000075.
Values sent between devices are 32-bit elements; how exact they have to be, the bound alone decides.
A program may use at most 32 MiB of HBM per device.

```python
import jax
import jax.numpy as jnp

NLON = 1440
F = 5
LEV = 16
NLAT = 576
POLAR = 96


def draw_cutoff(key, part):
    row_index = jnp.arange(NLAT, dtype=jnp.int32)
    distance = jnp.minimum(row_index, NLAT - 1 - row_index)
    half_lon = NLON // 2
    jitter = jax.random.randint(key, (NLAT,), -4, 5).astype(jnp.int32)
    base_value = distance * (half_lon - 1) // POLAR
    values = jnp.clip(base_value + jitter, 1, half_lon - 1)
    values = jnp.where(distance == 0, 1, values)
    values = jnp.where(distance >= POLAR, half_lon, values)
    return values.astype(jnp.int32)


def level_of(rng, dims, split, least, largest):
    loudness = 1.0
    for dim, shards_of in split:
        steps = jax.random.uniform(jax.random.fold_in(jax.random.fold_in(rng, 6), dim), (shards_of,), jnp.float32, least / len(split), largest / len(split))
        loudness = loudness * jnp.repeat(jnp.exp(steps), dims[dim] // shards_of).reshape((-1,) + (1,) * (len(dims) - 1 - dim))
    return loudness


def normal_values(key, dims, scale, most, cuts=(), kind=jnp.bfloat16):
    factor_of = level_of(key, dims, cuts, -0.22, 0.18) if cuts else 1.0
    values = jax.random.normal(key, dims, jnp.float32) * scale * factor_of
    return jnp.minimum(jnp.maximum(values, -most), most).astype(kind)


def setup_inputs(seed: int = 0) -> dict:
    streams_of = jax.random.split(jax.random.key(seed), 5)
    return {
        "tracers": normal_values(streams_of[0], (F, LEV, NLAT, NLON), 1.0, 6.0, ((2, 64), (3, 12)), jnp.float32),
        "zonal_wind": jnp.clip(jax.random.uniform(streams_of[1], (LEV, NLAT, NLON), jnp.float32, -0.45, 0.45) * level_of(streams_of[1], (LEV, NLAT, NLON), ((1, 64), (2, 12)), -0.4, 0.0), -0.45, 0.45),
        "meridional_wind": jnp.clip(jax.random.uniform(streams_of[2], (LEV, NLAT, NLON), jnp.float32, -0.45, 0.45) * level_of(streams_of[2], (LEV, NLAT, NLON), ((1, 64), (2, 12)), -0.4, 0.0), -0.45, 0.45),
        "cutoff": draw_cutoff(jax.random.fold_in(streams_of[4], 71), 0),
    }


def extend(field, flip):
    half_lon = field.shape[-1] // 2
    north = jnp.roll(field[..., :1, :], half_lon, axis=-1) * flip
    south = jnp.roll(field[..., -1:, :], half_lon, axis=-1) * flip
    padded = jnp.concatenate([north, field, south], axis=-2)
    return jnp.concatenate([padded[..., -1:], padded, padded[..., :1]], axis=-1)


def advect(q_pad, u_pad, v_pad):
    center = q_pad[..., 1:-1, 1:-1]
    u_mid = u_pad[..., 1:-1, 1:-1]
    east_speed = 0.5 * (u_mid + u_pad[..., 1:-1, 2:])
    west_speed = 0.5 * (u_pad[..., 1:-1, :-2] + u_mid)
    east_flux = jnp.maximum(east_speed, 0.0) * center + jnp.minimum(east_speed, 0.0) * q_pad[..., 1:-1, 2:]
    west_flux = jnp.maximum(west_speed, 0.0) * q_pad[..., 1:-1, :-2] + jnp.minimum(west_speed, 0.0) * center
    v_mid = v_pad[..., 1:-1, 1:-1]
    south_speed = 0.5 * (v_mid + v_pad[..., 2:, 1:-1])
    north_speed = 0.5 * (v_pad[..., :-2, 1:-1] + v_mid)
    south_flux = jnp.maximum(south_speed, 0.0) * center + jnp.minimum(south_speed, 0.0) * q_pad[..., 2:, 1:-1]
    north_flux = jnp.maximum(north_speed, 0.0) * q_pad[..., :-2, 1:-1] + jnp.minimum(north_speed, 0.0) * center
    return center - (east_flux - west_flux) - (south_flux - north_flux)


def reference(tracers, zonal_wind, meridional_wind, cutoff):
    stepped = advect(extend(tracers, 1.0), extend(zonal_wind, 1.0), extend(meridional_wind, -1.0))
    spectrum = jnp.fft.rfft(stepped, axis=-1)
    wave_number = jnp.arange(NLON // 2 + 1).astype(jnp.int32)
    keep = wave_number[None, :] <= cutoff.astype(jnp.int32)[:, None]
    spectrum = jnp.where(keep, spectrum, 0.0)
    return jnp.fft.irfft(spectrum, n=NLON, axis=-1).astype(jnp.float32)
```

```python
import functools
import math

import jax
import jax.numpy as jnp
import ml_dtypes
import numpy as np
from jax import lax
from jax.experimental import pallas as pl
from jax.experimental.pallas import tpu as pltpu
from jax.sharding import PartitionSpec as P

MESH = pl.DeviceIdType.MESH
POLAR_ROWS = 96
SECTORS = 12
LANES = 128


def split_bf16(table):
    high = table.astype(ml_dtypes.bfloat16)
    low = (table - high.astype(np.float64)).astype(ml_dtypes.bfloat16)
    return high, low


@functools.lru_cache(maxsize=None)
def dft_tables(circle, sector):
    forward = np.zeros((6, 256, 256))
    inverse = np.zeros((6, 256, 256))
    waves = np.zeros((8, 256))
    m = np.arange(sector)

    def put(block, column, k, part, weight, real_half):
        phase = 2.0 * math.pi * ((m * k) % circle) / circle
        cos, sin = np.cos(phase), np.sin(phase)
        waves[block, column] = min(k, circle - k)
        if real_half is not None:
            base = 128 * real_half
            row = cos if part == 0 else -sin
            forward[block, base : base + sector, column] = row
            inverse[block, column, base : base + sector] = weight * row / circle
            return
        if part == 0:
            forward[block, :sector, column] = cos
            forward[block, 128 : 128 + sector, column] = sin
            inverse[block, column, :sector] = weight * cos / circle
            inverse[block, column, 128 : 128 + sector] = weight * sin / circle
        else:
            forward[block, :sector, column] = -sin
            forward[block, 128 : 128 + sector, column] = cos
            inverse[block, column, :sector] = -weight * sin / circle
            inverse[block, column, 128 : 128 + sector] = weight * cos / circle

    half = sector // 2
    for q in range(half + 1):
        put(0, q, SECTORS * q, 0, 1.0 if q in (0, half) else 2.0, 0)
    for q in range(1, half):
        put(0, half + q, SECTORS * q, 1, 2.0, 0)
    for q in range(half):
        put(0, 128 + q, 6 + SECTORS * q, 0, 2.0, 1)
        put(0, 128 + half + q, 6 + SECTORS * q, 1, 2.0, 1)
    for r in range(1, 6):
        for q in range(sector):
            put(r, q, r + SECTORS * q, 0, 2.0, None)
            put(r, 128 + q, r + SECTORS * q, 1, 2.0, None)
    return split_bf16(forward) + split_bf16(inverse) + (waves.astype(np.int32),)


def combine(terms):
    groups = {}
    for coefficient, array in terms:
        size = round(abs(coefficient), 6)
        if size < 1e-6:
            continue
        groups.setdefault(size, []).append((coefficient, array))
    total = None
    for size in sorted(groups, reverse=True):
        part = None
        for coefficient, array in groups[size]:
            if part is None:
                part = array if coefficient > 0 else -array
            else:
                part = part + array if coefficient > 0 else part - array
        if size != 1.0:
            part = part * abs(groups[size][0][0])
        total = part if total is None else total + part
    return total


def cos12(i):
    return math.cos(2.0 * math.pi * (i % 12) / 12)


def sin12(i):
    return math.sin(2.0 * math.pi * (i % 12) / 12)


def sector_dft(x):
    sums = [None] + [x[j] + x[12 - j] for j in range(1, 6)]
    differences = [None] + [x[j] - x[12 - j] for j in range(1, 6)]
    real, imag = [], []
    for r in range(7):
        terms = [(1.0, x[0]), (1.0 if r % 2 == 0 else -1.0, x[6])]
        terms += [(cos12(j * r), sums[j]) for j in range(1, 6)]
        real.append(combine(terms))
        if 0 < r < 6:
            imag.append(combine([(-sin12(j * r), differences[j]) for j in range(1, 6)]))
        else:
            imag.append(None)
    return [(real[0], real[6])] + [(real[r], imag[r]) for r in range(1, 6)]


def sector_inverse(w):
    out = [None] * 12
    for j in range(7):
        terms = [(1.0, w[0][0]), (1.0 if j % 2 == 0 else -1.0, w[0][1])]
        terms += [(cos12(j * r), w[r][0]) for r in range(1, 6)]
        even = combine(terms)
        if j in (0, 6):
            out[j] = even
            continue
        odd = combine([(sin12(j * r), w[r][1]) for r in range(1, 6)])
        out[j] = even - odd
        out[12 - j] = even + odd
    return out


def split_dot(x, high, low):
    x_high = x.astype(jnp.bfloat16)
    x_low = (x - x_high.astype(jnp.float32)).astype(jnp.bfloat16)
    dot = functools.partial(jnp.dot, preferred_element_type=jnp.float32)
    return dot(x_high, high) + (dot(x_low, high) + dot(x_high, low))


def kernel(
    lat_count, fields, rows,
    q_hbm, u_hbm, v_hbm, cut_ref, fh_hbm, fl_hbm, ih_hbm, il_hbm, waves_ref,
    out_ref,
    q_in, u_in, v_in, q_pad, u_pad, v_pad, edge_out, edge_in, side_out, side_in,
    fh, fl, ih, il, stepped, land, done, result,
    load_sem, table_sem, halo_send, halo_recv, go_send, go_recv, back_send, back_recv,
):
    lat, lon = lax.axis_index("lat"), lax.axis_index("lon")
    chip, core = lon // 2, lax.rem(lon, 2)
    slabs = fields * rows
    tiles = 2 * slabs
    first = 15 * chip + 8 * core
    low_edge, high_edge = lat == 0, lat == lat_count - 1
    polar = jnp.logical_or(
        lat * rows < POLAR_ROWS, (lat_count - 1 - lat) * rows < POLAR_ROWS
    )
    across = lax.rem(lon + 6, SECTORS)
    north = (jnp.where(low_edge, 0, lat - 1), jnp.where(low_edge, across, lon))
    south = (jnp.where(high_edge, lat, lat + 1), jnp.where(high_edge, across, lon))
    west = (lat, lax.rem(lon + SECTORS - 1, SECTORS))
    east = (lat, lax.rem(lon + 1, SECTORS))

    loads = [
        pltpu.make_async_copy(q_hbm, q_in, load_sem.at[0]),
        pltpu.make_async_copy(u_hbm, u_in, load_sem.at[1]),
        pltpu.make_async_copy(v_hbm, v_in, load_sem.at[2]),
    ]
    for load in loads:
        load.start()
    tables = [
        pltpu.make_async_copy(source, target, table_sem.at[i])
        for i, (source, target) in enumerate(((fh_hbm, fh), (fl_hbm, fl), (ih_hbm, ih), (il_hbm, il)))
    ]

    barrier = pltpu.get_barrier_semaphore()
    for target in (north, south, west, east):
        pl.semaphore_signal(barrier, inc=1, device_id=target, device_id_type=MESH)

    @pl.when(polar)
    def _():
        for offset in range(2, SECTORS - 1):
            pl.semaphore_signal(
                barrier, inc=1, device_id=(lat, lax.rem(lon + offset, SECTORS)), device_id_type=MESH
            )
        for table in tables:
            table.start()

    for load in loads:
        load.wait()

    sector = q_in.shape[-1]
    lane = lax.broadcasted_iota(jnp.int32, (16, LANES), 1)
    east_pack = jnp.zeros((16, LANES), jnp.float32)
    west_pack = jnp.zeros((16, LANES), jnp.float32)
    for f in range(fields + 1):
        for r in range(rows):
            s = f * rows + r
            source, pad = (q_in.at[f], q_pad.at[f]) if f < fields else (u_in, u_pad)
            pad[r, :, pl.ds(0, sector)] = source[r]
            x = pad[r]
            west_pack = jnp.where(lane == s, pltpu.roll(x, s, 1), west_pack)
            east_pack = jnp.where(
                lane == s, pltpu.roll(x, (s - (sector - 1)) % LANES, 1), east_pack
            )
    for r in range(rows):
        v_pad[r, :, pl.ds(0, sector)] = v_in[r]
    side_out[0] = west_pack
    side_out[1] = east_pack
    for side, row in ((0, 0), (1, rows - 1)):
        for f in range(fields):
            edge_out[side, f] = q_pad[f, row]
        edge_out[side, fields] = v_pad[row]

    @pl.when(polar)
    def _():
        pl.semaphore_wait(barrier, 4 + SECTORS - 3)

    @pl.when(jnp.logical_not(polar))
    def _():
        pl.semaphore_wait(barrier, 4)

    def edge_copy(side, slot, target):
        return pltpu.make_async_remote_copy(
            src_ref=edge_out.at[side],
            dst_ref=edge_in.at[slot],
            send_sem=halo_send.at[side],
            recv_sem=halo_recv.at[slot],
            device_id=target,
            device_id_type=MESH,
        )

    to_north = edge_copy(0, jnp.where(low_edge, 0, 1), north)
    to_south = edge_copy(1, jnp.where(high_edge, 1, 0), south)
    to_west = pltpu.make_async_remote_copy(
        src_ref=side_out.at[0], dst_ref=side_in.at[1], send_sem=halo_send.at[2],
        recv_sem=halo_recv.at[2], device_id=west, device_id_type=MESH,
    )
    to_east = pltpu.make_async_remote_copy(
        src_ref=side_out.at[1], dst_ref=side_in.at[0], send_sem=halo_send.at[3],
        recv_sem=halo_recv.at[3], device_id=east, device_id_type=MESH,
    )
    for copy in (to_north, to_south, to_west, to_east):
        copy.start()
    to_west.wait_recv()
    to_east.wait_recv()
    edge_copy(0, 0, north).wait_recv()
    edge_copy(1, 1, south).wait_recv()

    from_west, from_east = side_in[0], side_in[1]

    def with_ghosts(x, s):
        x = jnp.where(lane == sector, pltpu.roll(from_east, (sector - s) % LANES, 1), x)
        return jnp.where(lane == LANES - 1, pltpu.roll(from_west, (LANES - 1 - s) % LANES, 1), x)

    flip_north = jnp.where(low_edge, -1.0, 1.0)
    flip_south = jnp.where(high_edge, -1.0, 1.0)
    for r in range(rows):
        u = with_ghosts(u_pad[r], fields * rows + r)
        east_speed = 0.5 * (u + pltpu.roll(u, LANES - 1, 1))
        west_speed = 0.5 * (pltpu.roll(u, 1, 1) + u)
        v = v_pad[r]
        v_next = v_pad[r + 1] if r < rows - 1 else edge_in[1, fields] * flip_south
        v_previous = v_pad[r - 1] if r > 0 else edge_in[0, fields] * flip_north
        south_speed = 0.5 * (v + v_next)
        north_speed = 0.5 * (v_previous + v)
        e_plus, e_minus = jnp.maximum(east_speed, 0.0), jnp.minimum(east_speed, 0.0)
        w_plus, w_minus = jnp.maximum(west_speed, 0.0), jnp.minimum(west_speed, 0.0)
        s_plus, s_minus = jnp.maximum(south_speed, 0.0), jnp.minimum(south_speed, 0.0)
        n_plus, n_minus = jnp.maximum(north_speed, 0.0), jnp.minimum(north_speed, 0.0)
        for f in range(fields):
            q = with_ghosts(q_pad[f, r], f * rows + r)
            q_next = q_pad[f, r + 1] if r < rows - 1 else edge_in[1, f]
            q_previous = q_pad[f, r - 1] if r > 0 else edge_in[0, f]
            east_flux = e_plus * q + e_minus * pltpu.roll(q, LANES - 1, 1)
            west_flux = w_plus * pltpu.roll(q, 1, 1) + w_minus * q
            south_flux = s_plus * q + s_minus * q_next
            north_flux = n_plus * q_previous + n_minus * q
            new = q - (east_flux - west_flux) - (south_flux - north_flux)
            new = jnp.where(lane < sector, new, 0.0)
            tile = 2 * (f * rows + r)
            stepped[tile] = new[:8]
            stepped[tile + 1] = new[8:]

    @pl.when(jnp.logical_not(polar))
    def _():
        out_ref[...] = stepped[pl.ds(0, tiles)]

    def peers():
        for offset in range(1, 6):
            for c in range(2):
                to_chip = lax.rem(chip + offset, 6)
                yield to_chip, c, 2 * to_chip + c

    def waiter(ref, sem):
        return pltpu.make_async_copy(ref, ref, sem)

    @pl.when(polar)
    def _():
        counts = ((4, 4), (4, 3))
        starts = (0, 4)

        def go(phase, to_first, count, to):
            pltpu.make_async_remote_copy(
                src_ref=stepped.at[pl.ds(to_first + starts[phase], count)],
                dst_ref=land.at[lon, pl.ds(starts[phase], count)],
                send_sem=go_send.at[phase], recv_sem=go_recv.at[phase],
                device_id=(lat, to), device_id_type=MESH,
            ).start()

        def back(phase, count, to):
            pltpu.make_async_remote_copy(
                src_ref=done.at[to, pl.ds(starts[phase], count)],
                dst_ref=result.at[pl.ds(first + starts[phase], count)],
                send_sem=back_send.at[phase], recv_sem=back_recv.at[phase],
                device_id=(lat, to), device_id_type=MESH,
            ).start()

        for phase in range(2):
            for to_chip, c, to in peers():
                go(phase, 15 * to_chip + 8 * c, counts[c][phase], to)
            for c in range(2):
                @pl.when(core == 1 - c)
                def _():
                    go(phase, 15 * chip + 8 * c, counts[c][phase], 2 * chip + c)

        land[lon] = stepped[pl.ds(first, 8)]
        for table in tables:
            table.wait()

        for phase in range(2):
            for c in range(2):
                @pl.when(core == c)
                def _():
                    count = counts[c][phase]
                    waiter(land.at[pl.ds(0, 11), pl.ds(0, count)], go_recv.at[phase]).wait()
            x = [land[j, pl.ds(starts[phase], 4)].reshape(32, LANES) for j in range(SECTORS)]
            limit = [cut_ref[lax.rem((first + starts[phase] + i) // 2, rows)] for i in range(4)]
            w = []
            for block, (a, b) in enumerate(sector_dft(x)):
                z = split_dot(jnp.concatenate([a, b], axis=1), fh[block], fl[block])
                wave = jnp.broadcast_to(waves_ref[pl.ds(block, 1)], (8, 256))
                z = jnp.concatenate(
                    [jnp.where(wave <= limit[i], z[8 * i : 8 * i + 8], 0.0) for i in range(4)], axis=0
                )
                y = split_dot(z, ih[block], il[block])
                w.append((y[:, :LANES], y[:, LANES:]))
            for j, y in enumerate(sector_inverse(w)):
                done[j, pl.ds(starts[phase], 4)] = y.reshape(4, 8, LANES)
            for c in range(2):
                @pl.when(core == c)
                def _():
                    count = counts[c][phase]
                    for _, _, to in peers():
                        back(phase, count, to)
                    back(phase, count, lon + 1 - 2 * c)
                    result[pl.ds(first + starts[phase], count)] = done[lon, pl.ds(starts[phase], count)]

        waiter(result.at[pl.ds(0, 44)], back_recv.at[0]).wait()
        for c in range(2):
            @pl.when(core == c)
            def _():
                waiter(result.at[pl.ds(0, 35 + counts[1 - c][1])], back_recv.at[1]).wait()
                waiter(stepped.at[pl.ds(0, 35 + counts[1 - c][1])], go_send.at[1]).wait()
                waiter(done.at[pl.ds(0, 11), pl.ds(0, counts[c][1])], back_send.at[1]).wait()
        waiter(stepped.at[pl.ds(0, 44)], go_send.at[0]).wait()
        waiter(done.at[pl.ds(0, 11), pl.ds(0, 4)], back_send.at[0]).wait()
        out_ref[...] = result[pl.ds(0, tiles)]

    for copy in (to_north, to_south, to_west, to_east):
        copy.wait_send()


def body(lat_count, tracers, zonal_wind, meridional_wind, cutoff):
    fields, levels, rows, sector = tracers.shape
    q = jnp.transpose(tracers, (0, 2, 1, 3))
    u = jnp.transpose(zonal_wind, (1, 0, 2))
    v = jnp.transpose(meridional_wind, (1, 0, 2))
    tables = [jnp.asarray(t) for t in dft_tables(SECTORS * sector, sector)]
    tiles = fields * rows * 2
    f32, bf16 = jnp.float32, jnp.bfloat16
    dma = pltpu.SemaphoreType.DMA
    anywhere = pl.BlockSpec(memory_space=pl.ANY)
    vmem = pl.BlockSpec(memory_space=pltpu.VMEM)
    out = pl.pallas_call(
        functools.partial(kernel, lat_count, fields, rows),
        out_shape=jax.ShapeDtypeStruct((tiles, 8, LANES), f32),
        in_specs=[anywhere] * 3 + [pl.BlockSpec(memory_space=pltpu.SMEM)] + [anywhere] * 4 + [vmem],
        out_specs=vmem,
        scratch_shapes=[
            pltpu.VMEM((fields, rows, levels, sector), f32),
            pltpu.VMEM((rows, levels, sector), f32),
            pltpu.VMEM((rows, levels, sector), f32),
            pltpu.VMEM((fields, rows, levels, LANES), f32),
            pltpu.VMEM((rows, levels, LANES), f32),
            pltpu.VMEM((rows, levels, LANES), f32),
            pltpu.VMEM((2, fields + 1, levels, LANES), f32),
            pltpu.VMEM((2, fields + 1, levels, LANES), f32),
            pltpu.VMEM((2, levels, LANES), f32),
            pltpu.VMEM((2, levels, LANES), f32),
            pltpu.VMEM((6, 256, 256), bf16),
            pltpu.VMEM((6, 256, 256), bf16),
            pltpu.VMEM((6, 256, 256), bf16),
            pltpu.VMEM((6, 256, 256), bf16),
            pltpu.VMEM((96, 8, LANES), f32),
            pltpu.VMEM((SECTORS, 8, 8, LANES), f32),
            pltpu.VMEM((SECTORS, 8, 8, LANES), f32),
            pltpu.VMEM((96, 8, LANES), f32),
            dma((3,)), dma((4,)), dma((4,)), dma((4,)), dma((2,)), dma((2,)), dma((2,)), dma((2,)),
        ],
        compiler_params=pltpu.CompilerParams(
            collective_id=0, has_side_effects=True, vmem_limit_bytes=40 * 1024 * 1024
        ),
    )(q, u, v, cutoff, *tables)
    out = out.reshape(fields, rows, levels, LANES)[..., :sector]
    return jnp.transpose(out, (0, 2, 1, 3))


def solution(mesh):
    in_specs = (P(None, None, "lat", "lon"), P(None, "lat", "lon"), P(None, "lat", "lon"), P("lat"))
    out_specs = P(None, None, "lat", "lon")
    return jax.shard_map(
        functools.partial(body, mesh.shape["lat"]),
        mesh=mesh, in_specs=in_specs, out_specs=out_specs, check_vma=False,
    )
```

```python
import functools
import math

import jax
import jax.numpy as jnp
import ml_dtypes
import numpy as np
from jax import lax
from jax.experimental import pallas as pl
from jax.experimental.pallas import tpu as pltpu
from jax.sharding import PartitionSpec as P

MESH = pl.DeviceIdType.MESH
POLAR_ROWS = 96
SECTORS = 12
LANES = 128


def split_bf16(table):
    high = table.astype(ml_dtypes.bfloat16)
    low = (table - high.astype(np.float64)).astype(ml_dtypes.bfloat16)
    return high, low


@functools.lru_cache(maxsize=None)
def dft_tables(circle, sector):
    forward = np.zeros((6, 256, 256))
    inverse = np.zeros((6, 256, 256))
    waves = np.zeros((8, 256))
    m = np.arange(sector)

    def put(block, column, k, part, weight, real_half):
        phase = 2.0 * math.pi * ((m * k) % circle) / circle
        cos, sin = np.cos(phase), np.sin(phase)
        waves[block, column] = min(k, circle - k)
        if real_half is not None:
            base = 128 * real_half
            row = cos if part == 0 else -sin
            forward[block, base : base + sector, column] = row
            inverse[block, column, base : base + sector] = weight * row / circle
            return
        if part == 0:
            forward[block, :sector, column] = cos
            forward[block, 128 : 128 + sector, column] = sin
            inverse[block, column, :sector] = weight * cos / circle
            inverse[block, column, 128 : 128 + sector] = weight * sin / circle
        else:
            forward[block, :sector, column] = -sin
            forward[block, 128 : 128 + sector, column] = cos
            inverse[block, column, :sector] = -weight * sin / circle
            inverse[block, column, 128 : 128 + sector] = weight * cos / circle

    half = sector // 2
    for q in range(half + 1):
        put(0, q, SECTORS * q, 0, 1.0 if q in (0, half) else 2.0, 0)
    for q in range(1, half):
        put(0, half + q, SECTORS * q, 1, 2.0, 0)
    for q in range(half):
        put(0, 128 + q, 6 + SECTORS * q, 0, 2.0, 1)
        put(0, 128 + half + q, 6 + SECTORS * q, 1, 2.0, 1)
    for r in range(1, 6):
        for q in range(sector):
            put(r, q, r + SECTORS * q, 0, 2.0, None)
            put(r, 128 + q, r + SECTORS * q, 1, 2.0, None)
    return split_bf16(forward) + split_bf16(inverse) + (waves.astype(np.int32),)


def combine(terms):
    groups = {}
    for coefficient, array in terms:
        size = round(abs(coefficient), 6)
        if size < 1e-6:
            continue
        groups.setdefault(size, []).append((coefficient, array))
    total = None
    for size in sorted(groups, reverse=True):
        part = None
        for coefficient, array in groups[size]:
            if part is None:
                part = array if coefficient > 0 else -array
            else:
                part = part + array if coefficient > 0 else part - array
        if size != 1.0:
            part = part * abs(groups[size][0][0])
        total = part if total is None else total + part
    return total


def cos12(i):
    return math.cos(2.0 * math.pi * (i % 12) / 12)


def sin12(i):
    return math.sin(2.0 * math.pi * (i % 12) / 12)


def sector_dft(x):
    sums = [None] + [x[j] + x[12 - j] for j in range(1, 6)]
    differences = [None] + [x[j] - x[12 - j] for j in range(1, 6)]
    real, imag = [], []
    for r in range(7):
        terms = [(1.0, x[0]), (1.0 if r % 2 == 0 else -1.0, x[6])]
        terms += [(cos12(j * r), sums[j]) for j in range(1, 6)]
        real.append(combine(terms))
        if 0 < r < 6:
            imag.append(combine([(-sin12(j * r), differences[j]) for j in range(1, 6)]))
        else:
            imag.append(None)
    return [(real[0], real[6])] + [(real[r], imag[r]) for r in range(1, 6)]


def sector_inverse(w):
    out = [None] * 12
    for j in range(7):
        terms = [(1.0, w[0][0]), (1.0 if j % 2 == 0 else -1.0, w[0][1])]
        terms += [(cos12(j * r), w[r][0]) for r in range(1, 6)]
        even = combine(terms)
        if j in (0, 6):
            out[j] = even
            continue
        odd = combine([(sin12(j * r), w[r][1]) for r in range(1, 6)])
        out[j] = even - odd
        out[12 - j] = even + odd
    return out


def split_dot(x, high, low):
    x_high = x.astype(jnp.bfloat16)
    x_low = (x - x_high.astype(jnp.float32)).astype(jnp.bfloat16)
    dot = functools.partial(jnp.dot, preferred_element_type=jnp.float32)
    return dot(x_high, high) + (dot(x_low, high) + dot(x_high, low))


def kernel(
    lat_count, fields, rows,
    q_hbm, u_hbm, v_hbm, cut_hbm, fh_hbm, fl_hbm, ih_hbm, il_hbm, waves_hbm,
    out_ref,
    q_in, u_in, v_in, q_pad, u_pad, v_pad, edge_out, edge_in, side_out, side_in,
    fh, fl, ih, il, waves_ref, cut_ref, stepped, land, done, result,
    load_sem, table_sem, halo_send, halo_recv, go_send, go_recv, back_send, back_recv,
):
    lat, lon = lax.axis_index("lat"), lax.axis_index("lon")
    chip, core = lon // 2, lax.rem(lon, 2)
    slabs = fields * rows
    tiles = 2 * slabs
    first = 15 * chip + 8 * core
    low_edge, high_edge = lat == 0, lat == lat_count - 1
    polar = jnp.logical_or(
        lat * rows < POLAR_ROWS, (lat_count - 1 - lat) * rows < POLAR_ROWS
    )
    across = lax.rem(lon + 6, SECTORS)
    north = (jnp.where(low_edge, 0, lat - 1), jnp.where(low_edge, across, lon))
    south = (jnp.where(high_edge, lat, lat + 1), jnp.where(high_edge, across, lon))
    west = (lat, lax.rem(lon + SECTORS - 1, SECTORS))
    east = (lat, lax.rem(lon + 1, SECTORS))

    loads = [
        pltpu.make_async_copy(q_hbm, q_in, load_sem.at[0]),
        pltpu.make_async_copy(u_hbm, u_in, load_sem.at[1]),
        pltpu.make_async_copy(v_hbm, v_in, load_sem.at[2]),
    ]
    for load in loads:
        load.start()
    tables = [
        pltpu.make_async_copy(source, target, table_sem.at[i])
        for i, (source, target) in enumerate(
            ((fh_hbm, fh), (fl_hbm, fl), (ih_hbm, ih), (il_hbm, il), (waves_hbm, waves_ref), (cut_hbm, cut_ref))
        )
    ]

    barrier = pltpu.get_barrier_semaphore()
    for target in (north, south, west, east):
        pl.semaphore_signal(barrier, inc=1, device_id=target, device_id_type=MESH)

    @pl.when(polar)
    def _():
        for offset in range(2, SECTORS - 1):
            pl.semaphore_signal(
                barrier, inc=1, device_id=(lat, lax.rem(lon + offset, SECTORS)), device_id_type=MESH
            )
        for table in tables:
            table.start()

    for load in loads:
        load.wait()

    sector = q_in.shape[-1]
    lane = lax.broadcasted_iota(jnp.int32, (16, LANES), 1)
    east_pack = jnp.zeros((16, LANES), jnp.float32)
    west_pack = jnp.zeros((16, LANES), jnp.float32)
    for f in range(fields + 1):
        for r in range(rows):
            s = f * rows + r
            source, pad = (q_in.at[f], q_pad.at[f]) if f < fields else (u_in, u_pad)
            pad[r, :, pl.ds(0, sector)] = source[r]
            x = pad[r]
            west_pack = jnp.where(lane == s, pltpu.roll(x, s, 1), west_pack)
            east_pack = jnp.where(
                lane == s, pltpu.roll(x, (s - (sector - 1)) % LANES, 1), east_pack
            )
    for r in range(rows):
        v_pad[r, :, pl.ds(0, sector)] = v_in[r]
    side_out[0] = west_pack
    side_out[1] = east_pack
    for side, row in ((0, 0), (1, rows - 1)):
        for f in range(fields):
            edge_out[side, f] = q_pad[f, row]
        edge_out[side, fields] = v_pad[row]

    @pl.when(polar)
    def _():
        pl.semaphore_wait(barrier, 4 + SECTORS - 3)

    @pl.when(jnp.logical_not(polar))
    def _():
        pl.semaphore_wait(barrier, 4)

    def edge_copy(side, slot, target):
        return pltpu.make_async_remote_copy(
            src_ref=edge_out.at[side],
            dst_ref=edge_in.at[slot],
            send_sem=halo_send.at[side],
            recv_sem=halo_recv.at[slot],
            device_id=target,
            device_id_type=MESH,
        )

    to_north = edge_copy(0, jnp.where(low_edge, 0, 1), north)
    to_south = edge_copy(1, jnp.where(high_edge, 1, 0), south)
    to_west = pltpu.make_async_remote_copy(
        src_ref=side_out.at[0], dst_ref=side_in.at[1], send_sem=halo_send.at[2],
        recv_sem=halo_recv.at[2], device_id=west, device_id_type=MESH,
    )
    to_east = pltpu.make_async_remote_copy(
        src_ref=side_out.at[1], dst_ref=side_in.at[0], send_sem=halo_send.at[3],
        recv_sem=halo_recv.at[3], device_id=east, device_id_type=MESH,
    )
    for copy in (to_north, to_south, to_west, to_east):
        copy.start()
    to_west.wait_recv()
    to_east.wait_recv()
    edge_copy(0, 0, north).wait_recv()
    edge_copy(1, 1, south).wait_recv()

    from_west, from_east = side_in[0], side_in[1]

    def with_ghosts(x, s):
        x = jnp.where(lane == sector, pltpu.roll(from_east, (sector - s) % LANES, 1), x)
        return jnp.where(lane == LANES - 1, pltpu.roll(from_west, (LANES - 1 - s) % LANES, 1), x)

    flip_north = jnp.where(low_edge, -1.0, 1.0)
    flip_south = jnp.where(high_edge, -1.0, 1.0)
    for r in range(rows):
        u = with_ghosts(u_pad[r], fields * rows + r)
        east_speed = 0.5 * (u + pltpu.roll(u, LANES - 1, 1))
        west_speed = 0.5 * (pltpu.roll(u, 1, 1) + u)
        v = v_pad[r]
        v_next = v_pad[r + 1] if r < rows - 1 else edge_in[1, fields] * flip_south
        v_previous = v_pad[r - 1] if r > 0 else edge_in[0, fields] * flip_north
        south_speed = 0.5 * (v + v_next)
        north_speed = 0.5 * (v_previous + v)
        e_plus, e_minus = jnp.maximum(east_speed, 0.0), jnp.minimum(east_speed, 0.0)
        w_plus, w_minus = jnp.maximum(west_speed, 0.0), jnp.minimum(west_speed, 0.0)
        s_plus, s_minus = jnp.maximum(south_speed, 0.0), jnp.minimum(south_speed, 0.0)
        n_plus, n_minus = jnp.maximum(north_speed, 0.0), jnp.minimum(north_speed, 0.0)
        for f in range(fields):
            q = with_ghosts(q_pad[f, r], f * rows + r)
            q_next = q_pad[f, r + 1] if r < rows - 1 else edge_in[1, f]
            q_previous = q_pad[f, r - 1] if r > 0 else edge_in[0, f]
            east_flux = e_plus * q + e_minus * pltpu.roll(q, LANES - 1, 1)
            west_flux = w_plus * pltpu.roll(q, 1, 1) + w_minus * q
            south_flux = s_plus * q + s_minus * q_next
            north_flux = n_plus * q_previous + n_minus * q
            new = q - (east_flux - west_flux) - (south_flux - north_flux)
            new = jnp.where(lane < sector, new, 0.0)
            tile = 2 * (f * rows + r)
            stepped[tile] = new[:8]
            stepped[tile + 1] = new[8:]

    @pl.when(jnp.logical_not(polar))
    def _():
        out_ref[...] = stepped[pl.ds(0, tiles)]

    def peers():
        for offset in range(1, 6):
            for c in range(2):
                to_chip = lax.rem(chip + offset, 6)
                yield to_chip, c, 2 * to_chip + c

    def waiter(ref, sem):
        return pltpu.make_async_copy(ref, ref, sem)

    @pl.when(polar)
    def _():
        counts = ((4, 4), (4, 3))
        starts = (0, 4)

        def go(phase, to_first, count, to):
            pltpu.make_async_remote_copy(
                src_ref=stepped.at[pl.ds(to_first + starts[phase], count)],
                dst_ref=land.at[lon, pl.ds(starts[phase], count)],
                send_sem=go_send.at[phase], recv_sem=go_recv.at[phase],
                device_id=(lat, to), device_id_type=MESH,
            ).start()

        def back(phase, count, to):
            pltpu.make_async_remote_copy(
                src_ref=done.at[to, pl.ds(starts[phase], count)],
                dst_ref=result.at[pl.ds(first + starts[phase], count)],
                send_sem=back_send.at[phase], recv_sem=back_recv.at[phase],
                device_id=(lat, to), device_id_type=MESH,
            ).start()

        for phase in range(2):
            for to_chip, c, to in peers():
                go(phase, 15 * to_chip + 8 * c, counts[c][phase], to)
            for c in range(2):
                @pl.when(core == 1 - c)
                def _():
                    go(phase, 15 * chip + 8 * c, counts[c][phase], 2 * chip + c)

        land[lon] = stepped[pl.ds(first, 8)]
        for table in tables:
            table.wait()

        for phase in range(2):
            for c in range(2):
                @pl.when(core == c)
                def _():
                    count = counts[c][phase]
                    waiter(land.at[pl.ds(0, 11), pl.ds(0, count)], go_recv.at[phase]).wait()
            x = [land[j, pl.ds(starts[phase], 4)].reshape(32, LANES) for j in range(SECTORS)]
            limit = [cut_ref[lax.rem((first + starts[phase] + i) // 2, rows)] for i in range(4)]
            w = []
            for block, (a, b) in enumerate(sector_dft(x)):
                z = split_dot(jnp.concatenate([a, b], axis=1), fh[block], fl[block])
                wave = jnp.broadcast_to(waves_ref[pl.ds(block, 1)], (8, 256))
                z = jnp.concatenate(
                    [jnp.where(wave <= limit[i], z[8 * i : 8 * i + 8], 0.0) for i in range(4)], axis=0
                )
                y = split_dot(z, ih[block], il[block])
                w.append((y[:, :LANES], y[:, LANES:]))
            for j, y in enumerate(sector_inverse(w)):
                done[j, pl.ds(starts[phase], 4)] = y.reshape(4, 8, LANES)
            for c in range(2):
                @pl.when(core == c)
                def _():
                    count = counts[c][phase]
                    for _, _, to in peers():
                        back(phase, count, to)
                    back(phase, count, lon + 1 - 2 * c)
                    result[pl.ds(first + starts[phase], count)] = done[lon, pl.ds(starts[phase], count)]

        waiter(result.at[pl.ds(0, 44)], back_recv.at[0]).wait()
        for c in range(2):
            @pl.when(core == c)
            def _():
                waiter(result.at[pl.ds(0, 35 + counts[1 - c][1])], back_recv.at[1]).wait()
                waiter(stepped.at[pl.ds(0, 35 + counts[1 - c][1])], go_send.at[1]).wait()
                waiter(done.at[pl.ds(0, 11), pl.ds(0, counts[c][1])], back_send.at[1]).wait()
        waiter(stepped.at[pl.ds(0, 44)], go_send.at[0]).wait()
        waiter(done.at[pl.ds(0, 11), pl.ds(0, 4)], back_send.at[0]).wait()
        out_ref[...] = result[pl.ds(0, tiles)]

    for copy in (to_north, to_south, to_west, to_east):
        copy.wait_send()


def body(lat_count, tracers, zonal_wind, meridional_wind, cutoff):
    fields, levels, rows, sector = tracers.shape
    q = jnp.transpose(tracers, (0, 2, 1, 3))
    u = jnp.transpose(zonal_wind, (1, 0, 2))
    v = jnp.transpose(meridional_wind, (1, 0, 2))
    tables = [jnp.asarray(t) for t in dft_tables(SECTORS * sector, sector)]
    tiles = fields * rows * 2
    f32, bf16 = jnp.float32, jnp.bfloat16
    dma = pltpu.SemaphoreType.DMA
    hbm = pl.BlockSpec(memory_space=pltpu.HBM)
    vmem = pl.BlockSpec(memory_space=pltpu.VMEM)
    out = pl.pallas_call(
        functools.partial(kernel, lat_count, fields, rows),
        out_shape=jax.ShapeDtypeStruct((tiles, 8, LANES), f32),
        in_specs=[hbm] * 9,
        out_specs=vmem,
        scratch_shapes=[
            pltpu.VMEM((fields, rows, levels, sector), f32),
            pltpu.VMEM((rows, levels, sector), f32),
            pltpu.VMEM((rows, levels, sector), f32),
            pltpu.VMEM((fields, rows, levels, LANES), f32),
            pltpu.VMEM((rows, levels, LANES), f32),
            pltpu.VMEM((rows, levels, LANES), f32),
            pltpu.VMEM((2, fields + 1, levels, LANES), f32),
            pltpu.VMEM((2, fields + 1, levels, LANES), f32),
            pltpu.VMEM((2, levels, LANES), f32),
            pltpu.VMEM((2, levels, LANES), f32),
            pltpu.VMEM((6, 256, 256), bf16),
            pltpu.VMEM((6, 256, 256), bf16),
            pltpu.VMEM((6, 256, 256), bf16),
            pltpu.VMEM((6, 256, 256), bf16),
            pltpu.VMEM((8, 256), jnp.int32),
            pltpu.SMEM((rows,), jnp.int32),
            pltpu.VMEM((96, 8, LANES), f32),
            pltpu.VMEM((SECTORS, 8, 8, LANES), f32),
            pltpu.VMEM((SECTORS, 8, 8, LANES), f32),
            pltpu.VMEM((96, 8, LANES), f32),
            dma((3,)), dma((6,)), dma((4,)), dma((4,)), dma((2,)), dma((2,)), dma((2,)), dma((2,)),
        ],
        compiler_params=pltpu.CompilerParams(
            collective_id=0, has_side_effects=True, vmem_limit_bytes=60 * 1024 * 1024
        ),
    )(q, u, v, cutoff, *tables)
    out = out.reshape(fields, rows, levels, LANES)[..., :sector]
    return jnp.transpose(out, (0, 2, 1, 3))


def solution(mesh):
    in_specs = (P(None, None, "lat", "lon"), P(None, "lat", "lon"), P(None, "lat", "lon"), P("lat"))
    out_specs = P(None, None, "lat", "lon")
    return jax.shard_map(
        functools.partial(body, mesh.shape["lat"]),
        mesh=mesh, in_specs=in_specs, out_specs=out_specs, check_vma=False,
    )
```

```python
import functools
import math

import jax
import jax.numpy as jnp
import ml_dtypes
import numpy as np
from jax import lax
from jax.experimental import pallas as pl
from jax.experimental.pallas import tpu as pltpu
from jax.sharding import PartitionSpec as P

MESH = pl.DeviceIdType.MESH
POLAR_ROWS = 96
SECTORS = 12
LANES = 128
STRIDE = 16


def split_bf16(table):
    high = table.astype(ml_dtypes.bfloat16)
    low = (table - high.astype(np.float64)).astype(ml_dtypes.bfloat16)
    return high, low


@functools.lru_cache(maxsize=None)
def dft_tables(circle, sector):
    forward = np.zeros((6, 256, 256))
    inverse = np.zeros((6, 256, 256))
    waves = np.zeros((8, 256))
    m = np.arange(sector)

    def put(block, column, k, part, weight, real_half):
        phase = 2.0 * math.pi * ((m * k) % circle) / circle
        cos, sin = np.cos(phase), np.sin(phase)
        waves[block, column] = min(k, circle - k)
        if real_half is not None:
            base = 128 * real_half
            row = cos if part == 0 else -sin
            forward[block, base : base + sector, column] = row
            inverse[block, column, base : base + sector] = weight * row / circle
            return
        if part == 0:
            forward[block, :sector, column] = cos
            forward[block, 128 : 128 + sector, column] = sin
            inverse[block, column, :sector] = weight * cos / circle
            inverse[block, column, 128 : 128 + sector] = weight * sin / circle
        else:
            forward[block, :sector, column] = -sin
            forward[block, 128 : 128 + sector, column] = cos
            inverse[block, column, :sector] = -weight * sin / circle
            inverse[block, column, 128 : 128 + sector] = weight * cos / circle

    half = sector // 2
    for q in range(half + 1):
        put(0, q, SECTORS * q, 0, 1.0 if q in (0, half) else 2.0, 0)
    for q in range(1, half):
        put(0, half + q, SECTORS * q, 1, 2.0, 0)
    for q in range(half):
        put(0, 128 + q, 6 + SECTORS * q, 0, 2.0, 1)
        put(0, 128 + half + q, 6 + SECTORS * q, 1, 2.0, 1)
    for r in range(1, 6):
        for q in range(sector):
            put(r, q, r + SECTORS * q, 0, 2.0, None)
            put(r, 128 + q, r + SECTORS * q, 1, 2.0, None)
    return split_bf16(forward) + split_bf16(inverse) + (waves.astype(np.float32),)


def combine(terms):
    groups = {}
    for coefficient, array in terms:
        size = round(abs(coefficient), 6)
        if size < 1e-6:
            continue
        groups.setdefault(size, []).append((coefficient, array))
    total = None
    for size in sorted(groups, reverse=True):
        part = None
        for coefficient, array in groups[size]:
            if part is None:
                part = array if coefficient > 0 else -array
            else:
                part = part + array if coefficient > 0 else part - array
        if size != 1.0:
            part = part * abs(groups[size][0][0])
        total = part if total is None else total + part
    return total


def cos12(i):
    return math.cos(2.0 * math.pi * (i % 12) / 12)


def sin12(i):
    return math.sin(2.0 * math.pi * (i % 12) / 12)


def sector_dft(x):
    sums = [None] + [x[j] + x[12 - j] for j in range(1, 6)]
    differences = [None] + [x[j] - x[12 - j] for j in range(1, 6)]
    real, imag = [], []
    for r in range(7):
        terms = [(1.0, x[0]), (1.0 if r % 2 == 0 else -1.0, x[6])]
        terms += [(cos12(j * r), sums[j]) for j in range(1, 6)]
        real.append(combine(terms))
        if 0 < r < 6:
            imag.append(combine([(-sin12(j * r), differences[j]) for j in range(1, 6)]))
        else:
            imag.append(None)
    return [(real[0], real[6])] + [(real[r], imag[r]) for r in range(1, 6)]


def sector_inverse(w):
    out = [None] * 12
    for j in range(7):
        terms = [(1.0, w[0][0]), (1.0 if j % 2 == 0 else -1.0, w[0][1])]
        terms += [(cos12(j * r), w[r][0]) for r in range(1, 6)]
        even = combine(terms)
        if j in (0, 6):
            out[j] = even
            continue
        odd = combine([(sin12(j * r), w[r][1]) for r in range(1, 6)])
        out[j] = even - odd
        out[12 - j] = even + odd
    return out


def split_dot(x, high, low):
    x_high = x.astype(jnp.bfloat16)
    x_low = (x - x_high.astype(jnp.float32)).astype(jnp.bfloat16)
    dot = functools.partial(jnp.dot, preferred_element_type=jnp.float32)
    return dot(x_high, high) + (dot(x_low, high) + dot(x_high, low))


def kernel(
    lat_count, fields, rows,
    q_hbm, u_hbm, v_hbm, cut_hbm, fh_hbm, fl_hbm, ih_hbm, il_hbm, waves_hbm,
    out_ref,
    q_in, u_in, v_in, q_pad, u_pad, v_pad, edge_out, edge_in, side_out, side_in,
    fh, fl, ih, il, waves_ref, cut_ref, cut_out, cut_rows, stepped, relay, land, done, result,
    load_sem, table_sem, halo_send, halo_recv, cut_send, cut_recv, relay_send, relay_recv,
    go_send, go_recv, back_send, back_recv,
):
    lat, lon = lax.axis_index("lat"), lax.axis_index("lon")
    chip, core = lon // 2, lax.rem(lon, 2)
    tiles = 2 * fields * rows
    low_edge, high_edge = lat == 0, lat == lat_count - 1
    caps = -(-POLAR_ROWS // rows)
    in_north, in_south = lat < caps, lat >= lat_count - caps
    main = jnp.logical_or(in_north, in_south)
    helper = jnp.logical_or(
        jnp.logical_and(lat >= STRIDE, lat < STRIDE + caps),
        jnp.logical_and(lat >= lat_count - STRIDE - caps, lat < lat_count - STRIDE),
    )
    mate = jnp.where(jnp.logical_or(in_north, lat >= lat_count // 2), STRIDE, -STRIDE)
    mate = lat + jnp.where(in_south, -STRIDE, mate)
    team = jnp.where(main, lat, mate)
    across = lax.rem(lon + 6, SECTORS)
    north = (jnp.where(low_edge, 0, lat - 1), jnp.where(low_edge, across, lon))
    south = (jnp.where(high_edge, lat, lat + 1), jnp.where(high_edge, across, lon))
    west = (lat, lax.rem(lon + SECTORS - 1, SECTORS))
    east = (lat, lax.rem(lon + 1, SECTORS))
    slot = jnp.where(chip < 3, 2 * chip, 11 - 2 * chip)
    starts = (
        jnp.where(main, 2 * lon, 48 + 4 * slot + 2 * core),
        jnp.where(main, 24 + 2 * lon, 72 + 3 * slot + 2 * core),
    )

    def turned(offset):
        return lax.rem(lon + offset, SECTORS)

    def greet(target):
        pl.semaphore_signal(barrier, inc=1, device_id=target, device_id_type=MESH)

    def waiter(ref, sem):
        return pltpu.make_async_copy(ref, ref, sem)

    def send(source, target, send_sem, recv_sem, device):
        pltpu.make_async_remote_copy(
            src_ref=source, dst_ref=target, send_sem=send_sem, recv_sem=recv_sem,
            device_id=device, device_id_type=MESH,
        ).start()

    loads = [
        pltpu.make_async_copy(q_hbm, q_in, load_sem.at[0]),
        pltpu.make_async_copy(u_hbm, u_in, load_sem.at[1]),
        pltpu.make_async_copy(v_hbm, v_in, load_sem.at[2]),
    ]
    for load in loads:
        load.start()
    tables = [
        pltpu.make_async_copy(source, target, table_sem.at[i])
        for i, (source, target) in enumerate(
            ((cut_hbm, cut_ref), (waves_hbm, waves_ref), (fh_hbm, fh), (fl_hbm, fl), (ih_hbm, ih), (il_hbm, il))
        )
    ]

    barrier = pltpu.get_barrier_semaphore()
    for target in (north, south, west, east):
        greet(target)

    @pl.when(jnp.logical_or(main, helper))
    def _():
        for offset in range(2, SECTORS - 1):
            greet((lat, turned(offset)))
        for table in tables:
            table.start()

    @pl.when(main)
    def _():
        for offset in range(SECTORS):
            greet((mate, turned(offset)))

    @pl.when(helper)
    def _():
        greet((mate, lon))

    for load in loads:
        load.wait()

    sector = q_in.shape[-1]
    lane = lax.broadcasted_iota(jnp.int32, (16, LANES), 1)
    east_pack = jnp.zeros((16, LANES), jnp.float32)
    west_pack = jnp.zeros((16, LANES), jnp.float32)
    for f in range(fields + 1):
        for r in range(rows):
            s = f * rows + r
            source, pad = (q_in.at[f], q_pad.at[f]) if f < fields else (u_in, u_pad)
            pad[r, :, pl.ds(0, sector)] = source[r]
            x = pad[r]
            west_pack = jnp.where(lane == s, pltpu.roll(x, s, 1), west_pack)
            east_pack = jnp.where(
                lane == s, pltpu.roll(x, (s - (sector - 1)) % LANES, 1), east_pack
            )
    for r in range(rows):
        v_pad[r, :, pl.ds(0, sector)] = v_in[r]
    side_out[0] = west_pack
    side_out[1] = east_pack
    for side, row in ((0, 0), (1, rows - 1)):
        for f in range(fields):
            edge_out[side, f] = q_pad[f, row]
        edge_out[side, fields] = v_pad[row]

    @pl.when(main)
    def _():
        pl.semaphore_wait(barrier, 4 + SECTORS - 3 + 1)

    @pl.when(helper)
    def _():
        pl.semaphore_wait(barrier, 4 + SECTORS - 3 + SECTORS)

    @pl.when(jnp.logical_not(jnp.logical_or(main, helper)))
    def _():
        pl.semaphore_wait(barrier, 4)

    def edge_copy(side, slot, target):
        return pltpu.make_async_remote_copy(
            src_ref=edge_out.at[side],
            dst_ref=edge_in.at[slot],
            send_sem=halo_send.at[side],
            recv_sem=halo_recv.at[slot],
            device_id=target,
            device_id_type=MESH,
        )

    to_north = edge_copy(0, jnp.where(low_edge, 0, 1), north)
    to_south = edge_copy(1, jnp.where(high_edge, 1, 0), south)
    to_west = pltpu.make_async_remote_copy(
        src_ref=side_out.at[0], dst_ref=side_in.at[1], send_sem=halo_send.at[2],
        recv_sem=halo_recv.at[2], device_id=west, device_id_type=MESH,
    )
    to_east = pltpu.make_async_remote_copy(
        src_ref=side_out.at[1], dst_ref=side_in.at[0], send_sem=halo_send.at[3],
        recv_sem=halo_recv.at[3], device_id=east, device_id_type=MESH,
    )
    for copy in (to_north, to_south, to_west, to_east):
        copy.start()

    @pl.when(main)
    def _():
        tables[0].wait()
        for r in range(rows):
            limit = jnp.full((1, LANES), cut_ref[r], jnp.int32).astype(jnp.float32)
            cut_out[pl.ds(r, 1)] = limit
            cut_rows[pl.ds(r, 1)] = limit
        cut_out[pl.ds(rows, 16 - rows)] = jnp.zeros((16 - rows, LANES), jnp.float32)
        send(cut_out, cut_rows, cut_send, cut_recv, (mate, lon))

    @pl.when(helper)
    def _():
        for phase in range(2):
            for group in range(3):
                count = (8, 6)[phase]
                chunk = relay.at[pl.ds(24 * phase + count * group, count)]
                waiter(chunk, relay_recv.at[3 * phase + group]).wait()
                for place, to_chip in enumerate((group, 5 - group)):
                    for c in range(2):
                        to = 2 * to_chip + c
                        n = 2 - phase * c
                        at = 24 * phase + count * group + count // 2 * place + 2 * c

                        @pl.when(lon != to)
                        def _():
                            send(
                                relay.at[pl.ds(at, n)], land.at[lon, pl.ds(2 * phase, n)],
                                go_send.at[phase], go_recv.at[phase], (lat, to),
                            )

                        @pl.when(lon == to)
                        def _():
                            land[lon, pl.ds(2 * phase, n)] = relay[pl.ds(at, n)]

    to_west.wait_recv()
    to_east.wait_recv()
    edge_copy(0, 0, north).wait_recv()
    edge_copy(1, 1, south).wait_recv()

    from_west, from_east = side_in[0], side_in[1]

    def with_ghosts(x, s):
        x = jnp.where(lane == sector, pltpu.roll(from_east, (sector - s) % LANES, 1), x)
        return jnp.where(lane == LANES - 1, pltpu.roll(from_west, (LANES - 1 - s) % LANES, 1), x)

    flip_north = jnp.where(low_edge, -1.0, 1.0)
    flip_south = jnp.where(high_edge, -1.0, 1.0)
    for r in range(rows):
        u = with_ghosts(u_pad[r], fields * rows + r)
        east_speed = 0.5 * (u + pltpu.roll(u, LANES - 1, 1))
        west_speed = 0.5 * (pltpu.roll(u, 1, 1) + u)
        v = v_pad[r]
        v_next = v_pad[r + 1] if r < rows - 1 else edge_in[1, fields] * flip_south
        v_previous = v_pad[r - 1] if r > 0 else edge_in[0, fields] * flip_north
        south_speed = 0.5 * (v + v_next)
        north_speed = 0.5 * (v_previous + v)
        e_plus, e_minus = jnp.maximum(east_speed, 0.0), jnp.minimum(east_speed, 0.0)
        w_plus, w_minus = jnp.maximum(west_speed, 0.0), jnp.minimum(west_speed, 0.0)
        s_plus, s_minus = jnp.maximum(south_speed, 0.0), jnp.minimum(south_speed, 0.0)
        n_plus, n_minus = jnp.maximum(north_speed, 0.0), jnp.minimum(north_speed, 0.0)
        for f in range(fields):
            q = with_ghosts(q_pad[f, r], f * rows + r)
            q_next = q_pad[f, r + 1] if r < rows - 1 else edge_in[1, f]
            q_previous = q_pad[f, r - 1] if r > 0 else edge_in[0, f]
            east_flux = e_plus * q + e_minus * pltpu.roll(q, LANES - 1, 1)
            west_flux = w_plus * pltpu.roll(q, 1, 1) + w_minus * q
            south_flux = s_plus * q + s_minus * q_next
            north_flux = n_plus * q_previous + n_minus * q
            new = q - (east_flux - west_flux) - (south_flux - north_flux)
            new = jnp.where(lane < sector, new, 0.0)
            tile = 2 * (f * rows + r)
            stepped[tile] = new[:8]
            stepped[tile + 1] = new[8:]

    @pl.when(jnp.logical_not(main))
    def _():
        out_ref[...] = stepped[...]

    @pl.when(main)
    def _():
        for phase in range(2):
            for group in range(3):
                count = (8, 6)[phase]
                at = 24 * phase + count * group
                send(
                    stepped.at[pl.ds(48 + at, count)], relay.at[pl.ds(at, count)],
                    relay_send, relay_recv.at[3 * phase + group], (mate, lon),
                )
            for offset in range(1, SECTORS):
                to = turned(offset)
                send(
                    stepped.at[pl.ds(24 * phase + 2 * to, 2)], land.at[lon, pl.ds(2 * phase, 2)],
                    go_send.at[phase], go_recv.at[phase], (lat, to),
                )
            land[lon, pl.ds(2 * phase, 2)] = stepped[pl.ds(24 * phase + 2 * lon, 2)]

    @pl.when(helper)
    def _():
        waiter(cut_rows, cut_recv).wait()
        tables[0].wait()

    @pl.when(jnp.logical_or(main, helper))
    def _():
        short = jnp.logical_and(helper, core == 1)
        for table in tables[1:]:
            table.wait()
        for phase in range(2):
            for n in range(1, 3) if phase else (2,):
                @pl.when(short == (n == 1) if phase else core >= 0)
                def _():
                    waiter(land.at[pl.ds(0, 11), pl.ds(0, n)], go_recv.at[phase]).wait()
            x = [land[j, pl.ds(2 * phase, 2)].reshape(16, LANES) for j in range(SECTORS)]
            limits = []
            for i in range(2):
                row = lax.rem((starts[phase] + i) // 2, rows)
                limit = jnp.broadcast_to(cut_rows[pl.ds(row, 1)], (8, LANES))
                limits.append(jnp.concatenate([limit, limit], axis=1))
            limits = jnp.concatenate(limits, axis=0)
            w = []
            for block, (a, b) in enumerate(sector_dft(x)):
                z = split_dot(jnp.concatenate([a, b], axis=1), fh[block], fl[block])
                wave = jnp.broadcast_to(waves_ref[pl.ds(block, 1)], (16, 256))
                z = jnp.where(wave <= limits, z, 0.0)
                y = split_dot(z, ih[block], il[block])
                w.append((y[:, :LANES], y[:, LANES:]))
            for j, y in enumerate(sector_inverse(w)):
                done[j, pl.ds(2 * phase, 2)] = y.reshape(2, 8, LANES)
            for n in range(1, 3) if phase else (2,):
                @pl.when(short == (n == 1) if phase else core >= 0)
                def _():
                    def back(to):
                        send(
                            done.at[to, pl.ds(2 * phase, n)], result.at[pl.ds(starts[phase], n)],
                            back_send.at[phase], back_recv.at[phase], (team, to),
                        )

                    for offset in range(1, SECTORS):
                        back(turned(offset))

                    @pl.when(helper)
                    def _():
                        back(lon)

            @pl.when(main)
            def _():
                result[pl.ds(starts[phase], 2)] = done[lon, pl.ds(2 * phase, 2)]

    @pl.when(main)
    def _():
        waiter(result.at[pl.ds(0, 46)], back_recv.at[0]).wait()
        waiter(result.at[pl.ds(0, 40)], back_recv.at[1]).wait()
        out_ref[...] = result[...]
        for phase in range(2):
            waiter(stepped.at[pl.ds(0, 22)], go_send.at[phase]).wait()
            waiter(stepped.at[pl.ds(0, 22)], back_send.at[phase]).wait()
        waiter(stepped.at[pl.ds(0, 42)], relay_send).wait()
        waiter(cut_out, cut_send).wait()

    @pl.when(helper)
    def _():
        waiter(stepped.at[pl.ds(0, 22)], go_send.at[0]).wait()
        waiter(stepped.at[pl.ds(0, 24)], back_send.at[0]).wait()
        for c in range(2):
            @pl.when(core == c)
            def _():
                waiter(stepped.at[pl.ds(0, 16 + c)], go_send.at[1]).wait()
                waiter(stepped.at[pl.ds(0, 24 - 12 * c)], back_send.at[1]).wait()

    for copy in (to_north, to_south, to_west, to_east):
        copy.wait_send()


def body(lat_count, tracers, zonal_wind, meridional_wind, cutoff):
    fields, levels, rows, sector = tracers.shape
    q = jnp.transpose(tracers, (0, 2, 1, 3))
    u = jnp.transpose(zonal_wind, (1, 0, 2))
    v = jnp.transpose(meridional_wind, (1, 0, 2))
    tables = [jnp.asarray(t) for t in dft_tables(SECTORS * sector, sector)]
    tiles = fields * rows * 2
    f32, bf16 = jnp.float32, jnp.bfloat16
    dma = pltpu.SemaphoreType.DMA
    hbm = pl.BlockSpec(memory_space=pltpu.HBM)
    vmem = pl.BlockSpec(memory_space=pltpu.VMEM)
    out = pl.pallas_call(
        functools.partial(kernel, lat_count, fields, rows),
        out_shape=jax.ShapeDtypeStruct((tiles, 8, LANES), f32),
        in_specs=[hbm] * 9,
        out_specs=vmem,
        scratch_shapes=[
            pltpu.VMEM((fields, rows, levels, sector), f32),
            pltpu.VMEM((rows, levels, sector), f32),
            pltpu.VMEM((rows, levels, sector), f32),
            pltpu.VMEM((fields, rows, levels, LANES), f32),
            pltpu.VMEM((rows, levels, LANES), f32),
            pltpu.VMEM((rows, levels, LANES), f32),
            pltpu.VMEM((2, fields + 1, levels, LANES), f32),
            pltpu.VMEM((2, fields + 1, levels, LANES), f32),
            pltpu.VMEM((2, levels, LANES), f32),
            pltpu.VMEM((2, levels, LANES), f32),
            pltpu.VMEM((6, 256, 256), bf16),
            pltpu.VMEM((6, 256, 256), bf16),
            pltpu.VMEM((6, 256, 256), bf16),
            pltpu.VMEM((6, 256, 256), bf16),
            pltpu.VMEM((8, 256), f32),
            pltpu.SMEM((rows,), jnp.int32),
            pltpu.VMEM((16, LANES), f32),
            pltpu.VMEM((16, LANES), f32),
            pltpu.VMEM((tiles, 8, LANES), f32),
            pltpu.VMEM((42, 8, LANES), f32),
            pltpu.VMEM((SECTORS, 4, 8, LANES), f32),
            pltpu.VMEM((SECTORS, 4, 8, LANES), f32),
            pltpu.VMEM((tiles, 8, LANES), f32),
            dma((3,)), dma((6,)), dma((4,)), dma((4,)), dma, dma, dma, dma((6,)),
            dma((2,)), dma((2,)), dma((2,)), dma((2,)),
        ],
        compiler_params=pltpu.CompilerParams(
            collective_id=0, has_side_effects=True, vmem_limit_bytes=60 * 1024 * 1024
        ),
    )(q, u, v, cutoff, *tables)
    out = out.reshape(fields, rows, levels, LANES)[..., :sector]
    return jnp.transpose(out, (0, 2, 1, 3))


def solution(mesh):
    in_specs = (P(None, None, "lat", "lon"), P(None, "lat", "lon"), P(None, "lat", "lon"), P("lat"))
    out_specs = P(None, None, "lat", "lon")
    return jax.shard_map(
        functools.partial(body, mesh.shape["lat"]),
        mesh=mesh, in_specs=in_specs, out_specs=out_specs, check_vma=False,
    )
```

```python
import functools
import math

import jax
import jax.numpy as jnp
import ml_dtypes
import numpy as np
from jax import lax
from jax.experimental import pallas as pl
from jax.experimental.pallas import tpu as pltpu
from jax.sharding import PartitionSpec as P

MESH = pl.DeviceIdType.MESH
POLAR_ROWS = 96
SECTORS = 12
LANES = 128
STRIDE = 16
OFFSETS = (1, 11, 2, 10, 3, 9, 4, 8, 5, 7, 6)


def slab_order(fields, rows):
    order = [(f, r) for r in range(1, rows - 1) for f in range(fields)]
    return order + [(f, r) for r in (0, rows - 1) for f in range(fields)]


def split_bf16(table):
    high = table.astype(ml_dtypes.bfloat16)
    low = (table - high.astype(np.float64)).astype(ml_dtypes.bfloat16)
    return high, low


@functools.lru_cache(maxsize=None)
def dft_tables(circle, sector):
    forward = np.zeros((6, 256, 256))
    inverse = np.zeros((6, 256, 256))
    waves = np.zeros((8, 256))
    m = np.arange(sector)

    def put(block, column, k, part, weight, real_half):
        phase = 2.0 * math.pi * ((m * k) % circle) / circle
        cos, sin = np.cos(phase), np.sin(phase)
        waves[block, column] = min(k, circle - k)
        if real_half is not None:
            base = 128 * real_half
            row = cos if part == 0 else -sin
            forward[block, base : base + sector, column] = row
            inverse[block, column, base : base + sector] = weight * row / circle
            return
        if part == 0:
            forward[block, :sector, column] = cos
            forward[block, 128 : 128 + sector, column] = sin
            inverse[block, column, :sector] = weight * cos / circle
            inverse[block, column, 128 : 128 + sector] = weight * sin / circle
        else:
            forward[block, :sector, column] = -sin
            forward[block, 128 : 128 + sector, column] = cos
            inverse[block, column, :sector] = -weight * sin / circle
            inverse[block, column, 128 : 128 + sector] = weight * cos / circle

    half = sector // 2
    for q in range(half + 1):
        put(0, q, SECTORS * q, 0, 1.0 if q in (0, half) else 2.0, 0)
    for q in range(1, half):
        put(0, half + q, SECTORS * q, 1, 2.0, 0)
    for q in range(half):
        put(0, 128 + q, 6 + SECTORS * q, 0, 2.0, 1)
        put(0, 128 + half + q, 6 + SECTORS * q, 1, 2.0, 1)
    for r in range(1, 6):
        for q in range(sector):
            put(r, q, r + SECTORS * q, 0, 2.0, None)
            put(r, 128 + q, r + SECTORS * q, 1, 2.0, None)
    return split_bf16(forward) + split_bf16(inverse) + (waves.astype(np.float32),)


def combine(terms):
    groups = {}
    for coefficient, array in terms:
        size = round(abs(coefficient), 6)
        if size < 1e-6:
            continue
        groups.setdefault(size, []).append((coefficient, array))
    total = None
    for size in sorted(groups, reverse=True):
        part = None
        for coefficient, array in groups[size]:
            if part is None:
                part = array if coefficient > 0 else -array
            else:
                part = part + array if coefficient > 0 else part - array
        if size != 1.0:
            part = part * abs(groups[size][0][0])
        total = part if total is None else total + part
    return total


def cos12(i):
    return math.cos(2.0 * math.pi * (i % 12) / 12)


def sin12(i):
    return math.sin(2.0 * math.pi * (i % 12) / 12)


def sector_dft(x):
    sums = [None] + [x[j] + x[12 - j] for j in range(1, 6)]
    differences = [None] + [x[j] - x[12 - j] for j in range(1, 6)]
    real, imag = [], []
    for r in range(7):
        terms = [(1.0, x[0]), (1.0 if r % 2 == 0 else -1.0, x[6])]
        terms += [(cos12(j * r), sums[j]) for j in range(1, 6)]
        real.append(combine(terms))
        if 0 < r < 6:
            imag.append(combine([(-sin12(j * r), differences[j]) for j in range(1, 6)]))
        else:
            imag.append(None)
    return [(real[0], real[6])] + [(real[r], imag[r]) for r in range(1, 6)]


def sector_inverse(w):
    out = [None] * 12
    for j in range(7):
        terms = [(1.0, w[0][0]), (1.0 if j % 2 == 0 else -1.0, w[0][1])]
        terms += [(cos12(j * r), w[r][0]) for r in range(1, 6)]
        even = combine(terms)
        if j in (0, 6):
            out[j] = even
            continue
        odd = combine([(sin12(j * r), w[r][1]) for r in range(1, 6)])
        out[j] = even - odd
        out[12 - j] = even + odd
    return out


def split_dot(x, high, low):
    x_high = x.astype(jnp.bfloat16)
    x_low = (x - x_high.astype(jnp.float32)).astype(jnp.bfloat16)
    dot = functools.partial(jnp.dot, preferred_element_type=jnp.float32)
    return dot(x_high, high) + (dot(x_low, high) + dot(x_high, low))


def kernel(
    lat_count, fields, rows,
    q_hbm, u_hbm, v_hbm, cut_hbm, fh_hbm, fl_hbm, ih_hbm, il_hbm, waves_hbm,
    out_ref,
    q_in, u_in, v_in, q_pad, u_pad, v_pad, edge_out, edge_in, side_out, side_in,
    fh, fl, ih, il, waves_ref, cut_ref, cut_out, cut_rows, stepped, relay, land, done, result,
    load_sem, table_sem, halo_send, halo_recv, cut_send, cut_recv, relay_send, relay_recv,
    go_send, go_recv, back_send, back_recv,
):
    lat, lon = lax.axis_index("lat"), lax.axis_index("lon")
    chip, core = lon // 2, lax.rem(lon, 2)
    tiles = 2 * fields * rows
    low_edge, high_edge = lat == 0, lat == lat_count - 1
    caps = -(-POLAR_ROWS // rows)
    in_north, in_south = lat < caps, lat >= lat_count - caps
    main = jnp.logical_or(in_north, in_south)
    helper = jnp.logical_or(
        jnp.logical_and(lat >= STRIDE, lat < STRIDE + caps),
        jnp.logical_and(lat >= lat_count - STRIDE - caps, lat < lat_count - STRIDE),
    )
    mate = jnp.where(jnp.logical_or(in_north, lat >= lat_count // 2), STRIDE, -STRIDE)
    mate = lat + jnp.where(in_south, -STRIDE, mate)
    team = jnp.where(main, lat, mate)
    across = lax.rem(lon + 6, SECTORS)
    north = (jnp.where(low_edge, 0, lat - 1), jnp.where(low_edge, across, lon))
    south = (jnp.where(high_edge, lat, lat + 1), jnp.where(high_edge, across, lon))
    west = (lat, lax.rem(lon + SECTORS - 1, SECTORS))
    east = (lat, lax.rem(lon + 1, SECTORS))
    slot = jnp.where(chip < 3, 2 * chip, 11 - 2 * chip)
    starts = (
        jnp.where(main, 24 + 2 * lon, 4 * slot + 2 * core),
        jnp.where(main, 66 + 2 * lon, 48 + 3 * slot + 2 * core),
    )
    order = slab_order(fields, rows)
    half = STRIDE // 2
    place = lax.rem(lat, STRIDE)
    far_north = jnp.logical_and(lax.rem(place, half) == 0, jnp.logical_not(low_edge))
    far_south = jnp.logical_and(lax.rem(place, half) == half - 1, jnp.logical_not(high_edge))
    upper = place >= half
    lower_far = jnp.logical_and(place < half, jnp.logical_or(far_north, far_south))

    def turned(offset):
        return lax.rem(lon + offset, SECTORS)

    def greet(target):
        pl.semaphore_signal(barrier, inc=1, device_id=target, device_id_type=MESH)

    def waiter(ref, sem):
        return pltpu.make_async_copy(ref, ref, sem)

    def send(source, target, send_sem, recv_sem, device):
        pltpu.make_async_remote_copy(
            src_ref=source, dst_ref=target, send_sem=send_sem, recv_sem=recv_sem,
            device_id=device, device_id_type=MESH,
        ).start()

    loads = [
        pltpu.make_async_copy(q_hbm, q_in, load_sem.at[0]),
        pltpu.make_async_copy(u_hbm, u_in, load_sem.at[1]),
        pltpu.make_async_copy(v_hbm, v_in, load_sem.at[2]),
    ]
    for load in loads:
        load.start()
    tables = [
        pltpu.make_async_copy(source, target, table_sem.at[i])
        for i, (source, target) in enumerate(
            ((cut_hbm, cut_ref), (waves_hbm, waves_ref), (fh_hbm, fh), (fl_hbm, fl), (ih_hbm, ih), (il_hbm, il))
        )
    ]

    barrier = pltpu.get_barrier_semaphore()
    greet(west)
    greet(east)
    for target, far in ((north, far_north), (south, far_south)):
        @pl.when(jnp.logical_not(jnp.logical_and(upper, far)))
        def _():
            greet(target)

    @pl.when(jnp.logical_or(main, helper))
    def _():
        for offset in range(2, SECTORS - 1):
            greet((lat, turned(offset)))
        for table in tables:
            table.start()

    @pl.when(main)
    def _():
        for offset in range(SECTORS):
            greet((mate, turned(offset)))

    @pl.when(helper)
    def _():
        greet((mate, lon))

    for load in loads:
        load.wait()

    sector = q_in.shape[-1]
    lane = lax.broadcasted_iota(jnp.int32, (16, LANES), 1)
    east_pack = jnp.zeros((16, LANES), jnp.float32)
    west_pack = jnp.zeros((16, LANES), jnp.float32)
    for f in range(fields + 1):
        for r in range(rows):
            s = f * rows + r
            source, pad = (q_in.at[f], q_pad.at[f]) if f < fields else (u_in, u_pad)
            pad[r, :, pl.ds(0, sector)] = source[r]
            x = pad[r]
            west_pack = jnp.where(lane == s, pltpu.roll(x, s, 1), west_pack)
            east_pack = jnp.where(
                lane == s, pltpu.roll(x, (s - (sector - 1)) % LANES, 1), east_pack
            )
    for r in range(rows):
        v_pad[r, :, pl.ds(0, sector)] = v_in[r]
    side_out[0] = west_pack
    side_out[1] = east_pack
    for side, row in ((0, 0), (1, rows - 1)):
        for f in range(fields):
            edge_out[side, f] = q_pad[f, row]
        edge_out[side, fields] = v_pad[row]

    greeted = jnp.where(main, 4 + SECTORS - 3 + 1, jnp.where(helper, 4 + SECTORS - 3 + SECTORS, 4))
    pl.semaphore_wait(barrier, greeted - jnp.where(lower_far, 1, 0))

    def edge_copy(side, slot, target):
        return pltpu.make_async_remote_copy(
            src_ref=edge_out.at[side],
            dst_ref=edge_in.at[slot],
            send_sem=halo_send.at[side],
            recv_sem=halo_recv.at[slot],
            device_id=target,
            device_id_type=MESH,
        )

    to_north = edge_copy(0, jnp.where(low_edge, 0, 1), north)
    to_south = edge_copy(1, jnp.where(high_edge, 1, 0), south)
    to_west = pltpu.make_async_remote_copy(
        src_ref=side_out.at[0], dst_ref=side_in.at[1], send_sem=halo_send.at[2],
        recv_sem=halo_recv.at[2], device_id=west, device_id_type=MESH,
    )
    to_east = pltpu.make_async_remote_copy(
        src_ref=side_out.at[1], dst_ref=side_in.at[0], send_sem=halo_send.at[3],
        recv_sem=halo_recv.at[3], device_id=east, device_id_type=MESH,
    )
    to_west.start()
    to_east.start()
    for copy, far in ((to_north, far_north), (to_south, far_south)):
        @pl.when(jnp.logical_or(upper, jnp.logical_not(far)))
        def _():
            copy.start()

    def edges_arrive():
        edge_copy(0, 0, north).wait_recv()
        edge_copy(1, 1, south).wait_recv()
        for copy, far in ((to_north, far_north), (to_south, far_south)):
            @pl.when(jnp.logical_and(lower_far, far))
            def _():
                copy.start()

    flip_north = jnp.where(low_edge, -1.0, 1.0)
    flip_south = jnp.where(high_edge, -1.0, 1.0)

    def step(slabs, winds):
        from_west, from_east = side_in[0], side_in[1]

        def with_ghosts(x, s):
            x = jnp.where(lane == sector, pltpu.roll(from_east, (sector - s) % LANES, 1), x)
            return jnp.where(lane == LANES - 1, pltpu.roll(from_west, (LANES - 1 - s) % LANES, 1), x)

        for p in slabs:
            f, r = order[p]
            if r not in winds:
                u = with_ghosts(u_pad[r], fields * rows + r)
                v = v_pad[r]
                v_next = v_pad[r + 1] if r < rows - 1 else edge_in[1, fields] * flip_south
                v_previous = v_pad[r - 1] if r > 0 else edge_in[0, fields] * flip_north
                speeds = (
                    0.5 * (u + pltpu.roll(u, LANES - 1, 1)), 0.5 * (pltpu.roll(u, 1, 1) + u),
                    0.5 * (v + v_next), 0.5 * (v_previous + v),
                )
                winds[r] = [(jnp.maximum(x, 0.0), jnp.minimum(x, 0.0)) for x in speeds]
            (e_plus, e_minus), (w_plus, w_minus), (s_plus, s_minus), (n_plus, n_minus) = winds[r]
            q = with_ghosts(q_pad[f, r], f * rows + r)
            q_next = q_pad[f, r + 1] if r < rows - 1 else edge_in[1, f]
            q_previous = q_pad[f, r - 1] if r > 0 else edge_in[0, f]
            east_flux = e_plus * q + e_minus * pltpu.roll(q, LANES - 1, 1)
            west_flux = w_plus * pltpu.roll(q, 1, 1) + w_minus * q
            south_flux = s_plus * q + s_minus * q_next
            north_flux = n_plus * q_previous + n_minus * q
            new = q - (east_flux - west_flux) - (south_flux - north_flux)
            new = jnp.where(lane < sector, new, 0.0)
            stepped[2 * p] = new[:8]
            stepped[2 * p + 1] = new[8:]

    def hand_out(source):
        for p, (f, r) in enumerate(order):
            out_ref[pl.ds(2 * (f * rows + r), 2)] = source[pl.ds(2 * p, 2)]

    @pl.when(main)
    def _():
        tables[0].wait()
        for r in range(rows):
            limit = jnp.full((1, LANES), cut_ref[r], jnp.int32).astype(jnp.float32)
            cut_out[pl.ds(r, 1)] = limit
            cut_rows[pl.ds(r, 1)] = limit
        cut_out[pl.ds(rows, 16 - rows)] = jnp.zeros((16 - rows, LANES), jnp.float32)
        send(cut_out, cut_rows, cut_send, cut_recv, (mate, lon))

    @pl.when(helper)
    def _():
        for phase in range(2):
            for group in range(3):
                count = (8, 6)[phase]
                chunk = relay.at[pl.ds(24 * phase + count * group, count)]
                waiter(chunk, relay_recv.at[3 * phase + group]).wait()
                for place, to_chip in enumerate((group, 5 - group)):
                    for c in range(2):
                        to = 2 * to_chip + c
                        n = 2 - phase * c
                        at = 24 * phase + count * group + count // 2 * place + 2 * c

                        @pl.when(lon != to)
                        def _():
                            send(
                                relay.at[pl.ds(at, n)], land.at[lon, pl.ds(2 * phase, n)],
                                go_send.at[phase], go_recv.at[phase], (lat, to),
                            )

                        @pl.when(lon == to)
                        def _():
                            land[lon, pl.ds(2 * phase, n)] = relay[pl.ds(at, n)]

    to_west.wait_recv()
    to_east.wait_recv()

    @pl.when(main)
    def _():
        winds = {}

        def for_helper(phase):
            for group in range(3):
                count = (8, 6)[phase]
                at = 48 * phase + count * group
                step(range(at // 2, (at + count) // 2), winds)
                send(
                    stepped.at[pl.ds(at, count)], relay.at[pl.ds(24 * phase + count * group, count)],
                    relay_send, relay_recv.at[3 * phase + group], (mate, lon),
                )

        def for_line(phase):
            at = (24, 66)[phase]
            for offset in OFFSETS:
                to = turned(offset)
                send(
                    stepped.at[pl.ds(at + 2 * to, 2)], land.at[lon, pl.ds(2 * phase, 2)],
                    go_send.at[phase], go_recv.at[phase], (lat, to),
                )
            land[lon, pl.ds(2 * phase, 2)] = stepped[pl.ds(at + 2 * lon, 2)]

        for_helper(0)
        step(range(12, 24), winds)
        for_line(0)
        for_helper(1)
        step(range(33, 35), winds)
        edges_arrive()
        step(range(35, 45), winds)
        for_line(1)

    @pl.when(helper)
    def _():
        waiter(cut_rows, cut_recv).wait()
        tables[0].wait()

    @pl.when(jnp.logical_or(main, helper))
    def _():
        short = jnp.logical_and(helper, core == 1)
        for table in tables[1:]:
            table.wait()
        for phase in range(2):
            for n in range(1, 3) if phase else (2,):
                @pl.when(short == (n == 1) if phase else core >= 0)
                def _():
                    waiter(land.at[pl.ds(0, 11), pl.ds(0, n)], go_recv.at[phase]).wait()
            x = [land[j, pl.ds(2 * phase, 2)].reshape(16, LANES) for j in range(SECTORS)]
            limits = []
            for i in range(2):
                p = (starts[phase] + i) // 2
                row = 1 + p // fields
                row = jnp.where(p < fields * (rows - 1), jnp.where(row < rows - 1, row, 0), rows - 1)
                limit = jnp.broadcast_to(cut_rows[pl.ds(row, 1)], (8, LANES))
                limits.append(jnp.concatenate([limit, limit], axis=1))
            limits = jnp.concatenate(limits, axis=0)
            w = []
            for block, (a, b) in enumerate(sector_dft(x)):
                z = split_dot(jnp.concatenate([a, b], axis=1), fh[block], fl[block])
                wave = jnp.broadcast_to(waves_ref[pl.ds(block, 1)], (16, 256))
                z = jnp.where(wave <= limits, z, 0.0)
                y = split_dot(z, ih[block], il[block])
                w.append((y[:, :LANES], y[:, LANES:]))
            for j, y in enumerate(sector_inverse(w)):
                done[j, pl.ds(2 * phase, 2)] = y.reshape(2, 8, LANES)
            for n in range(1, 3) if phase else (2,):
                @pl.when(short == (n == 1) if phase else core >= 0)
                def _():
                    def back(to):
                        send(
                            done.at[to, pl.ds(2 * phase, n)], result.at[pl.ds(starts[phase], n)],
                            back_send.at[phase], back_recv.at[phase], (team, to),
                        )

                    for offset in OFFSETS:
                        back(turned(offset))

                    @pl.when(helper)
                    def _():
                        back(lon)

            @pl.when(main)
            def _():
                result[pl.ds(starts[phase], 2)] = done[lon, pl.ds(2 * phase, 2)]

    @pl.when(main)
    def _():
        waiter(result.at[pl.ds(0, 46)], back_recv.at[0]).wait()
        waiter(result.at[pl.ds(0, 40)], back_recv.at[1]).wait()
        hand_out(result)
        for phase in range(2):
            waiter(stepped.at[pl.ds(0, 22)], go_send.at[phase]).wait()
            waiter(stepped.at[pl.ds(0, 22)], back_send.at[phase]).wait()
        waiter(stepped.at[pl.ds(0, 42)], relay_send).wait()
        waiter(cut_out, cut_send).wait()

    @pl.when(helper)
    def _():
        waiter(stepped.at[pl.ds(0, 22)], go_send.at[0]).wait()
        waiter(stepped.at[pl.ds(0, 24)], back_send.at[0]).wait()
        for c in range(2):
            @pl.when(core == c)
            def _():
                waiter(stepped.at[pl.ds(0, 16 + c)], go_send.at[1]).wait()
                waiter(stepped.at[pl.ds(0, 24 - 12 * c)], back_send.at[1]).wait()

    @pl.when(jnp.logical_not(main))
    def _():
        edges_arrive()
        step(range(len(order)), {})
        hand_out(stepped)

    for copy in (to_north, to_south, to_west, to_east):
        copy.wait_send()


def body(lat_count, tracers, zonal_wind, meridional_wind, cutoff):
    fields, levels, rows, sector = tracers.shape
    q = jnp.transpose(tracers, (0, 2, 1, 3))
    u = jnp.transpose(zonal_wind, (1, 0, 2))
    v = jnp.transpose(meridional_wind, (1, 0, 2))
    tables = [jnp.asarray(t) for t in dft_tables(SECTORS * sector, sector)]
    tiles = fields * rows * 2
    f32, bf16 = jnp.float32, jnp.bfloat16
    dma = pltpu.SemaphoreType.DMA
    hbm = pl.BlockSpec(memory_space=pltpu.HBM)
    vmem = pl.BlockSpec(memory_space=pltpu.VMEM)
    out = pl.pallas_call(
        functools.partial(kernel, lat_count, fields, rows),
        out_shape=jax.ShapeDtypeStruct((tiles, 8, LANES), f32),
        in_specs=[hbm] * 9,
        out_specs=vmem,
        scratch_shapes=[
            pltpu.VMEM((fields, rows, levels, sector), f32),
            pltpu.VMEM((rows, levels, sector), f32),
            pltpu.VMEM((rows, levels, sector), f32),
            pltpu.VMEM((fields, rows, levels, LANES), f32),
            pltpu.VMEM((rows, levels, LANES), f32),
            pltpu.VMEM((rows, levels, LANES), f32),
            pltpu.VMEM((2, fields + 1, levels, LANES), f32),
            pltpu.VMEM((2, fields + 1, levels, LANES), f32),
            pltpu.VMEM((2, levels, LANES), f32),
            pltpu.VMEM((2, levels, LANES), f32),
            pltpu.VMEM((6, 256, 256), bf16),
            pltpu.VMEM((6, 256, 256), bf16),
            pltpu.VMEM((6, 256, 256), bf16),
            pltpu.VMEM((6, 256, 256), bf16),
            pltpu.VMEM((8, 256), f32),
            pltpu.SMEM((rows,), jnp.int32),
            pltpu.VMEM((16, LANES), f32),
            pltpu.VMEM((16, LANES), f32),
            pltpu.VMEM((tiles, 8, LANES), f32),
            pltpu.VMEM((42, 8, LANES), f32),
            pltpu.VMEM((SECTORS, 4, 8, LANES), f32),
            pltpu.VMEM((SECTORS, 4, 8, LANES), f32),
            pltpu.VMEM((tiles, 8, LANES), f32),
            dma((3,)), dma((6,)), dma((4,)), dma((4,)), dma, dma, dma, dma((6,)),
            dma((2,)), dma((2,)), dma((2,)), dma((2,)),
        ],
        compiler_params=pltpu.CompilerParams(
            collective_id=0, has_side_effects=True, vmem_limit_bytes=60 * 1024 * 1024
        ),
    )(q, u, v, cutoff, *tables)
    out = out.reshape(fields, rows, levels, LANES)[..., :sector]
    return jnp.transpose(out, (0, 2, 1, 3))


def solution(mesh):
    in_specs = (P(None, None, "lat", "lon"), P(None, "lat", "lon"), P(None, "lat", "lon"), P("lat"))
    out_specs = P(None, None, "lat", "lon")
    return jax.shard_map(
        functools.partial(body, mesh.shape["lat"]),
        mesh=mesh, in_specs=in_specs, out_specs=out_specs, check_vma=False,
    )
```

```python
import functools
import math

import jax
import jax.numpy as jnp
import ml_dtypes
import numpy as np
from jax import lax
from jax.experimental import pallas as pl
from jax.experimental.pallas import tpu as pltpu
from jax.sharding import PartitionSpec as P

MESH = pl.DeviceIdType.MESH
POLAR_ROWS = 96
SECTORS = 12
LANES = 128
STRIDE = 16
OFFSETS = (1, 11, 2, 10, 3, 9, 4, 8, 5, 7, 6)


def slab_order(fields, rows):
    order = [(f, r) for r in range(1, rows - 1) for f in range(fields)]
    return order + [(f, r) for r in (0, rows - 1) for f in range(fields)]


def split_bf16(table):
    high = table.astype(ml_dtypes.bfloat16)
    low = (table - high.astype(np.float64)).astype(ml_dtypes.bfloat16)
    return high, low


@functools.lru_cache(maxsize=None)
def dft_tables(circle, sector):
    forward = np.zeros((6, 256, 256))
    inverse = np.zeros((6, 256, 256))
    waves = np.zeros((8, 256))
    m = np.arange(sector)

    def put(block, column, k, part, weight, real_half):
        phase = 2.0 * math.pi * ((m * k) % circle) / circle
        cos, sin = np.cos(phase), np.sin(phase)
        waves[block, column] = min(k, circle - k)
        if real_half is not None:
            base = 128 * real_half
            row = cos if part == 0 else -sin
            forward[block, base : base + sector, column] = row
            inverse[block, column, base : base + sector] = weight * row / circle
            return
        if part == 0:
            forward[block, :sector, column] = cos
            forward[block, 128 : 128 + sector, column] = sin
            inverse[block, column, :sector] = weight * cos / circle
            inverse[block, column, 128 : 128 + sector] = weight * sin / circle
        else:
            forward[block, :sector, column] = -sin
            forward[block, 128 : 128 + sector, column] = cos
            inverse[block, column, :sector] = -weight * sin / circle
            inverse[block, column, 128 : 128 + sector] = weight * cos / circle

    half = sector // 2
    for q in range(half + 1):
        put(0, q, SECTORS * q, 0, 1.0 if q in (0, half) else 2.0, 0)
    for q in range(1, half):
        put(0, half + q, SECTORS * q, 1, 2.0, 0)
    for q in range(half):
        put(0, 128 + q, 6 + SECTORS * q, 0, 2.0, 1)
        put(0, 128 + half + q, 6 + SECTORS * q, 1, 2.0, 1)
    for r in range(1, 6):
        for q in range(sector):
            put(r, q, r + SECTORS * q, 0, 2.0, None)
            put(r, 128 + q, r + SECTORS * q, 1, 2.0, None)
    return split_bf16(forward) + split_bf16(inverse) + (waves.astype(np.float32),)


def combine(terms):
    groups = {}
    for coefficient, array in terms:
        size = round(abs(coefficient), 6)
        if size < 1e-6:
            continue
        groups.setdefault(size, []).append((coefficient, array))
    total = None
    for size in sorted(groups, reverse=True):
        part = None
        for coefficient, array in groups[size]:
            if part is None:
                part = array if coefficient > 0 else -array
            else:
                part = part + array if coefficient > 0 else part - array
        if size != 1.0:
            part = part * abs(groups[size][0][0])
        total = part if total is None else total + part
    return total


def cos12(i):
    return math.cos(2.0 * math.pi * (i % 12) / 12)


def sin12(i):
    return math.sin(2.0 * math.pi * (i % 12) / 12)


def sector_dft(x):
    sums = [None] + [x[j] + x[12 - j] for j in range(1, 6)]
    differences = [None] + [x[j] - x[12 - j] for j in range(1, 6)]
    real, imag = [], []
    for r in range(7):
        terms = [(1.0, x[0]), (1.0 if r % 2 == 0 else -1.0, x[6])]
        terms += [(cos12(j * r), sums[j]) for j in range(1, 6)]
        real.append(combine(terms))
        if 0 < r < 6:
            imag.append(combine([(-sin12(j * r), differences[j]) for j in range(1, 6)]))
        else:
            imag.append(None)
    return [(real[0], real[6])] + [(real[r], imag[r]) for r in range(1, 6)]


def sector_inverse(w):
    out = [None] * 12
    for j in range(7):
        terms = [(1.0, w[0][0]), (1.0 if j % 2 == 0 else -1.0, w[0][1])]
        terms += [(cos12(j * r), w[r][0]) for r in range(1, 6)]
        even = combine(terms)
        if j in (0, 6):
            out[j] = even
            continue
        odd = combine([(sin12(j * r), w[r][1]) for r in range(1, 6)])
        out[j] = even - odd
        out[12 - j] = even + odd
    return out


def split_dot(x, high, low):
    x_high = x.astype(jnp.bfloat16)
    x_low = (x - x_high.astype(jnp.float32)).astype(jnp.bfloat16)
    dot = functools.partial(jnp.dot, preferred_element_type=jnp.float32)
    return dot(x_high, high) + (dot(x_low, high) + dot(x_high, low))


def kernel(
    lat_count, fields, rows,
    q_hbm, u_hbm, v_hbm, cut_hbm, fh_hbm, fl_hbm, ih_hbm, il_hbm, waves_hbm,
    out_ref,
    q_in, u_in, v_in, q_pad, u_pad, v_pad, edge_out, edge_in, side_out, side_in,
    fh, fl, ih, il, waves_ref, cut_ref, cut_out, cut_rows, stepped, relay, land, done, result,
    load_sem, table_sem, halo_send, halo_recv, cut_send, cut_recv, relay_send, relay_recv, hello,
    go_send, go_recv, back_send, back_recv,
):
    lat, lon = lax.axis_index("lat"), lax.axis_index("lon")
    chip, core = lon // 2, lax.rem(lon, 2)
    tiles = 2 * fields * rows
    low_edge, high_edge = lat == 0, lat == lat_count - 1
    caps = -(-POLAR_ROWS // rows)
    in_north, in_south = lat < caps, lat >= lat_count - caps
    main = jnp.logical_or(in_north, in_south)
    helper = jnp.logical_or(
        jnp.logical_and(lat >= STRIDE, lat < STRIDE + caps),
        jnp.logical_and(lat >= lat_count - STRIDE - caps, lat < lat_count - STRIDE),
    )
    mate = jnp.where(jnp.logical_or(in_north, lat >= lat_count // 2), STRIDE, -STRIDE)
    mate = lat + jnp.where(in_south, -STRIDE, mate)
    team = jnp.where(main, lat, mate)
    across = lax.rem(lon + 6, SECTORS)
    north = (jnp.where(low_edge, 0, lat - 1), jnp.where(low_edge, across, lon))
    south = (jnp.where(high_edge, lat, lat + 1), jnp.where(high_edge, across, lon))
    west = (lat, lax.rem(lon + SECTORS - 1, SECTORS))
    east = (lat, lax.rem(lon + 1, SECTORS))
    starts = (
        jnp.where(main, 24 + 2 * lon, 2 * lon),
        jnp.where(main, 66 + 2 * lon, 48 + 3 * chip + 2 * core),
    )
    first = jnp.where(low_edge, 1, 0)
    rank = lax.rem(lon + SECTORS - first, SECTORS)
    order = slab_order(fields, rows)
    half = STRIDE // 2
    place = lax.rem(lat, STRIDE)
    far_north = jnp.logical_and(lax.rem(place, half) == 0, jnp.logical_not(low_edge))
    far_south = jnp.logical_and(lax.rem(place, half) == half - 1, jnp.logical_not(high_edge))
    upper = place >= half
    north_late = jnp.logical_or(
        jnp.logical_and(far_north, jnp.logical_not(upper)), jnp.logical_and(lat == 1, lon == 0)
    )
    south_late = jnp.logical_and(far_south, jnp.logical_not(upper))
    late_for_north = jnp.logical_and(far_north, upper)
    late_for_south = jnp.logical_or(
        jnp.logical_and(far_south, upper), jnp.logical_and(low_edge, lon == 0)
    )

    def ranked(t):
        return lax.rem(t + first, SECTORS)

    def turned(offset):
        return lax.rem(lon + offset, SECTORS)

    def greet(target):
        pl.semaphore_signal(barrier, inc=1, device_id=target, device_id_type=MESH)

    def waiter(ref, sem):
        return pltpu.make_async_copy(ref, ref, sem)

    def send(source, target, send_sem, recv_sem, device):
        pltpu.make_async_remote_copy(
            src_ref=source, dst_ref=target, send_sem=send_sem, recv_sem=recv_sem,
            device_id=device, device_id_type=MESH,
        ).start()

    loads = [
        pltpu.make_async_copy(q_hbm, q_in, load_sem.at[0]),
        pltpu.make_async_copy(u_hbm, u_in, load_sem.at[1]),
        pltpu.make_async_copy(v_hbm, v_in, load_sem.at[2]),
    ]
    for load in loads:
        load.start()
    tables = [
        pltpu.make_async_copy(source, target, table_sem.at[i])
        for i, (source, target) in enumerate(
            ((cut_hbm, cut_ref), (waves_hbm, waves_ref), (fh_hbm, fh), (fl_hbm, fl), (ih_hbm, ih), (il_hbm, il))
        )
    ]

    barrier = pltpu.get_barrier_semaphore()
    for target, pole, late in ((north, low_edge, late_for_north), (south, high_edge, late_for_south)):
        @pl.when(jnp.logical_not(jnp.logical_or(pole, late)))
        def _():
            greet(target)

    team_member = jnp.logical_or(main, helper)

    @pl.when(team_member)
    def _():
        for t in range(1, SECTORS):
            @pl.when(t > rank)
            def _():
                greet((lat, ranked(t)))

    @pl.when(jnp.logical_not(team_member))
    def _():
        greet(west)
        greet(east)

    @pl.when(helper)
    def _():
        greet((mate, lon))

    greeted = jnp.where(main, rank + 1, jnp.where(helper, rank, 2))
    for pole, late in ((low_edge, north_late), (high_edge, south_late)):
        greeted += jnp.where(jnp.logical_or(pole, late), 0, 1)
    pl.semaphore_wait(barrier, greeted)

    @pl.when(team_member)
    def _():
        for t in range(SECTORS - 1):
            @pl.when(t < rank)
            def _():
                pl.semaphore_signal(
                    hello.at[rank], inc=1, device_id=(lat, ranked(t)), device_id_type=MESH
                )

    for load in loads:
        load.wait()

    @pl.when(team_member)
    def _():
        for table in tables:
            table.start()

    sector = q_in.shape[-1]
    lane = lax.broadcasted_iota(jnp.int32, (16, LANES), 1)
    east_pack = jnp.zeros((16, LANES), jnp.float32)
    west_pack = jnp.zeros((16, LANES), jnp.float32)
    for f in range(fields + 1):
        for r in range(rows):
            s = f * rows + r
            source, pad = (q_in.at[f], q_pad.at[f]) if f < fields else (u_in, u_pad)
            pad[r, :, pl.ds(0, sector)] = source[r]
            x = pad[r]
            west_pack = jnp.where(lane == s, pltpu.roll(x, s, 1), west_pack)
            east_pack = jnp.where(
                lane == s, pltpu.roll(x, (s - (sector - 1)) % LANES, 1), east_pack
            )
    for r in range(rows):
        v_pad[r, :, pl.ds(0, sector)] = v_in[r]
    side_out[0] = west_pack
    side_out[1] = east_pack
    for side, row in ((0, 0), (1, rows - 1)):
        for f in range(fields):
            edge_out[side, f] = q_pad[f, row]
        edge_out[side, fields] = v_pad[row]

    def edge_copy(side, slot, target):
        return pltpu.make_async_remote_copy(
            src_ref=edge_out.at[side],
            dst_ref=edge_in.at[slot],
            send_sem=halo_send.at[side],
            recv_sem=halo_recv.at[slot],
            device_id=target,
            device_id_type=MESH,
        )

    to_north = edge_copy(0, jnp.where(low_edge, 0, 1), north)
    to_south = edge_copy(1, jnp.where(high_edge, 1, 0), south)
    to_west = pltpu.make_async_remote_copy(
        src_ref=side_out.at[0], dst_ref=side_in.at[1], send_sem=halo_send.at[2],
        recv_sem=halo_recv.at[2], device_id=west, device_id_type=MESH,
    )
    to_east = pltpu.make_async_remote_copy(
        src_ref=side_out.at[1], dst_ref=side_in.at[0], send_sem=halo_send.at[3],
        recv_sem=halo_recv.at[3], device_id=east, device_id_type=MESH,
    )
    for copy, pole, late in ((to_north, low_edge, north_late), (to_south, high_edge, south_late)):
        @pl.when(jnp.logical_not(jnp.logical_or(pole, late)))
        def _():
            copy.start()

    @pl.when(jnp.logical_not(team_member))
    def _():
        to_west.start()
        to_east.start()

    @pl.when(main)
    def _():
        @pl.when(rank > 0)
        def _():
            to_west.start()

        @pl.when(rank < SECTORS - 1)
        def _():
            pl.semaphore_wait(hello.at[rank + 1], 1)

        to_east.start()

        @pl.when(rank == 0)
        def _():
            pl.semaphore_wait(hello.at[SECTORS - 1], 1)
            to_west.start()

    def edges_arrive():
        edge_copy(0, 0, north).wait_recv()
        edge_copy(1, 1, south).wait_recv()
        for copy, late in ((to_north, north_late), (to_south, south_late)):
            @pl.when(late)
            def _():
                copy.start()

    ghosts = set()
    flip_north = jnp.where(low_edge, -1.0, 1.0)
    flip_south = jnp.where(high_edge, -1.0, 1.0)

    def set_ghosts(slabs):
        from_west, from_east = side_in[0], side_in[1]
        wanted = []
        for p in slabs:
            f, r = order[p]
            if (fields, r) not in ghosts:
                wanted.append((fields, r))
                ghosts.add((fields, r))
            wanted.append((f, r))
        for f, r in wanted:
            s = f * rows + r
            pad = q_pad.at[f] if f < fields else u_pad
            x = jnp.where(lane == sector, pltpu.roll(from_east, (sector - s) % LANES, 1), pad[r])
            pad[r] = jnp.where(lane == LANES - 1, pltpu.roll(from_west, (LANES - 1 - s) % LANES, 1), x)

    def step(slabs, winds):
        for p in slabs:
            f, r = order[p]
            if r not in winds:
                u = u_pad[r]
                v = v_pad[r]
                v_next = v_pad[r + 1] if r < rows - 1 else edge_in[1, fields] * flip_south
                v_previous = v_pad[r - 1] if r > 0 else edge_in[0, fields] * flip_north
                speeds = (
                    0.5 * (u + pltpu.roll(u, LANES - 1, 1)), 0.5 * (pltpu.roll(u, 1, 1) + u),
                    0.5 * (v + v_next), 0.5 * (v_previous + v),
                )
                winds[r] = [(jnp.maximum(x, 0.0), jnp.minimum(x, 0.0)) for x in speeds]
            (e_plus, e_minus), (w_plus, w_minus), (s_plus, s_minus), (n_plus, n_minus) = winds[r]
            q = q_pad[f, r]
            q_next = q_pad[f, r + 1] if r < rows - 1 else edge_in[1, f]
            q_previous = q_pad[f, r - 1] if r > 0 else edge_in[0, f]
            east_flux = e_plus * q + e_minus * pltpu.roll(q, LANES - 1, 1)
            west_flux = w_plus * pltpu.roll(q, 1, 1) + w_minus * q
            south_flux = s_plus * q + s_minus * q_next
            north_flux = n_plus * q_previous + n_minus * q
            new = q - (east_flux - west_flux) - (south_flux - north_flux)
            new = jnp.where(lane < sector, new, 0.0)
            stepped[2 * p] = new[:8]
            stepped[2 * p + 1] = new[8:]

    def hand_out(source):
        for p, (f, r) in enumerate(order):
            out_ref[pl.ds(2 * (f * rows + r), 2)] = source[pl.ds(2 * p, 2)]

    @pl.when(main)
    def _():
        tables[0].wait()
        for r in range(rows):
            limit = jnp.full((1, LANES), cut_ref[r], jnp.int32).astype(jnp.float32)
            cut_out[pl.ds(r, 1)] = limit
            cut_rows[pl.ds(r, 1)] = limit
        cut_out[pl.ds(rows, 16 - rows)] = jnp.zeros((16 - rows, LANES), jnp.float32)
        send(cut_out, cut_rows, cut_send, cut_recv, (mate, lon))

    @pl.when(helper)
    def _():
        for phase in range(2):
            for group in range(3):
                count = (8, 6)[phase]
                chunk = relay.at[pl.ds(24 * phase + count * group, count)]
                waiter(chunk, relay_recv.at[3 * phase + group]).wait()
                for to in range(4 * group, 4 * group + 4):
                    c = to % 2
                    n = 2 - phase * c
                    at = 24 * phase + count * group + count // 2 * (to // 2 % 2) + 2 * c

                    if phase == 0:
                        @pl.when(to > rank)
                        def _():
                            pl.semaphore_wait(hello.at[to], 1)

                    @pl.when(lon != to)
                    def _():
                        send(
                            relay.at[pl.ds(at, n)], land.at[lon, pl.ds(2 * phase, n)],
                            go_send.at[phase], go_recv.at[phase], (lat, to),
                        )

                    @pl.when(lon == to)
                    def _():
                        land[lon, pl.ds(2 * phase, n)] = relay[pl.ds(at, n)]

        to_west.start()
        to_east.start()

    def sides_arrive():
        to_west.wait_recv()
        to_east.wait_recv()

    @pl.when(main)
    def _():
        winds = {}
        ghosts.clear()
        sides_arrive()

        def for_helper(phase):
            for group in range(3):
                count = (8, 6)[phase]
                at = 48 * phase + count * group
                step(range(at // 2, (at + count) // 2), winds)
                send(
                    stepped.at[pl.ds(at, count)], relay.at[pl.ds(24 * phase + count * group, count)],
                    relay_send, relay_recv.at[3 * phase + group], (mate, lon),
                )

        def for_line(phase):
            at = (24, 66)[phase]
            for t in range(SECTORS):
                to = ranked(t)
                if phase == 0:
                    @pl.when(jnp.logical_and(t > rank + 1, jnp.logical_or(rank > 0, t < SECTORS - 1)))
                    def _():
                        pl.semaphore_wait(hello.at[t], 1)

                @pl.when(t != rank)
                def _():
                    send(
                        stepped.at[pl.ds(at + 2 * to, 2)], land.at[lon, pl.ds(2 * phase, 2)],
                        go_send.at[phase], go_recv.at[phase], (lat, to),
                    )
            land[lon, pl.ds(2 * phase, 2)] = stepped[pl.ds(at + 2 * lon, 2)]

        set_ghosts(range(24))
        for_helper(0)
        step(range(12, 24), winds)
        for_line(0)
        for copy, pole in ((to_north, low_edge), (to_south, high_edge)):
            @pl.when(pole)
            def _():
                copy.start()

        set_ghosts(range(24, 45))
        for_helper(1)
        step(range(33, 35), winds)
        edges_arrive()
        step(range(35, 45), winds)
        for_line(1)

    @pl.when(helper)
    def _():
        waiter(cut_rows, cut_recv).wait()
        tables[0].wait()

    @pl.when(jnp.logical_or(main, helper))
    def _():
        short = jnp.logical_and(helper, core == 1)
        for table in tables[1:]:
            table.wait()
        for phase in range(2):
            for n in range(1, 3) if phase else (2,):
                @pl.when(short == (n == 1) if phase else core >= 0)
                def _():
                    waiter(land.at[pl.ds(0, 11), pl.ds(0, n)], go_recv.at[phase]).wait()
            x = [land[j, pl.ds(2 * phase, 2)].reshape(16, LANES) for j in range(SECTORS)]
            limits = []
            for i in range(2):
                p = (starts[phase] + i) // 2
                row = 1 + p // fields
                row = jnp.where(p < fields * (rows - 1), jnp.where(row < rows - 1, row, 0), rows - 1)
                limit = jnp.broadcast_to(cut_rows[pl.ds(row, 1)], (8, LANES))
                limits.append(jnp.concatenate([limit, limit], axis=1))
            limits = jnp.concatenate(limits, axis=0)
            w = []
            for block, (a, b) in enumerate(sector_dft(x)):
                z = split_dot(jnp.concatenate([a, b], axis=1), fh[block], fl[block])
                wave = jnp.broadcast_to(waves_ref[pl.ds(block, 1)], (16, 256))
                z = jnp.where(wave <= limits, z, 0.0)
                y = split_dot(z, ih[block], il[block])
                w.append((y[:, :LANES], y[:, LANES:]))
            for j, y in enumerate(sector_inverse(w)):
                done[j, pl.ds(2 * phase, 2)] = y.reshape(2, 8, LANES)
            for n in range(1, 3) if phase else (2,):
                @pl.when(short == (n == 1) if phase else core >= 0)
                def _():
                    def back(to):
                        send(
                            done.at[to, pl.ds(2 * phase, n)], result.at[pl.ds(starts[phase], n)],
                            back_send.at[phase], back_recv.at[phase], (team, to),
                        )

                    for offset in OFFSETS:
                        back(turned(offset))

                    @pl.when(helper)
                    def _():
                        back(lon)

            @pl.when(main)
            def _():
                result[pl.ds(starts[phase], 2)] = done[lon, pl.ds(2 * phase, 2)]

    @pl.when(main)
    def _():
        waiter(result.at[pl.ds(0, 46)], back_recv.at[0]).wait()
        waiter(result.at[pl.ds(0, 40)], back_recv.at[1]).wait()
        hand_out(result)
        for phase in range(2):
            waiter(stepped.at[pl.ds(0, 22)], go_send.at[phase]).wait()
            waiter(stepped.at[pl.ds(0, 22)], back_send.at[phase]).wait()
        waiter(stepped.at[pl.ds(0, 42)], relay_send).wait()
        waiter(cut_out, cut_send).wait()

    @pl.when(helper)
    def _():
        waiter(stepped.at[pl.ds(0, 22)], go_send.at[0]).wait()
        waiter(stepped.at[pl.ds(0, 24)], back_send.at[0]).wait()
        for c in range(2):
            @pl.when(core == c)
            def _():
                waiter(stepped.at[pl.ds(0, 16 + c)], go_send.at[1]).wait()
                waiter(stepped.at[pl.ds(0, 24 - 12 * c)], back_send.at[1]).wait()

    @pl.when(jnp.logical_not(main))
    def _():
        ghosts.clear()
        sides_arrive()
        set_ghosts(range(len(order)))
        edges_arrive()
        step(range(len(order)), {})
        hand_out(stepped)

    for copy in (to_north, to_south, to_west, to_east):
        copy.wait_send()


def body(lat_count, tracers, zonal_wind, meridional_wind, cutoff):
    fields, levels, rows, sector = tracers.shape
    q = jnp.transpose(tracers, (0, 2, 1, 3))
    u = jnp.transpose(zonal_wind, (1, 0, 2))
    v = jnp.transpose(meridional_wind, (1, 0, 2))
    tables = [jnp.asarray(t) for t in dft_tables(SECTORS * sector, sector)]
    tiles = fields * rows * 2
    f32, bf16 = jnp.float32, jnp.bfloat16
    dma = pltpu.SemaphoreType.DMA
    hbm = pl.BlockSpec(memory_space=pltpu.HBM)
    vmem = pl.BlockSpec(memory_space=pltpu.VMEM)
    out = pl.pallas_call(
        functools.partial(kernel, lat_count, fields, rows),
        out_shape=jax.ShapeDtypeStruct((tiles, 8, LANES), f32),
        in_specs=[hbm] * 9,
        out_specs=vmem,
        scratch_shapes=[
            pltpu.VMEM((fields, rows, levels, sector), f32),
            pltpu.VMEM((rows, levels, sector), f32),
            pltpu.VMEM((rows, levels, sector), f32),
            pltpu.VMEM((fields, rows, levels, LANES), f32),
            pltpu.VMEM((rows, levels, LANES), f32),
            pltpu.VMEM((rows, levels, LANES), f32),
            pltpu.VMEM((2, fields + 1, levels, LANES), f32),
            pltpu.VMEM((2, fields + 1, levels, LANES), f32),
            pltpu.VMEM((2, levels, LANES), f32),
            pltpu.VMEM((2, levels, LANES), f32),
            pltpu.VMEM((6, 256, 256), bf16),
            pltpu.VMEM((6, 256, 256), bf16),
            pltpu.VMEM((6, 256, 256), bf16),
            pltpu.VMEM((6, 256, 256), bf16),
            pltpu.VMEM((8, 256), f32),
            pltpu.SMEM((rows,), jnp.int32),
            pltpu.VMEM((16, LANES), f32),
            pltpu.VMEM((16, LANES), f32),
            pltpu.VMEM((tiles, 8, LANES), f32),
            pltpu.VMEM((42, 8, LANES), f32),
            pltpu.VMEM((SECTORS, 4, 8, LANES), f32),
            pltpu.VMEM((SECTORS, 4, 8, LANES), f32),
            pltpu.VMEM((tiles, 8, LANES), f32),
            dma((3,)), dma((6,)), dma((4,)), dma((4,)), dma, dma, dma, dma((6,)), pltpu.SemaphoreType.REGULAR((SECTORS,)),
            dma((2,)), dma((2,)), dma((2,)), dma((2,)),
        ],
        compiler_params=pltpu.CompilerParams(
            collective_id=0, has_side_effects=True, vmem_limit_bytes=60 * 1024 * 1024
        ),
    )(q, u, v, cutoff, *tables)
    out = out.reshape(fields, rows, levels, LANES)[..., :sector]
    return jnp.transpose(out, (0, 2, 1, 3))


def solution(mesh):
    in_specs = (P(None, None, "lat", "lon"), P(None, "lat", "lon"), P(None, "lat", "lon"), P("lat"))
    out_specs = P(None, None, "lat", "lon")
    return jax.shard_map(
        functools.partial(body, mesh.shape["lat"]),
        mesh=mesh, in_specs=in_specs, out_specs=out_specs, check_vma=False,
    )
```

```python
import functools
import math

import jax
import jax.numpy as jnp
import ml_dtypes
import numpy as np
from jax import lax
from jax.experimental import pallas as pl
from jax.experimental.pallas import tpu as pltpu
from jax.sharding import PartitionSpec as P

MESH = pl.DeviceIdType.MESH
POLAR_ROWS = 96
SECTORS = 12
LANES = 128
STRIDE = 16
OFFSETS = (1, 11, 2, 10, 3, 9, 4, 8, 5, 7, 6)


def slab_order(fields, rows):
    order = [(f, r) for r in range(1, rows - 1) for f in range(fields)]
    return order + [(f, r) for r in (0, rows - 1) for f in range(fields)]


def split_bf16(table):
    high = table.astype(ml_dtypes.bfloat16)
    low = (table - high.astype(np.float64)).astype(ml_dtypes.bfloat16)
    return high, low


@functools.lru_cache(maxsize=None)
def dft_tables(circle, sector):
    forward = np.zeros((6, 256, 256))
    inverse = np.zeros((6, 256, 256))
    waves = np.zeros((8, 256))
    m = np.arange(sector)

    def put(block, column, k, part, weight, real_half):
        phase = 2.0 * math.pi * ((m * k) % circle) / circle
        cos, sin = np.cos(phase), np.sin(phase)
        waves[block, column] = min(k, circle - k)
        if real_half is not None:
            base = 128 * real_half
            row = cos if part == 0 else -sin
            forward[block, base : base + sector, column] = row
            inverse[block, column, base : base + sector] = weight * row / circle
            return
        if part == 0:
            forward[block, :sector, column] = cos
            forward[block, 128 : 128 + sector, column] = sin
            inverse[block, column, :sector] = weight * cos / circle
            inverse[block, column, 128 : 128 + sector] = weight * sin / circle
        else:
            forward[block, :sector, column] = -sin
            forward[block, 128 : 128 + sector, column] = cos
            inverse[block, column, :sector] = -weight * sin / circle
            inverse[block, column, 128 : 128 + sector] = weight * cos / circle

    half = sector // 2
    for q in range(half + 1):
        put(0, q, SECTORS * q, 0, 1.0 if q in (0, half) else 2.0, 0)
    for q in range(1, half):
        put(0, half + q, SECTORS * q, 1, 2.0, 0)
    for q in range(half):
        put(0, 128 + q, 6 + SECTORS * q, 0, 2.0, 1)
        put(0, 128 + half + q, 6 + SECTORS * q, 1, 2.0, 1)
    for r in range(1, 6):
        for q in range(sector):
            put(r, q, r + SECTORS * q, 0, 2.0, None)
            put(r, 128 + q, r + SECTORS * q, 1, 2.0, None)
    return split_bf16(forward) + split_bf16(inverse) + (waves.astype(np.float32),)


def combine(terms):
    groups = {}
    for coefficient, array in terms:
        size = round(abs(coefficient), 6)
        if size < 1e-6:
            continue
        groups.setdefault(size, []).append((coefficient, array))
    total = None
    for size in sorted(groups, reverse=True):
        part = None
        for coefficient, array in groups[size]:
            if part is None:
                part = array if coefficient > 0 else -array
            else:
                part = part + array if coefficient > 0 else part - array
        if size != 1.0:
            part = part * abs(groups[size][0][0])
        total = part if total is None else total + part
    return total


def cos12(i):
    return math.cos(2.0 * math.pi * (i % 12) / 12)


def sin12(i):
    return math.sin(2.0 * math.pi * (i % 12) / 12)


def sector_dft(x):
    sums = [None] + [x[j] + x[12 - j] for j in range(1, 6)]
    differences = [None] + [x[j] - x[12 - j] for j in range(1, 6)]
    real, imag = [], []
    for r in range(7):
        terms = [(1.0, x[0]), (1.0 if r % 2 == 0 else -1.0, x[6])]
        terms += [(cos12(j * r), sums[j]) for j in range(1, 6)]
        real.append(combine(terms))
        if 0 < r < 6:
            imag.append(combine([(-sin12(j * r), differences[j]) for j in range(1, 6)]))
        else:
            imag.append(None)
    return [(real[0], real[6])] + [(real[r], imag[r]) for r in range(1, 6)]


def sector_inverse(w):
    out = [None] * 12
    for j in range(7):
        terms = [(1.0, w[0][0]), (1.0 if j % 2 == 0 else -1.0, w[0][1])]
        terms += [(cos12(j * r), w[r][0]) for r in range(1, 6)]
        even = combine(terms)
        if j in (0, 6):
            out[j] = even
            continue
        odd = combine([(sin12(j * r), w[r][1]) for r in range(1, 6)])
        out[j] = even - odd
        out[12 - j] = even + odd
    return out


def split_dot(x, high, low):
    x_high = x.astype(jnp.bfloat16)
    x_low = (x - x_high.astype(jnp.float32)).astype(jnp.bfloat16)
    dot = functools.partial(jnp.dot, preferred_element_type=jnp.float32)
    return dot(x_high, high) + (dot(x_low, high) + dot(x_high, low))


def kernel(
    lat_count, fields, rows,
    q_hbm, u_hbm, v_hbm, cut_hbm, fh_hbm, fl_hbm, ih_hbm, il_hbm, waves_hbm,
    out_ref,
    q_in, u_in, v_in, q_pad, u_pad, v_pad, edge_out, edge_in, side_out, side_in,
    fh, fl, ih, il, waves_ref, cut_ref, cut_out, cut_rows, stepped, relay, land, done, result,
    load_sem, table_sem, halo_send, halo_recv, cut_send, cut_recv, relay_send, relay_recv, hello,
    go_send, go_recv, back_send, back_recv,
):
    lat, lon = lax.axis_index("lat"), lax.axis_index("lon")
    chip, core = lon // 2, lax.rem(lon, 2)
    tiles = 2 * fields * rows
    low_edge, high_edge = lat == 0, lat == lat_count - 1
    caps = -(-POLAR_ROWS // rows)
    in_north, in_south = lat < caps, lat >= lat_count - caps
    main = jnp.logical_or(in_north, in_south)
    helper = jnp.logical_or(
        jnp.logical_and(lat >= STRIDE, lat < STRIDE + caps),
        jnp.logical_and(lat >= lat_count - STRIDE - caps, lat < lat_count - STRIDE),
    )
    mate = jnp.where(jnp.logical_or(in_north, lat >= lat_count // 2), STRIDE, -STRIDE)
    mate = lat + jnp.where(in_south, -STRIDE, mate)
    team = jnp.where(main, lat, mate)
    across = lax.rem(lon + 6, SECTORS)
    north = (jnp.where(low_edge, 0, lat - 1), jnp.where(low_edge, across, lon))
    south = (jnp.where(high_edge, lat, lat + 1), jnp.where(high_edge, across, lon))
    west = (lat, lax.rem(lon + SECTORS - 1, SECTORS))
    east = (lat, lax.rem(lon + 1, SECTORS))
    starts = (
        jnp.where(main, 24 + 2 * lon, 2 * lon),
        jnp.where(main, 66 + 2 * lon, 48 + 3 * chip + 2 * core),
    )
    first = jnp.where(low_edge, 1, 0)
    rank = lax.rem(lon + SECTORS - first, SECTORS)
    eager = lax.rem(lat, STRIDE) < STRIDE // 2
    order = slab_order(fields, rows)
    half = STRIDE // 2
    place = lax.rem(lat, STRIDE)
    far_north = jnp.logical_and(lax.rem(place, half) == 0, jnp.logical_not(low_edge))
    far_south = jnp.logical_and(lax.rem(place, half) == half - 1, jnp.logical_not(high_edge))
    upper = place >= half
    north_late = jnp.logical_or(
        jnp.logical_and(far_north, jnp.logical_not(upper)), jnp.logical_and(lat == 1, lon == 0)
    )
    south_late = jnp.logical_and(far_south, jnp.logical_not(upper))
    late_for_north = jnp.logical_and(far_north, upper)
    late_for_south = jnp.logical_or(
        jnp.logical_and(far_south, upper), jnp.logical_and(low_edge, lon == 0)
    )

    def ranked(t):
        return lax.rem(t + first, SECTORS)

    def turned(offset):
        return lax.rem(lon + offset, SECTORS)

    def greet(target):
        pl.semaphore_signal(barrier, inc=1, device_id=target, device_id_type=MESH)

    def waiter(ref, sem):
        return pltpu.make_async_copy(ref, ref, sem)

    def send(source, target, send_sem, recv_sem, device):
        pltpu.make_async_remote_copy(
            src_ref=source, dst_ref=target, send_sem=send_sem, recv_sem=recv_sem,
            device_id=device, device_id_type=MESH,
        ).start()

    loads = [
        pltpu.make_async_copy(q_hbm, q_in, load_sem.at[0]),
        pltpu.make_async_copy(u_hbm, u_in, load_sem.at[1]),
        pltpu.make_async_copy(v_hbm, v_in, load_sem.at[2]),
    ]
    for load in loads:
        load.start()
    tables = [
        pltpu.make_async_copy(source, target, table_sem.at[i])
        for i, (source, target) in enumerate(
            ((cut_hbm, cut_ref), (waves_hbm, waves_ref), (fh_hbm, fh), (fl_hbm, fl), (ih_hbm, ih), (il_hbm, il))
        )
    ]

    barrier = pltpu.get_barrier_semaphore()
    for target, pole, late in ((north, low_edge, late_for_north), (south, high_edge, late_for_south)):
        @pl.when(jnp.logical_not(jnp.logical_or(pole, late)))
        def _():
            greet(target)

    team_member = jnp.logical_or(main, helper)

    @pl.when(team_member)
    def _():
        for t in range(SECTORS):
            @pl.when(jnp.logical_or(t > rank, jnp.logical_and(t < rank, jnp.logical_not(eager))))
            def _():
                greet((lat, ranked(t)))

    @pl.when(jnp.logical_not(team_member))
    def _():
        greet(west)
        greet(east)

    @pl.when(helper)
    def _():
        greet((mate, lon))

    seen = jnp.where(eager, rank, SECTORS - 1)
    greeted = jnp.where(main, seen + 1, jnp.where(helper, seen, 2))
    for pole, late in ((low_edge, north_late), (high_edge, south_late)):
        greeted += jnp.where(jnp.logical_or(pole, late), 0, 1)
    pl.semaphore_wait(barrier, greeted)

    @pl.when(team_member)
    def _():
        for t in range(SECTORS - 1):
            @pl.when(jnp.logical_and(t < rank, eager))
            def _():
                pl.semaphore_signal(
                    hello.at[rank], inc=1, device_id=(lat, ranked(t)), device_id_type=MESH
                )

    for load in loads:
        load.wait()

    @pl.when(team_member)
    def _():
        for table in tables:
            table.start()

    sector = q_in.shape[-1]
    lane = lax.broadcasted_iota(jnp.int32, (16, LANES), 1)
    east_pack = jnp.zeros((16, LANES), jnp.float32)
    west_pack = jnp.zeros((16, LANES), jnp.float32)
    for f in range(fields + 1):
        for r in range(rows):
            s = f * rows + r
            source, pad = (q_in.at[f], q_pad.at[f]) if f < fields else (u_in, u_pad)
            pad[r, :, pl.ds(0, sector)] = source[r]
            x = pad[r]
            west_pack = jnp.where(lane == s, pltpu.roll(x, s, 1), west_pack)
            east_pack = jnp.where(
                lane == s, pltpu.roll(x, (s - (sector - 1)) % LANES, 1), east_pack
            )
    for r in range(rows):
        v_pad[r, :, pl.ds(0, sector)] = v_in[r]
    side_out[0] = west_pack
    side_out[1] = east_pack
    for side, row in ((0, 0), (1, rows - 1)):
        for f in range(fields):
            edge_out[side, f] = q_pad[f, row]
        edge_out[side, fields] = v_pad[row]

    def edge_copy(side, slot, target):
        return pltpu.make_async_remote_copy(
            src_ref=edge_out.at[side],
            dst_ref=edge_in.at[slot],
            send_sem=halo_send.at[side],
            recv_sem=halo_recv.at[slot],
            device_id=target,
            device_id_type=MESH,
        )

    to_north = edge_copy(0, jnp.where(low_edge, 0, 1), north)
    to_south = edge_copy(1, jnp.where(high_edge, 1, 0), south)
    to_west = pltpu.make_async_remote_copy(
        src_ref=side_out.at[0], dst_ref=side_in.at[1], send_sem=halo_send.at[2],
        recv_sem=halo_recv.at[2], device_id=west, device_id_type=MESH,
    )
    to_east = pltpu.make_async_remote_copy(
        src_ref=side_out.at[1], dst_ref=side_in.at[0], send_sem=halo_send.at[3],
        recv_sem=halo_recv.at[3], device_id=east, device_id_type=MESH,
    )
    for copy, pole, late in ((to_north, low_edge, north_late), (to_south, high_edge, south_late)):
        @pl.when(jnp.logical_not(jnp.logical_or(pole, late)))
        def _():
            copy.start()

    @pl.when(jnp.logical_not(team_member))
    def _():
        to_west.start()
        to_east.start()

    @pl.when(main)
    def _():
        @pl.when(rank > 0)
        def _():
            to_west.start()

        @pl.when(jnp.logical_and(rank < SECTORS - 1, eager))
        def _():
            pl.semaphore_wait(hello.at[rank + 1], 1)

        to_east.start()

        @pl.when(rank == 0)
        def _():
            @pl.when(eager)
            def _():
                pl.semaphore_wait(hello.at[SECTORS - 1], 1)

            to_west.start()

    def edges_arrive():
        edge_copy(0, 0, north).wait_recv()
        edge_copy(1, 1, south).wait_recv()
        for copy, late in ((to_north, north_late), (to_south, south_late)):
            @pl.when(late)
            def _():
                copy.start()

    ghosts = set()
    flip_north = jnp.where(low_edge, -1.0, 1.0)
    flip_south = jnp.where(high_edge, -1.0, 1.0)

    def set_ghosts(slabs):
        from_west, from_east = side_in[0], side_in[1]
        wanted = []
        for p in slabs:
            f, r = order[p]
            if (fields, r) not in ghosts:
                wanted.append((fields, r))
                ghosts.add((fields, r))
            wanted.append((f, r))
        for f, r in wanted:
            s = f * rows + r
            pad = q_pad.at[f] if f < fields else u_pad
            x = jnp.where(lane == sector, pltpu.roll(from_east, (sector - s) % LANES, 1), pad[r])
            pad[r] = jnp.where(lane == LANES - 1, pltpu.roll(from_west, (LANES - 1 - s) % LANES, 1), x)

    def step(slabs, winds):
        for p in slabs:
            f, r = order[p]
            if r not in winds:
                u = u_pad[r]
                v = v_pad[r]
                v_next = v_pad[r + 1] if r < rows - 1 else edge_in[1, fields] * flip_south
                v_previous = v_pad[r - 1] if r > 0 else edge_in[0, fields] * flip_north
                speeds = (
                    0.5 * (u + pltpu.roll(u, LANES - 1, 1)), 0.5 * (pltpu.roll(u, 1, 1) + u),
                    0.5 * (v + v_next), 0.5 * (v_previous + v),
                )
                winds[r] = [(jnp.maximum(x, 0.0), jnp.minimum(x, 0.0)) for x in speeds]
            (e_plus, e_minus), (w_plus, w_minus), (s_plus, s_minus), (n_plus, n_minus) = winds[r]
            q = q_pad[f, r]
            q_next = q_pad[f, r + 1] if r < rows - 1 else edge_in[1, f]
            q_previous = q_pad[f, r - 1] if r > 0 else edge_in[0, f]
            east_flux = e_plus * q + e_minus * pltpu.roll(q, LANES - 1, 1)
            west_flux = w_plus * pltpu.roll(q, 1, 1) + w_minus * q
            south_flux = s_plus * q + s_minus * q_next
            north_flux = n_plus * q_previous + n_minus * q
            new = q - (east_flux - west_flux) - (south_flux - north_flux)
            new = jnp.where(lane < sector, new, 0.0)
            stepped[2 * p] = new[:8]
            stepped[2 * p + 1] = new[8:]

    def hand_out(source):
        for p, (f, r) in enumerate(order):
            out_ref[f, r] = source[pl.ds(2 * p, 2)].reshape(16, LANES)[:, :sector]

    @pl.when(main)
    def _():
        tables[0].wait()
        for r in range(rows):
            limit = jnp.full((1, LANES), cut_ref[r], jnp.int32).astype(jnp.float32)
            cut_out[pl.ds(r, 1)] = limit
            cut_rows[pl.ds(r, 1)] = limit
        cut_out[pl.ds(rows, 16 - rows)] = jnp.zeros((16 - rows, LANES), jnp.float32)
        send(cut_out, cut_rows, cut_send, cut_recv, (mate, lon))

    @pl.when(helper)
    def _():
        for phase in range(2):
            for group in range(3):
                count = (8, 6)[phase]
                chunk = relay.at[pl.ds(24 * phase + count * group, count)]
                waiter(chunk, relay_recv.at[3 * phase + group]).wait()
                for to in range(4 * group, 4 * group + 4):
                    c = to % 2
                    n = 2 - phase * c
                    at = 24 * phase + count * group + count // 2 * (to // 2 % 2) + 2 * c

                    if phase == 0:
                        @pl.when(jnp.logical_and(to > rank, eager))
                        def _():
                            pl.semaphore_wait(hello.at[to], 1)

                    @pl.when(lon != to)
                    def _():
                        send(
                            relay.at[pl.ds(at, n)], land.at[lon, pl.ds(2 * phase, n)],
                            go_send.at[phase], go_recv.at[phase], (lat, to),
                        )

                    @pl.when(lon == to)
                    def _():
                        land[lon, pl.ds(2 * phase, n)] = relay[pl.ds(at, n)]

        to_west.start()
        to_east.start()

    def sides_arrive():
        to_west.wait_recv()
        to_east.wait_recv()

    @pl.when(main)
    def _():
        winds = {}
        ghosts.clear()
        sides_arrive()

        def for_helper(phase):
            for group in range(3):
                count = (8, 6)[phase]
                at = 48 * phase + count * group
                step(range(at // 2, (at + count) // 2), winds)
                send(
                    stepped.at[pl.ds(at, count)], relay.at[pl.ds(24 * phase + count * group, count)],
                    relay_send, relay_recv.at[3 * phase + group], (mate, lon),
                )

        def for_line(phase):
            at = (24, 66)[phase]
            for t in range(SECTORS):
                to = ranked(t)
                if phase == 0:
                    waits = jnp.logical_and(t > rank + 1, jnp.logical_or(rank > 0, t < SECTORS - 1))

                    @pl.when(jnp.logical_and(waits, eager))
                    def _():
                        pl.semaphore_wait(hello.at[t], 1)

                    for copy, pole in ((to_north, low_edge), (to_south, high_edge)):
                        @pl.when(jnp.logical_and(pole, to == across))
                        def _():
                            copy.start()

                @pl.when(t != rank)
                def _():
                    send(
                        stepped.at[pl.ds(at + 2 * to, 2)], land.at[lon, pl.ds(2 * phase, 2)],
                        go_send.at[phase], go_recv.at[phase], (lat, to),
                    )
            land[lon, pl.ds(2 * phase, 2)] = stepped[pl.ds(at + 2 * lon, 2)]

        set_ghosts(range(24))
        for_helper(0)
        step(range(12, 24), winds)
        for_line(0)
        set_ghosts(range(24, 45))
        for_helper(1)
        step(range(33, 35), winds)
        edges_arrive()
        step(range(35, 45), winds)
        for_line(1)

    @pl.when(helper)
    def _():
        waiter(cut_rows, cut_recv).wait()
        tables[0].wait()

    @pl.when(jnp.logical_or(main, helper))
    def _():
        short = jnp.logical_and(helper, core == 1)
        for table in tables[1:]:
            table.wait()
        for phase in range(2):
            for n in range(1, 3) if phase else (2,):
                @pl.when(short == (n == 1) if phase else core >= 0)
                def _():
                    waiter(land.at[pl.ds(0, 11), pl.ds(0, n)], go_recv.at[phase]).wait()
            x = [land[j, pl.ds(2 * phase, 2)].reshape(16, LANES) for j in range(SECTORS)]
            limits = []
            for i in range(2):
                p = (starts[phase] + i) // 2
                row = 1 + p // fields
                row = jnp.where(p < fields * (rows - 1), jnp.where(row < rows - 1, row, 0), rows - 1)
                limit = jnp.broadcast_to(cut_rows[pl.ds(row, 1)], (8, LANES))
                limits.append(jnp.concatenate([limit, limit], axis=1))
            limits = jnp.concatenate(limits, axis=0)
            w = []
            for block, (a, b) in enumerate(sector_dft(x)):
                z = split_dot(jnp.concatenate([a, b], axis=1), fh[block], fl[block])
                wave = jnp.broadcast_to(waves_ref[pl.ds(block, 1)], (16, 256))
                z = jnp.where(wave <= limits, z, 0.0)
                y = split_dot(z, ih[block], il[block])
                w.append((y[:, :LANES], y[:, LANES:]))
            for j, y in enumerate(sector_inverse(w)):
                done[j, pl.ds(2 * phase, 2)] = y.reshape(2, 8, LANES)
            for n in range(1, 3) if phase else (2,):
                @pl.when(short == (n == 1) if phase else core >= 0)
                def _():
                    def back(to):
                        send(
                            done.at[to, pl.ds(2 * phase, n)], result.at[pl.ds(starts[phase], n)],
                            back_send.at[phase], back_recv.at[phase], (team, to),
                        )

                    for offset in OFFSETS:
                        back(turned(offset))

                    @pl.when(helper)
                    def _():
                        back(lon)

            @pl.when(main)
            def _():
                result[pl.ds(starts[phase], 2)] = done[lon, pl.ds(2 * phase, 2)]

    @pl.when(main)
    def _():
        waiter(result.at[pl.ds(0, 46)], back_recv.at[0]).wait()
        waiter(result.at[pl.ds(0, 40)], back_recv.at[1]).wait()
        hand_out(result)
        for phase in range(2):
            waiter(stepped.at[pl.ds(0, 22)], go_send.at[phase]).wait()
            waiter(stepped.at[pl.ds(0, 22)], back_send.at[phase]).wait()
        waiter(stepped.at[pl.ds(0, 42)], relay_send).wait()
        waiter(cut_out, cut_send).wait()

    @pl.when(helper)
    def _():
        waiter(stepped.at[pl.ds(0, 22)], go_send.at[0]).wait()
        waiter(stepped.at[pl.ds(0, 24)], back_send.at[0]).wait()
        for c in range(2):
            @pl.when(core == c)
            def _():
                waiter(stepped.at[pl.ds(0, 16 + c)], go_send.at[1]).wait()
                waiter(stepped.at[pl.ds(0, 24 - 12 * c)], back_send.at[1]).wait()

    @pl.when(jnp.logical_not(main))
    def _():
        ghosts.clear()
        sides_arrive()
        set_ghosts(range(len(order)))
        edges_arrive()
        step(range(len(order)), {})
        hand_out(stepped)

    for copy in (to_north, to_south, to_west, to_east):
        copy.wait_send()


def body(lat_count, tracers, zonal_wind, meridional_wind, cutoff):
    fields, levels, rows, sector = tracers.shape
    q = jnp.transpose(tracers, (0, 2, 1, 3))
    u = jnp.transpose(zonal_wind, (1, 0, 2))
    v = jnp.transpose(meridional_wind, (1, 0, 2))
    tables = [jnp.asarray(t) for t in dft_tables(SECTORS * sector, sector)]
    tiles = fields * rows * 2
    f32, bf16 = jnp.float32, jnp.bfloat16
    dma = pltpu.SemaphoreType.DMA
    hbm = pl.BlockSpec(memory_space=pltpu.HBM)
    vmem = pl.BlockSpec(memory_space=pltpu.VMEM)
    out = pl.pallas_call(
        functools.partial(kernel, lat_count, fields, rows),
        out_shape=jax.ShapeDtypeStruct((fields, rows, levels, sector), f32),
        in_specs=[hbm] * 9,
        out_specs=vmem,
        scratch_shapes=[
            pltpu.VMEM((fields, rows, levels, sector), f32),
            pltpu.VMEM((rows, levels, sector), f32),
            pltpu.VMEM((rows, levels, sector), f32),
            pltpu.VMEM((fields, rows, levels, LANES), f32),
            pltpu.VMEM((rows, levels, LANES), f32),
            pltpu.VMEM((rows, levels, LANES), f32),
            pltpu.VMEM((2, fields + 1, levels, LANES), f32),
            pltpu.VMEM((2, fields + 1, levels, LANES), f32),
            pltpu.VMEM((2, levels, LANES), f32),
            pltpu.VMEM((2, levels, LANES), f32),
            pltpu.VMEM((6, 256, 256), bf16),
            pltpu.VMEM((6, 256, 256), bf16),
            pltpu.VMEM((6, 256, 256), bf16),
            pltpu.VMEM((6, 256, 256), bf16),
            pltpu.VMEM((8, 256), f32),
            pltpu.SMEM((rows,), jnp.int32),
            pltpu.VMEM((16, LANES), f32),
            pltpu.VMEM((16, LANES), f32),
            pltpu.VMEM((tiles, 8, LANES), f32),
            pltpu.VMEM((42, 8, LANES), f32),
            pltpu.VMEM((SECTORS, 4, 8, LANES), f32),
            pltpu.VMEM((SECTORS, 4, 8, LANES), f32),
            pltpu.VMEM((tiles, 8, LANES), f32),
            dma((3,)), dma((6,)), dma((4,)), dma((4,)), dma, dma, dma, dma((6,)), pltpu.SemaphoreType.REGULAR((SECTORS,)),
            dma((2,)), dma((2,)), dma((2,)), dma((2,)),
        ],
        compiler_params=pltpu.CompilerParams(
            collective_id=0, has_side_effects=True, vmem_limit_bytes=60 * 1024 * 1024
        ),
    )(q, u, v, cutoff, *tables)
    return jnp.transpose(out, (0, 2, 1, 3))


def solution(mesh):
    in_specs = (P(None, None, "lat", "lon"), P(None, "lat", "lon"), P(None, "lat", "lon"), P("lat"))
    out_specs = P(None, None, "lat", "lon")
    return jax.shard_map(
        functools.partial(body, mesh.shape["lat"]),
        mesh=mesh, in_specs=in_specs, out_specs=out_specs, check_vma=False,
    )
```

```python
import functools
import math

import jax
import jax.numpy as jnp
import ml_dtypes
import numpy as np
from jax import lax
from jax.experimental import pallas as pl
from jax.experimental.pallas import tpu as pltpu
from jax.sharding import PartitionSpec as P

MESH = pl.DeviceIdType.MESH
POLAR_ROWS = 96
SECTORS = 12
LANES = 128
STRIDE = 16
OFFSETS = (1, 11, 2, 10, 3, 9, 4, 8, 5, 7, 6)


def slab_order(fields, rows):
    order = [(f, r) for r in range(1, rows - 1) for f in range(fields)]
    return order + [(f, r) for r in (0, rows - 1) for f in range(fields)]


def split_bf16(table):
    high = table.astype(ml_dtypes.bfloat16)
    low = (table - high.astype(np.float64)).astype(ml_dtypes.bfloat16)
    return high, low


@functools.lru_cache(maxsize=None)
def dft_tables(circle, sector):
    forward = np.zeros((6, 256, 256))
    inverse = np.zeros((6, 256, 256))
    waves = np.zeros((8, 256))
    m = np.arange(sector)

    def put(block, column, k, part, weight, real_half):
        phase = 2.0 * math.pi * ((m * k) % circle) / circle
        cos, sin = np.cos(phase), np.sin(phase)
        waves[block, column] = min(k, circle - k)
        if real_half is not None:
            base = 128 * real_half
            row = cos if part == 0 else -sin
            forward[block, base : base + sector, column] = row
            inverse[block, column, base : base + sector] = weight * row / circle
            return
        if part == 0:
            forward[block, :sector, column] = cos
            forward[block, 128 : 128 + sector, column] = sin
            inverse[block, column, :sector] = weight * cos / circle
            inverse[block, column, 128 : 128 + sector] = weight * sin / circle
        else:
            forward[block, :sector, column] = -sin
            forward[block, 128 : 128 + sector, column] = cos
            inverse[block, column, :sector] = -weight * sin / circle
            inverse[block, column, 128 : 128 + sector] = weight * cos / circle

    half = sector // 2
    for q in range(half + 1):
        put(0, q, SECTORS * q, 0, 1.0 if q in (0, half) else 2.0, 0)
    for q in range(1, half):
        put(0, half + q, SECTORS * q, 1, 2.0, 0)
    for q in range(half):
        put(0, 128 + q, 6 + SECTORS * q, 0, 2.0, 1)
        put(0, 128 + half + q, 6 + SECTORS * q, 1, 2.0, 1)
    for r in range(1, 6):
        for q in range(sector):
            put(r, q, r + SECTORS * q, 0, 2.0, None)
            put(r, 128 + q, r + SECTORS * q, 1, 2.0, None)
    return split_bf16(forward) + split_bf16(inverse) + (waves.astype(np.float32),)


def combine(terms):
    groups = {}
    for coefficient, array in terms:
        size = round(abs(coefficient), 6)
        if size < 1e-6:
            continue
        groups.setdefault(size, []).append((coefficient, array))
    total = None
    for size in sorted(groups, reverse=True):
        part = None
        for coefficient, array in groups[size]:
            if part is None:
                part = array if coefficient > 0 else -array
            else:
                part = part + array if coefficient > 0 else part - array
        if size != 1.0:
            part = part * abs(groups[size][0][0])
        total = part if total is None else total + part
    return total


def cos12(i):
    return math.cos(2.0 * math.pi * (i % 12) / 12)


def sin12(i):
    return math.sin(2.0 * math.pi * (i % 12) / 12)


def sector_dft(x):
    sums = [None] + [x[j] + x[12 - j] for j in range(1, 6)]
    differences = [None] + [x[j] - x[12 - j] for j in range(1, 6)]
    real, imag = [], []
    for r in range(7):
        terms = [(1.0, x[0]), (1.0 if r % 2 == 0 else -1.0, x[6])]
        terms += [(cos12(j * r), sums[j]) for j in range(1, 6)]
        real.append(combine(terms))
        if 0 < r < 6:
            imag.append(combine([(-sin12(j * r), differences[j]) for j in range(1, 6)]))
        else:
            imag.append(None)
    return [(real[0], real[6])] + [(real[r], imag[r]) for r in range(1, 6)]


def sector_inverse(w):
    out = [None] * 12
    for j in range(7):
        terms = [(1.0, w[0][0]), (1.0 if j % 2 == 0 else -1.0, w[0][1])]
        terms += [(cos12(j * r), w[r][0]) for r in range(1, 6)]
        even = combine(terms)
        if j in (0, 6):
            out[j] = even
            continue
        odd = combine([(sin12(j * r), w[r][1]) for r in range(1, 6)])
        out[j] = even - odd
        out[12 - j] = even + odd
    return out


def split_dot(x, high, low):
    x_high = x.astype(jnp.bfloat16)
    x_low = (x - x_high.astype(jnp.float32)).astype(jnp.bfloat16)
    dot = functools.partial(jnp.dot, preferred_element_type=jnp.float32)
    return dot(x_high, high) + (dot(x_low, high) + dot(x_high, low))


def kernel(
    lat_count, fields, rows,
    q_hbm, u_hbm, v_hbm, cut_hbm, fh_hbm, fl_hbm, ih_hbm, il_hbm, waves_hbm,
    out_ref,
    q_in, u_in, v_in, q_pad, u_pad, v_pad, edge_out, edge_in, side_out, side_in,
    fh, fl, ih, il, waves_ref, cut_ref, cut_out, cut_rows, stepped, relay, land, done, result,
    load_sem, table_sem, halo_send, halo_recv, cut_send, cut_recv, relay_send, relay_recv, hello,
    go_send, go_recv, back_send, back_recv,
):
    lat, lon = lax.axis_index("lat"), lax.axis_index("lon")
    chip, core = lon // 2, lax.rem(lon, 2)
    tiles = 2 * fields * rows
    low_edge, high_edge = lat == 0, lat == lat_count - 1
    caps = -(-POLAR_ROWS // rows)
    in_north, in_south = lat < caps, lat >= lat_count - caps
    main = jnp.logical_or(in_north, in_south)
    helper = jnp.logical_or(
        jnp.logical_and(lat >= STRIDE, lat < STRIDE + caps),
        jnp.logical_and(lat >= lat_count - STRIDE - caps, lat < lat_count - STRIDE),
    )
    mate = jnp.where(jnp.logical_or(in_north, lat >= lat_count // 2), STRIDE, -STRIDE)
    mate = lat + jnp.where(in_south, -STRIDE, mate)
    team = jnp.where(main, lat, mate)
    across = lax.rem(lon + 6, SECTORS)
    north = (jnp.where(low_edge, 0, lat - 1), jnp.where(low_edge, across, lon))
    south = (jnp.where(high_edge, lat, lat + 1), jnp.where(high_edge, across, lon))
    west = (lat, lax.rem(lon + SECTORS - 1, SECTORS))
    east = (lat, lax.rem(lon + 1, SECTORS))
    first = jnp.where(low_edge, 1, 0)
    rank = lax.rem(lon + SECTORS - first, SECTORS)
    eager = lax.rem(lat, STRIDE) < STRIDE // 2
    inwards = jnp.where(chip < 3, 2 * chip, 11 - 2 * chip)
    slot = jnp.where(eager, chip, inwards)
    starts = (
        jnp.where(main, 24 + 2 * lon, 4 * slot + 2 * core),
        jnp.where(main, 66 + 2 * lon, 48 + 3 * inwards + 2 * core),
    )
    order = slab_order(fields, rows)
    half = STRIDE // 2
    place_in_run = lax.rem(lat, STRIDE)
    far_north = jnp.logical_and(lax.rem(place_in_run, half) == 0, jnp.logical_not(low_edge))
    far_south = jnp.logical_and(lax.rem(place_in_run, half) == half - 1, jnp.logical_not(high_edge))
    upper = place_in_run >= half
    north_late = jnp.logical_or(
        jnp.logical_and(far_north, jnp.logical_not(upper)), jnp.logical_and(lat == 1, lon == 0)
    )
    south_late = jnp.logical_and(far_south, jnp.logical_not(upper))
    late_for_north = jnp.logical_and(far_north, upper)
    late_for_south = jnp.logical_or(
        jnp.logical_and(far_south, upper), jnp.logical_and(low_edge, lon == 0)
    )

    def ranked(t):
        return lax.rem(t + first, SECTORS)

    def turned(offset):
        return lax.rem(lon + offset, SECTORS)

    def greet(target):
        pl.semaphore_signal(barrier, inc=1, device_id=target, device_id_type=MESH)

    def waiter(ref, sem):
        return pltpu.make_async_copy(ref, ref, sem)

    def send(source, target, send_sem, recv_sem, device):
        pltpu.make_async_remote_copy(
            src_ref=source, dst_ref=target, send_sem=send_sem, recv_sem=recv_sem,
            device_id=device, device_id_type=MESH,
        ).start()

    loads = [
        pltpu.make_async_copy(q_hbm, q_in, load_sem.at[0]),
        pltpu.make_async_copy(u_hbm, u_in, load_sem.at[1]),
        pltpu.make_async_copy(v_hbm, v_in, load_sem.at[2]),
    ]
    for load in loads:
        load.start()
    tables = [
        pltpu.make_async_copy(source, target, table_sem.at[i])
        for i, (source, target) in enumerate(
            ((cut_hbm, cut_ref), (waves_hbm, waves_ref), (fh_hbm, fh), (fl_hbm, fl), (ih_hbm, ih), (il_hbm, il))
        )
    ]

    barrier = pltpu.get_barrier_semaphore()
    for target, pole, late in ((north, low_edge, late_for_north), (south, high_edge, late_for_south)):
        @pl.when(jnp.logical_not(jnp.logical_or(pole, late)))
        def _():
            greet(target)

    team_member = jnp.logical_or(main, helper)

    @pl.when(team_member)
    def _():
        for t in range(SECTORS):
            @pl.when(jnp.logical_or(t > rank, jnp.logical_and(t < rank, jnp.logical_not(eager))))
            def _():
                greet((lat, ranked(t)))

    @pl.when(jnp.logical_not(team_member))
    def _():
        greet(west)
        greet(east)

    @pl.when(helper)
    def _():
        greet((mate, lon))

    seen = jnp.where(eager, rank, SECTORS - 1)
    greeted = jnp.where(main, seen + 1, jnp.where(helper, seen, 2))
    for pole, late in ((low_edge, north_late), (high_edge, south_late)):
        greeted += jnp.where(jnp.logical_or(pole, late), 0, 1)
    pl.semaphore_wait(barrier, greeted)

    @pl.when(team_member)
    def _():
        for t in range(SECTORS - 1):
            @pl.when(jnp.logical_and(t < rank, eager))
            def _():
                pl.semaphore_signal(
                    hello.at[rank], inc=1, device_id=(lat, ranked(t)), device_id_type=MESH
                )

    for load in loads:
        load.wait()

    @pl.when(team_member)
    def _():
        for table in tables:
            table.start()

    sector = q_in.shape[-1]
    lane = lax.broadcasted_iota(jnp.int32, (16, LANES), 1)
    east_pack = jnp.zeros((16, LANES), jnp.float32)
    west_pack = jnp.zeros((16, LANES), jnp.float32)
    for f in range(fields + 1):
        for r in range(rows):
            s = f * rows + r
            source, pad = (q_in.at[f], q_pad.at[f]) if f < fields else (u_in, u_pad)
            pad[r, :, pl.ds(0, sector)] = source[r]
            x = pad[r]
            west_pack = jnp.where(lane == s, pltpu.roll(x, s, 1), west_pack)
            east_pack = jnp.where(
                lane == s, pltpu.roll(x, (s - (sector - 1)) % LANES, 1), east_pack
            )
    for r in range(rows):
        v_pad[r, :, pl.ds(0, sector)] = v_in[r]
    side_out[0] = west_pack
    side_out[1] = east_pack
    for side, row in ((0, 0), (1, rows - 1)):
        for f in range(fields):
            edge_out[side, f] = q_pad[f, row]
        edge_out[side, fields] = v_pad[row]

    def edge_copy(side, slot, target):
        return pltpu.make_async_remote_copy(
            src_ref=edge_out.at[side],
            dst_ref=edge_in.at[slot],
            send_sem=halo_send.at[side],
            recv_sem=halo_recv.at[slot],
            device_id=target,
            device_id_type=MESH,
        )

    to_north = edge_copy(0, jnp.where(low_edge, 0, 1), north)
    to_south = edge_copy(1, jnp.where(high_edge, 1, 0), south)
    to_west = pltpu.make_async_remote_copy(
        src_ref=side_out.at[0], dst_ref=side_in.at[1], send_sem=halo_send.at[2],
        recv_sem=halo_recv.at[2], device_id=west, device_id_type=MESH,
    )
    to_east = pltpu.make_async_remote_copy(
        src_ref=side_out.at[1], dst_ref=side_in.at[0], send_sem=halo_send.at[3],
        recv_sem=halo_recv.at[3], device_id=east, device_id_type=MESH,
    )
    for copy, pole, late in ((to_north, low_edge, north_late), (to_south, high_edge, south_late)):
        @pl.when(jnp.logical_not(jnp.logical_or(pole, late)))
        def _():
            copy.start()

    @pl.when(jnp.logical_not(team_member))
    def _():
        to_west.start()
        to_east.start()

    @pl.when(main)
    def _():
        @pl.when(rank > 0)
        def _():
            to_west.start()

        @pl.when(jnp.logical_and(rank < SECTORS - 1, eager))
        def _():
            pl.semaphore_wait(hello.at[rank + 1], 1)

        to_east.start()

        @pl.when(rank == 0)
        def _():
            @pl.when(eager)
            def _():
                pl.semaphore_wait(hello.at[SECTORS - 1], 1)

            to_west.start()

    def edges_arrive():
        edge_copy(0, 0, north).wait_recv()
        edge_copy(1, 1, south).wait_recv()
        for copy, late in ((to_north, north_late), (to_south, south_late)):
            @pl.when(late)
            def _():
                copy.start()

    ghosts = set()
    flip_north = jnp.where(low_edge, -1.0, 1.0)
    flip_south = jnp.where(high_edge, -1.0, 1.0)

    def set_ghosts(slabs):
        from_west, from_east = side_in[0], side_in[1]
        wanted = []
        for p in slabs:
            f, r = order[p]
            if (fields, r) not in ghosts:
                wanted.append((fields, r))
                ghosts.add((fields, r))
            wanted.append((f, r))
        for f, r in wanted:
            s = f * rows + r
            pad = q_pad.at[f] if f < fields else u_pad
            x = jnp.where(lane == sector, pltpu.roll(from_east, (sector - s) % LANES, 1), pad[r])
            pad[r] = jnp.where(lane == LANES - 1, pltpu.roll(from_west, (LANES - 1 - s) % LANES, 1), x)

    def step(slabs, winds):
        for p in slabs:
            f, r = order[p]
            if r not in winds:
                u = u_pad[r]
                v = v_pad[r]
                v_next = v_pad[r + 1] if r < rows - 1 else edge_in[1, fields] * flip_south
                v_previous = v_pad[r - 1] if r > 0 else edge_in[0, fields] * flip_north
                speeds = (
                    0.5 * (u + pltpu.roll(u, LANES - 1, 1)), 0.5 * (pltpu.roll(u, 1, 1) + u),
                    0.5 * (v + v_next), 0.5 * (v_previous + v),
                )
                winds[r] = [(jnp.maximum(x, 0.0), jnp.minimum(x, 0.0)) for x in speeds]
            (e_plus, e_minus), (w_plus, w_minus), (s_plus, s_minus), (n_plus, n_minus) = winds[r]
            q = q_pad[f, r]
            q_next = q_pad[f, r + 1] if r < rows - 1 else edge_in[1, f]
            q_previous = q_pad[f, r - 1] if r > 0 else edge_in[0, f]
            east_flux = e_plus * q + e_minus * pltpu.roll(q, LANES - 1, 1)
            west_flux = w_plus * pltpu.roll(q, 1, 1) + w_minus * q
            south_flux = s_plus * q + s_minus * q_next
            north_flux = n_plus * q_previous + n_minus * q
            new = q - (east_flux - west_flux) - (south_flux - north_flux)
            new = jnp.where(lane < sector, new, 0.0)
            stepped[2 * p] = new[:8]
            stepped[2 * p + 1] = new[8:]

    def hand_out(source):
        for p, (f, r) in enumerate(order):
            out_ref[f, r] = source[pl.ds(2 * p, 2)].reshape(16, LANES)[:, :sector]

    @pl.when(main)
    def _():
        tables[0].wait()
        for r in range(rows):
            limit = jnp.full((1, LANES), cut_ref[r], jnp.int32).astype(jnp.float32)
            cut_out[pl.ds(r, 1)] = limit
            cut_rows[pl.ds(r, 1)] = limit
        cut_out[pl.ds(rows, 16 - rows)] = jnp.zeros((16 - rows, LANES), jnp.float32)
        send(cut_out, cut_rows, cut_send, cut_recv, (mate, lon))

    @pl.when(helper)
    def _():
        for phase in range(2):
            for group in range(3):
                count = (8, 6)[phase]
                chunk = relay.at[pl.ds(24 * phase + count * group, count)]
                waiter(chunk, relay_recv.at[3 * phase + group]).wait()
                for place, c in ((0, 0), (0, 1), (1, 0), (1, 1)):
                    to = 2 * (5 - group if place else group) + c
                    if phase == 0:
                        to = jnp.where(eager, 2 * (2 * group + place) + c, to)
                    n = 2 - phase * c
                    at = 24 * phase + count * group + count // 2 * place + 2 * c

                    if phase == 0:
                        @pl.when(jnp.logical_and(to > rank, eager))
                        def _():
                            pl.semaphore_wait(hello.at[to], 1)

                    @pl.when(lon != to)
                    def _():
                        send(
                            relay.at[pl.ds(at, n)], land.at[lon, pl.ds(2 * phase, n)],
                            go_send.at[phase], go_recv.at[phase], (lat, to),
                        )

                    @pl.when(lon == to)
                    def _():
                        land[lon, pl.ds(2 * phase, n)] = relay[pl.ds(at, n)]

        to_west.start()
        to_east.start()

    def sides_arrive():
        to_west.wait_recv()
        to_east.wait_recv()

    @pl.when(main)
    def _():
        winds = {}
        ghosts.clear()
        sides_arrive()

        def for_helper(phase):
            for group in range(3):
                count = (8, 6)[phase]
                at = 48 * phase + count * group
                step(range(at // 2, (at + count) // 2), winds)
                send(
                    stepped.at[pl.ds(at, count)], relay.at[pl.ds(24 * phase + count * group, count)],
                    relay_send, relay_recv.at[3 * phase + group], (mate, lon),
                )

        def for_line(phase):
            at = (24, 66)[phase]
            for t, offset in enumerate((0,) + OFFSETS):
                to = turned(offset)
                if phase == 0:
                    to = jnp.where(eager, ranked(t), to)
                    waits = jnp.logical_and(t > rank + 1, jnp.logical_or(rank > 0, t < SECTORS - 1))

                    @pl.when(jnp.logical_and(waits, eager))
                    def _():
                        pl.semaphore_wait(hello.at[t], 1)

                    for copy, pole in ((to_north, low_edge), (to_south, high_edge)):
                        @pl.when(jnp.logical_and(pole, to == across))
                        def _():
                            copy.start()

                @pl.when(to != lon)
                def _():
                    send(
                        stepped.at[pl.ds(at + 2 * to, 2)], land.at[lon, pl.ds(2 * phase, 2)],
                        go_send.at[phase], go_recv.at[phase], (lat, to),
                    )
            land[lon, pl.ds(2 * phase, 2)] = stepped[pl.ds(at + 2 * lon, 2)]

        set_ghosts(range(24))
        for_helper(0)
        step(range(12, 24), winds)
        for_line(0)
        set_ghosts(range(24, 45))
        for_helper(1)
        step(range(33, 35), winds)
        edges_arrive()
        step(range(35, 45), winds)
        for_line(1)

    @pl.when(helper)
    def _():
        waiter(cut_rows, cut_recv).wait()
        tables[0].wait()

    @pl.when(jnp.logical_or(main, helper))
    def _():
        short = jnp.logical_and(helper, core == 1)
        for table in tables[1:]:
            table.wait()
        for phase in range(2):
            for n in range(1, 3) if phase else (2,):
                @pl.when(short == (n == 1) if phase else core >= 0)
                def _():
                    waiter(land.at[pl.ds(0, 11), pl.ds(0, n)], go_recv.at[phase]).wait()
            x = [land[j, pl.ds(2 * phase, 2)].reshape(16, LANES) for j in range(SECTORS)]
            limits = []
            for i in range(2):
                p = (starts[phase] + i) // 2
                row = 1 + p // fields
                row = jnp.where(p < fields * (rows - 1), jnp.where(row < rows - 1, row, 0), rows - 1)
                limit = jnp.broadcast_to(cut_rows[pl.ds(row, 1)], (8, LANES))
                limits.append(jnp.concatenate([limit, limit], axis=1))
            limits = jnp.concatenate(limits, axis=0)
            w = []
            for block, (a, b) in enumerate(sector_dft(x)):
                z = split_dot(jnp.concatenate([a, b], axis=1), fh[block], fl[block])
                wave = jnp.broadcast_to(waves_ref[pl.ds(block, 1)], (16, 256))
                z = jnp.where(wave <= limits, z, 0.0)
                y = split_dot(z, ih[block], il[block])
                w.append((y[:, :LANES], y[:, LANES:]))
            for j, y in enumerate(sector_inverse(w)):
                done[j, pl.ds(2 * phase, 2)] = y.reshape(2, 8, LANES)
            for n in range(1, 3) if phase else (2,):
                @pl.when(short == (n == 1) if phase else core >= 0)
                def _():
                    def back(to):
                        send(
                            done.at[to, pl.ds(2 * phase, n)], result.at[pl.ds(starts[phase], n)],
                            back_send.at[phase], back_recv.at[phase], (team, to),
                        )

                    for offset in OFFSETS:
                        back(turned(offset))

                    @pl.when(helper)
                    def _():
                        back(lon)

            @pl.when(main)
            def _():
                result[pl.ds(starts[phase], 2)] = done[lon, pl.ds(2 * phase, 2)]

    @pl.when(main)
    def _():
        waiter(result.at[pl.ds(0, 46)], back_recv.at[0]).wait()
        waiter(result.at[pl.ds(0, 40)], back_recv.at[1]).wait()
        hand_out(result)
        for phase in range(2):
            waiter(stepped.at[pl.ds(0, 22)], go_send.at[phase]).wait()
            waiter(stepped.at[pl.ds(0, 22)], back_send.at[phase]).wait()
        waiter(stepped.at[pl.ds(0, 42)], relay_send).wait()
        waiter(cut_out, cut_send).wait()

    @pl.when(helper)
    def _():
        waiter(stepped.at[pl.ds(0, 22)], go_send.at[0]).wait()
        waiter(stepped.at[pl.ds(0, 24)], back_send.at[0]).wait()
        for c in range(2):
            @pl.when(core == c)
            def _():
                waiter(stepped.at[pl.ds(0, 16 + c)], go_send.at[1]).wait()
                waiter(stepped.at[pl.ds(0, 24 - 12 * c)], back_send.at[1]).wait()

    @pl.when(jnp.logical_not(main))
    def _():
        ghosts.clear()
        sides_arrive()
        set_ghosts(range(len(order)))
        edges_arrive()
        step(range(len(order)), {})
        hand_out(stepped)

    for copy in (to_north, to_south, to_west, to_east):
        copy.wait_send()


def body(lat_count, tracers, zonal_wind, meridional_wind, cutoff):
    fields, levels, rows, sector = tracers.shape
    q = jnp.transpose(tracers, (0, 2, 1, 3))
    u = jnp.transpose(zonal_wind, (1, 0, 2))
    v = jnp.transpose(meridional_wind, (1, 0, 2))
    tables = [jnp.asarray(t) for t in dft_tables(SECTORS * sector, sector)]
    tiles = fields * rows * 2
    f32, bf16 = jnp.float32, jnp.bfloat16
    dma = pltpu.SemaphoreType.DMA
    hbm = pl.BlockSpec(memory_space=pltpu.HBM)
    vmem = pl.BlockSpec(memory_space=pltpu.VMEM)
    out = pl.pallas_call(
        functools.partial(kernel, lat_count, fields, rows),
        out_shape=jax.ShapeDtypeStruct((fields, rows, levels, sector), f32),
        in_specs=[hbm] * 9,
        out_specs=vmem,
        scratch_shapes=[
            pltpu.VMEM((fields, rows, levels, sector), f32),
            pltpu.VMEM((rows, levels, sector), f32),
            pltpu.VMEM((rows, levels, sector), f32),
            pltpu.VMEM((fields, rows, levels, LANES), f32),
            pltpu.VMEM((rows, levels, LANES), f32),
            pltpu.VMEM((rows, levels, LANES), f32),
            pltpu.VMEM((2, fields + 1, levels, LANES), f32),
            pltpu.VMEM((2, fields + 1, levels, LANES), f32),
            pltpu.VMEM((2, levels, LANES), f32),
            pltpu.VMEM((2, levels, LANES), f32),
            pltpu.VMEM((6, 256, 256), bf16),
            pltpu.VMEM((6, 256, 256), bf16),
            pltpu.VMEM((6, 256, 256), bf16),
            pltpu.VMEM((6, 256, 256), bf16),
            pltpu.VMEM((8, 256), f32),
            pltpu.SMEM((rows,), jnp.int32),
            pltpu.VMEM((16, LANES), f32),
            pltpu.VMEM((16, LANES), f32),
            pltpu.VMEM((tiles, 8, LANES), f32),
            pltpu.VMEM((42, 8, LANES), f32),
            pltpu.VMEM((SECTORS, 4, 8, LANES), f32),
            pltpu.VMEM((SECTORS, 4, 8, LANES), f32),
            pltpu.VMEM((tiles, 8, LANES), f32),
            dma((3,)), dma((6,)), dma((4,)), dma((4,)), dma, dma, dma, dma((6,)), pltpu.SemaphoreType.REGULAR((SECTORS,)),
            dma((2,)), dma((2,)), dma((2,)), dma((2,)),
        ],
        compiler_params=pltpu.CompilerParams(
            collective_id=0, has_side_effects=True, vmem_limit_bytes=60 * 1024 * 1024
        ),
    )(q, u, v, cutoff, *tables)
    return jnp.transpose(out, (0, 2, 1, 3))


def solution(mesh):
    in_specs = (P(None, None, "lat", "lon"), P(None, "lat", "lon"), P(None, "lat", "lon"), P("lat"))
    out_specs = P(None, None, "lat", "lon")
    return jax.shard_map(
        functools.partial(body, mesh.shape["lat"]),
        mesh=mesh, in_specs=in_specs, out_specs=out_specs, check_vma=False,
    )
```

```python
import functools
import math

import jax
import jax.numpy as jnp
import ml_dtypes
import numpy as np
from jax import lax
from jax.experimental import pallas as pl
from jax.experimental.pallas import tpu as pltpu
from jax.sharding import PartitionSpec as P

MESH = pl.DeviceIdType.MESH
POLAR_ROWS = 96
SECTORS = 12
LANES = 128
STRIDE = 16
OFFSETS = (1, 11, 2, 10, 3, 9, 4, 8, 5, 7, 6)


def slab_order(fields, rows):
    order = [(f, r) for r in range(1, rows - 1) for f in range(fields)]
    return order + [(f, r) for r in (0, rows - 1) for f in range(fields)]


def split_bf16(table):
    high = table.astype(ml_dtypes.bfloat16)
    low = (table - high.astype(np.float64)).astype(ml_dtypes.bfloat16)
    return high, low


@functools.lru_cache(maxsize=None)
def dft_tables(circle, sector):
    forward = np.zeros((6, 256, 256))
    inverse = np.zeros((6, 256, 256))
    waves = np.zeros((8, 256))
    m = np.arange(sector)

    def put(block, column, k, part, weight, real_half):
        phase = 2.0 * math.pi * ((m * k) % circle) / circle
        cos, sin = np.cos(phase), np.sin(phase)
        waves[block, column] = min(k, circle - k)
        if real_half is not None:
            base = 128 * real_half
            row = cos if part == 0 else -sin
            forward[block, base : base + sector, column] = row
            inverse[block, column, base : base + sector] = weight * row / circle
            return
        if part == 0:
            forward[block, :sector, column] = cos
            forward[block, 128 : 128 + sector, column] = sin
            inverse[block, column, :sector] = weight * cos / circle
            inverse[block, column, 128 : 128 + sector] = weight * sin / circle
        else:
            forward[block, :sector, column] = -sin
            forward[block, 128 : 128 + sector, column] = cos
            inverse[block, column, :sector] = -weight * sin / circle
            inverse[block, column, 128 : 128 + sector] = weight * cos / circle

    half = sector // 2
    for q in range(half + 1):
        put(0, q, SECTORS * q, 0, 1.0 if q in (0, half) else 2.0, 0)
    for q in range(1, half):
        put(0, half + q, SECTORS * q, 1, 2.0, 0)
    for q in range(half):
        put(0, 128 + q, 6 + SECTORS * q, 0, 2.0, 1)
        put(0, 128 + half + q, 6 + SECTORS * q, 1, 2.0, 1)
    for r in range(1, 6):
        for q in range(sector):
            put(r, q, r + SECTORS * q, 0, 2.0, None)
            put(r, 128 + q, r + SECTORS * q, 1, 2.0, None)
    return split_bf16(forward) + split_bf16(inverse) + (waves.astype(np.float32),)


def combine(terms):
    groups = {}
    for coefficient, array in terms:
        size = round(abs(coefficient), 6)
        if size < 1e-6:
            continue
        groups.setdefault(size, []).append((coefficient, array))
    total = None
    for size in sorted(groups, reverse=True):
        part = None
        for coefficient, array in groups[size]:
            if part is None:
                part = array if coefficient > 0 else -array
            else:
                part = part + array if coefficient > 0 else part - array
        if size != 1.0:
            part = part * abs(groups[size][0][0])
        total = part if total is None else total + part
    return total


def cos12(i):
    return math.cos(2.0 * math.pi * (i % 12) / 12)


def sin12(i):
    return math.sin(2.0 * math.pi * (i % 12) / 12)


def sector_dft(x):
    sums = [None] + [x[j] + x[12 - j] for j in range(1, 6)]
    differences = [None] + [x[j] - x[12 - j] for j in range(1, 6)]
    real, imag = [], []
    for r in range(7):
        terms = [(1.0, x[0]), (1.0 if r % 2 == 0 else -1.0, x[6])]
        terms += [(cos12(j * r), sums[j]) for j in range(1, 6)]
        real.append(combine(terms))
        if 0 < r < 6:
            imag.append(combine([(-sin12(j * r), differences[j]) for j in range(1, 6)]))
        else:
            imag.append(None)
    return [(real[0], real[6])] + [(real[r], imag[r]) for r in range(1, 6)]


def sector_inverse(w):
    out = [None] * 12
    for j in range(7):
        terms = [(1.0, w[0][0]), (1.0 if j % 2 == 0 else -1.0, w[0][1])]
        terms += [(cos12(j * r), w[r][0]) for r in range(1, 6)]
        even = combine(terms)
        if j in (0, 6):
            out[j] = even
            continue
        odd = combine([(sin12(j * r), w[r][1]) for r in range(1, 6)])
        out[j] = even - odd
        out[12 - j] = even + odd
    return out


def split_dot(x, high, low):
    x_high = x.astype(jnp.bfloat16)
    x_low = (x - x_high.astype(jnp.float32)).astype(jnp.bfloat16)
    dot = functools.partial(jnp.dot, preferred_element_type=jnp.float32)
    return dot(x_high, high) + (dot(x_low, high) + dot(x_high, low))


def kernel(
    lat_count, fields, rows,
    q_hbm, u_hbm, v_hbm, cut_hbm, fh_hbm, fl_hbm, ih_hbm, il_hbm, waves_hbm,
    out_ref,
    q_in, u_in, v_in, q_pad, u_pad, v_pad, edge_out, edge_in, side_out, side_in, kept,
    fh, fl, ih, il, waves_ref, cut_ref, cut_out, cut_rows, stepped, relay, land, done, result,
    load_sem, table_sem, halo_send, halo_recv, kept_recv, cut_send, cut_recv, relay_send, relay_recv, hello, far_hello,
    go_send, go_recv, back_send, back_recv,
):
    lat, lon = lax.axis_index("lat"), lax.axis_index("lon")
    chip, core = lon // 2, lax.rem(lon, 2)
    tiles = 2 * fields * rows
    low_edge, high_edge = lat == 0, lat == lat_count - 1
    caps = -(-POLAR_ROWS // rows)
    in_north, in_south = lat < caps, lat >= lat_count - caps
    main = jnp.logical_or(in_north, in_south)
    helper = jnp.logical_or(
        jnp.logical_and(lat >= STRIDE, lat < STRIDE + caps),
        jnp.logical_and(lat >= lat_count - STRIDE - caps, lat < lat_count - STRIDE),
    )
    mate = jnp.where(jnp.logical_or(in_north, lat >= lat_count // 2), STRIDE, -STRIDE)
    mate = lat + jnp.where(in_south, -STRIDE, mate)
    team = jnp.where(main, lat, mate)
    across = lax.rem(lon + 6, SECTORS)
    north = (jnp.where(low_edge, 0, lat - 1), jnp.where(low_edge, across, lon))
    south = (jnp.where(high_edge, lat, lat + 1), jnp.where(high_edge, across, lon))
    west = (lat, lax.rem(lon + SECTORS - 1, SECTORS))
    east = (lat, lax.rem(lon + 1, SECTORS))
    first = jnp.where(low_edge, 1, 0)
    rank = lax.rem(lon + SECTORS - first, SECTORS)
    eager = lat >= 0
    inwards = jnp.where(chip < 3, 2 * chip, 11 - 2 * chip)
    slot = jnp.where(eager, chip, inwards)
    starts = (
        jnp.where(main, 24 + 2 * lon, 4 * slot + 2 * core),
        jnp.where(main, 66 + 2 * lon, 48 + 3 * inwards + 2 * core),
    )
    order = slab_order(fields, rows)
    half = STRIDE // 2
    place_in_run = lax.rem(lat, STRIDE)
    far_north = jnp.logical_and(lax.rem(place_in_run, half) == 0, jnp.logical_not(low_edge))
    far_south = jnp.logical_and(lax.rem(place_in_run, half) == half - 1, jnp.logical_not(high_edge))
    upper = place_in_run >= half
    north_late = jnp.logical_or(
        jnp.logical_and(far_north, jnp.logical_not(upper)), jnp.logical_and(lat == 1, lon == 0)
    )
    south_late = jnp.logical_and(far_south, jnp.logical_not(upper))
    late_for_north = jnp.logical_and(far_north, upper)
    late_for_south = jnp.logical_or(
        jnp.logical_and(far_south, upper), jnp.logical_and(low_edge, lon == 0)
    )

    def ranked(t):
        return lax.rem(t + first, SECTORS)

    def turned(offset):
        return lax.rem(lon + offset, SECTORS)

    def greet(target):
        pl.semaphore_signal(barrier, inc=1, device_id=target, device_id_type=MESH)

    def waiter(ref, sem):
        return pltpu.make_async_copy(ref, ref, sem)

    def send(source, target, send_sem, recv_sem, device):
        pltpu.make_async_remote_copy(
            src_ref=source, dst_ref=target, send_sem=send_sem, recv_sem=recv_sem,
            device_id=device, device_id_type=MESH,
        ).start()

    loads = [
        pltpu.make_async_copy(q_hbm, q_in, load_sem.at[0]),
        pltpu.make_async_copy(u_hbm, u_in, load_sem.at[1]),
        pltpu.make_async_copy(v_hbm, v_in, load_sem.at[2]),
    ]
    for load in loads:
        load.start()
    tables = [
        pltpu.make_async_copy(source, target, table_sem.at[i])
        for i, (source, target) in enumerate(
            ((cut_hbm, cut_ref), (waves_hbm, waves_ref), (fh_hbm, fh), (fl_hbm, fl), (ih_hbm, ih), (il_hbm, il))
        )
    ]

    barrier = pltpu.get_barrier_semaphore()
    for target, pole, late in ((north, low_edge, late_for_north), (south, high_edge, late_for_south)):
        @pl.when(jnp.logical_not(jnp.logical_or(pole, late)))
        def _():
            greet(target)

    team_member = jnp.logical_or(main, helper)

    @pl.when(team_member)
    def _():
        for t in range(SECTORS):
            @pl.when(jnp.logical_or(t > rank, jnp.logical_and(t < rank, jnp.logical_not(eager))))
            def _():
                greet((lat, ranked(t)))

    @pl.when(jnp.logical_not(team_member))
    def _():
        greet(west)
        greet(east)

    @pl.when(helper)
    def _():
        greet((mate, lon))

    seen = jnp.where(eager, rank, SECTORS - 1)
    greeted = jnp.where(main, seen + 1, jnp.where(helper, seen, 2))
    for pole, late in ((low_edge, north_late), (high_edge, south_late)):
        greeted += jnp.where(jnp.logical_or(pole, late), 0, 1)
    pl.semaphore_wait(barrier, greeted)

    for target, late in ((north, late_for_north), (south, late_for_south)):
        @pl.when(late)
        def _():
            pl.semaphore_signal(far_hello, inc=1, device_id=target, device_id_type=MESH)

    @pl.when(team_member)
    def _():
        for t in range(SECTORS - 1):
            @pl.when(jnp.logical_and(t < rank, eager))
            def _():
                pl.semaphore_signal(
                    hello.at[rank], inc=1, device_id=(lat, ranked(t)), device_id_type=MESH
                )

    for load in loads:
        load.wait()

    @pl.when(team_member)
    def _():
        for table in tables:
            table.start()

    sector = q_in.shape[-1]
    lane = lax.broadcasted_iota(jnp.int32, (16, LANES), 1)
    east_pack = jnp.zeros((16, LANES), jnp.float32)
    west_pack = jnp.zeros((16, LANES), jnp.float32)
    for f in range(fields + 1):
        for r in range(rows):
            s = f * rows + r
            source, pad = (q_in.at[f], q_pad.at[f]) if f < fields else (u_in, u_pad)
            pad[r, :, pl.ds(0, sector)] = source[r]
            x = pad[r]
            west_pack = jnp.where(lane == s, pltpu.roll(x, s, 1), west_pack)
            east_pack = jnp.where(
                lane == s, pltpu.roll(x, (s - (sector - 1)) % LANES, 1), east_pack
            )
    for r in range(rows):
        v_pad[r, :, pl.ds(0, sector)] = v_in[r]
    side_out[0] = west_pack
    side_out[1] = east_pack
    for side, row in ((0, 0), (1, rows - 1)):
        for f in range(fields):
            edge_out[side, f] = q_pad[f, row]
        edge_out[side, fields] = v_pad[row]

    def edge_copy(side, slot, target):
        return pltpu.make_async_remote_copy(
            src_ref=edge_out.at[side],
            dst_ref=edge_in.at[slot],
            send_sem=halo_send.at[side],
            recv_sem=halo_recv.at[slot],
            device_id=target,
            device_id_type=MESH,
        )

    to_north = edge_copy(0, jnp.where(low_edge, 0, 1), north)
    to_south = edge_copy(1, jnp.where(high_edge, 1, 0), south)
    to_west = pltpu.make_async_remote_copy(
        src_ref=side_out.at[0], dst_ref=side_in.at[1], send_sem=halo_send.at[2],
        recv_sem=halo_recv.at[2], device_id=west, device_id_type=MESH,
    )
    to_east = pltpu.make_async_remote_copy(
        src_ref=side_out.at[1], dst_ref=side_in.at[0], send_sem=halo_send.at[3],
        recv_sem=halo_recv.at[3], device_id=east, device_id_type=MESH,
    )
    for copy, pole, late in ((to_north, low_edge, north_late), (to_south, high_edge, south_late)):
        @pl.when(jnp.logical_not(jnp.logical_or(pole, late)))
        def _():
            copy.start()

    @pl.when(jnp.logical_not(team_member))
    def _():
        to_west.start()
        to_east.start()

    keeps = jnp.logical_and(low_edge, main)
    to_keeper = pltpu.make_async_remote_copy(
        src_ref=side_out.at[1], dst_ref=kept, send_sem=halo_send.at[3],
        recv_sem=kept_recv, device_id=(lat, 1), device_id_type=MESH,
    )
    from_keeper = pltpu.make_async_remote_copy(
        src_ref=kept, dst_ref=side_in.at[0], send_sem=halo_send.at[2],
        recv_sem=halo_recv.at[3], device_id=(lat, 0), device_id_type=MESH,
    )

    @pl.when(main)
    def _():
        to_kept = jnp.logical_and(keeps, lon == SECTORS - 1)

        @pl.when(jnp.logical_and(rank < SECTORS - 1, jnp.logical_not(to_kept)))
        def _():
            pl.semaphore_wait(hello.at[rank + 1], 1)

        @pl.when(jnp.logical_not(to_kept))
        def _():
            to_east.start()

        @pl.when(to_kept)
        def _():
            to_keeper.start()

        @pl.when(jnp.logical_and(keeps, lon == 1))
        def _():
            pl.semaphore_wait(hello.at[SECTORS - 1], 1)
            to_keeper.wait_recv()
            from_keeper.start()

    def edges_arrive():
        for copy, late in ((to_north, north_late), (to_south, south_late)):
            @pl.when(late)
            def _():
                pl.semaphore_wait(far_hello, 1)
                copy.start()

        edge_copy(0, 0, north).wait_recv()
        edge_copy(1, 1, south).wait_recv()

    ghosts = set()
    flip_north = jnp.where(low_edge, -1.0, 1.0)
    flip_south = jnp.where(high_edge, -1.0, 1.0)

    def set_ghosts(slabs, both):
        from_west = side_in[0]
        wanted = []
        for p in slabs:
            f, r = order[p]
            if (fields, r) not in ghosts:
                wanted.append((fields, r))
                ghosts.add((fields, r))
            wanted.append((f, r))
        for f, r in wanted:
            s = f * rows + r
            pad = q_pad.at[f] if f < fields else u_pad
            x = pad[r]
            if both:
                x = jnp.where(lane == sector, pltpu.roll(side_in[1], (sector - s) % LANES, 1), x)
            pad[r] = jnp.where(lane == LANES - 1, pltpu.roll(from_west, (LANES - 1 - s) % LANES, 1), x)

    def step(slabs, winds, whole=False):
        for p in slabs:
            f, r = order[p]
            if r not in winds:
                u = u_pad[r]
                v = v_pad[r]
                v_next = v_pad[r + 1] if r < rows - 1 else edge_in[1, fields] * flip_south
                v_previous = v_pad[r - 1] if r > 0 else edge_in[0, fields] * flip_north
                speeds = (
                    0.5 * (u + pltpu.roll(u, LANES - 1, 1)), 0.5 * (pltpu.roll(u, 1, 1) + u),
                    0.5 * (v + v_next), 0.5 * (v_previous + v),
                )
                winds[r] = [(jnp.maximum(x, 0.0), jnp.minimum(x, 0.0)) for x in speeds]
            (e_plus, e_minus), (w_plus, w_minus), (s_plus, s_minus), (n_plus, n_minus) = winds[r]
            q = q_pad[f, r]
            q_next = q_pad[f, r + 1] if r < rows - 1 else edge_in[1, f]
            q_previous = q_pad[f, r - 1] if r > 0 else edge_in[0, f]
            east_flux = e_plus * q + e_minus * pltpu.roll(q, LANES - 1, 1)
            west_flux = w_plus * pltpu.roll(q, 1, 1) + w_minus * q
            south_flux = s_plus * q + s_minus * q_next
            north_flux = n_plus * q_previous + n_minus * q
            rest = 0.0
            if not whole:
                east_flux = jnp.where(lane < sector - 1, east_flux, 0.0)
                rest = jnp.where(lane == LANES - 1, pltpu.roll(west_flux, LANES - 1, 1), 0.0)
            new = q - (east_flux - west_flux) - (south_flux - north_flux)
            new = jnp.where(lane < sector, new, rest)
            stepped[2 * p] = new[:8]
            stepped[2 * p + 1] = new[8:]

    def hand_out(source):
        for p, (f, r) in enumerate(order):
            out_ref[f, r] = source[pl.ds(2 * p, 2)].reshape(16, LANES)[:, :sector]

    @pl.when(main)
    def _():
        tables[0].wait()
        for r in range(rows):
            limit = jnp.full((1, LANES), cut_ref[r], jnp.int32).astype(jnp.float32)
            cut_out[pl.ds(r, 1)] = limit
            cut_rows[pl.ds(r, 1)] = limit
        cut_out[pl.ds(rows, 16 - rows)] = jnp.zeros((16 - rows, LANES), jnp.float32)
        send(cut_out, cut_rows, cut_send, cut_recv, (mate, lon))

    @pl.when(helper)
    def _():
        for phase in range(2):
            for group in range(3):
                count = (8, 6)[phase]
                if phase == 1 and group == 0:
                    waiter(stepped.at[pl.ds(0, 22)], go_send.at[0]).wait()
                chunk = relay.at[pl.ds(24 * phase + count * group, count)]
                waiter(chunk, relay_recv.at[3 * phase + group]).wait()
                for place, c in ((0, 0), (0, 1), (1, 0), (1, 1)):
                    to = 2 * (5 - group if place else group) + c
                    if phase == 0:
                        to = jnp.where(eager, 2 * (2 * group + place) + c, to)
                    n = 2 - phase * c
                    at = 24 * phase + count * group + count // 2 * place + 2 * c

                    if phase == 0:
                        @pl.when(jnp.logical_and(to > rank, eager))
                        def _():
                            pl.semaphore_wait(hello.at[to], 1)

                    @pl.when(lon != to)
                    def _():
                        send(
                            relay.at[pl.ds(at, n)], land.at[lon, pl.ds(2 * phase, n)],
                            go_send.at[phase], go_recv.at[phase], (lat, to),
                        )

                    @pl.when(lon == to)
                    def _():
                        land[lon, pl.ds(2 * phase, n)] = relay[pl.ds(at, n)]

        to_west.start()
        to_east.start()

    @pl.when(main)
    def _():
        winds = {}
        ghosts.clear()
        to_east.wait_recv()

        def for_helper(phase):
            for group in range(3):
                count = (8, 6)[phase]
                at = 48 * phase + count * group
                step(range(at // 2, (at + count) // 2), winds)
                send(
                    stepped.at[pl.ds(at, count)], relay.at[pl.ds(24 * phase + count * group, count)],
                    relay_send.at[phase], relay_recv.at[3 * phase + group], (mate, lon),
                )

        def for_line(phase):
            at = (24, 66)[phase]
            for t, offset in enumerate((0,) + OFFSETS):
                to = turned(offset)
                if phase == 0:
                    to = jnp.where(eager, ranked(t), to)
                    waits = t > rank + 1
                    if t == SECTORS - 1:
                        waits = jnp.logical_and(waits, jnp.logical_not(jnp.logical_and(keeps, lon == 1)))
                        waits = jnp.logical_or(waits, jnp.logical_and(keeps, lon == SECTORS - 1))

                    @pl.when(jnp.logical_and(waits, eager))
                    def _():
                        pl.semaphore_wait(hello.at[t], 1)

                    for copy, pole in ((to_north, low_edge), (to_south, high_edge)):
                        @pl.when(jnp.logical_and(pole, to == across))
                        def _():
                            copy.start()

                @pl.when(to != lon)
                def _():
                    send(
                        stepped.at[pl.ds(at + 2 * to, 2)], land.at[lon, pl.ds(2 * phase, 2)],
                        go_send.at[phase], go_recv.at[phase], (lat, to),
                    )
            land[lon, pl.ds(2 * phase, 2)] = stepped[pl.ds(at + 2 * lon, 2)]

        set_ghosts(range(24), False)
        for_helper(0)
        step(range(12, 24), winds)
        for_line(0)
        set_ghosts(range(24, 45), False)
        waiter(stepped.at[pl.ds(0, 24)], relay_send.at[0]).wait()
        for_helper(1)
        step(range(33, 35), winds)
        edges_arrive()
        step(range(35, 45), winds)
        waiter(stepped.at[pl.ds(0, 22)], go_send.at[0]).wait()
        for_line(1)

    @pl.when(helper)
    def _():
        waiter(cut_rows, cut_recv).wait()
        tables[0].wait()

    @pl.when(jnp.logical_or(main, helper))
    def _():
        short = jnp.logical_and(helper, core == 1)
        for table in tables[1:]:
            table.wait()
        for phase in range(2):
            for n in range(1, 3) if phase else (2,):
                @pl.when(short == (n == 1) if phase else core >= 0)
                def _():
                    waiter(land.at[pl.ds(0, 11), pl.ds(0, n)], go_recv.at[phase]).wait()
            x = [land[j, pl.ds(2 * phase, 2)].reshape(16, LANES) for j in range(SECTORS)]
            x = [
                jnp.where(lane < sector, x[j], 0.0)
                - jnp.where(lane == sector - 1, pltpu.roll(x[(j + 1) % SECTORS], sector, 1), 0.0)
                for j in range(SECTORS)
            ]
            limits = []
            for i in range(2):
                p = (starts[phase] + i) // 2
                row = 1 + p // fields
                row = jnp.where(p < fields * (rows - 1), jnp.where(row < rows - 1, row, 0), rows - 1)
                limit = jnp.broadcast_to(cut_rows[pl.ds(row, 1)], (8, LANES))
                limits.append(jnp.concatenate([limit, limit], axis=1))
            limits = jnp.concatenate(limits, axis=0)
            w = []
            for block, (a, b) in enumerate(sector_dft(x)):
                z = split_dot(jnp.concatenate([a, b], axis=1), fh[block], fl[block])
                wave = jnp.broadcast_to(waves_ref[pl.ds(block, 1)], (16, 256))
                z = jnp.where(wave <= limits, z, 0.0)
                y = split_dot(z, ih[block], il[block])
                w.append((y[:, :LANES], y[:, LANES:]))
            for j, y in enumerate(sector_inverse(w)):
                done[j, pl.ds(2 * phase, 2)] = y.reshape(2, 8, LANES)
            for n in range(1, 3) if phase else (2,):
                @pl.when(short == (n == 1) if phase else core >= 0)
                def _():
                    def back(to):
                        send(
                            done.at[to, pl.ds(2 * phase, n)], result.at[pl.ds(starts[phase], n)],
                            back_send.at[phase], back_recv.at[phase], (team, to),
                        )

                    for offset in OFFSETS:
                        back(turned(offset))

                    @pl.when(helper)
                    def _():
                        back(lon)

            @pl.when(main)
            def _():
                result[pl.ds(starts[phase], 2)] = done[lon, pl.ds(2 * phase, 2)]

    @pl.when(main)
    def _():
        waiter(result.at[pl.ds(0, 46)], back_recv.at[0]).wait()
        waiter(result.at[pl.ds(0, 40)], back_recv.at[1]).wait()
        hand_out(result)
        waiter(stepped.at[pl.ds(0, 22)], go_send.at[1]).wait()
        for phase in range(2):
            waiter(stepped.at[pl.ds(0, 22)], back_send.at[phase]).wait()
        waiter(stepped.at[pl.ds(0, 18)], relay_send.at[1]).wait()
        waiter(cut_out, cut_send).wait()

    @pl.when(helper)
    def _():
        waiter(stepped.at[pl.ds(0, 24)], back_send.at[0]).wait()
        for c in range(2):
            @pl.when(core == c)
            def _():
                waiter(stepped.at[pl.ds(0, 16 + c)], go_send.at[1]).wait()
                waiter(stepped.at[pl.ds(0, 24 - 12 * c)], back_send.at[1]).wait()

    @pl.when(jnp.logical_not(main))
    def _():
        ghosts.clear()
        to_west.wait_recv()
        to_east.wait_recv()
        set_ghosts(range(len(order)), True)
        edges_arrive()
        step(range(len(order)), {}, True)
        hand_out(stepped)

    for copy in (to_north, to_south, to_east):
        copy.wait_send()

    @pl.when(jnp.logical_or(jnp.logical_not(main), jnp.logical_and(keeps, lon == 1)))
    def _():
        to_west.wait_send()


def body(lat_count, tracers, zonal_wind, meridional_wind, cutoff):
    fields, levels, rows, sector = tracers.shape
    q = jnp.transpose(tracers, (0, 2, 1, 3))
    u = jnp.transpose(zonal_wind, (1, 0, 2))
    v = jnp.transpose(meridional_wind, (1, 0, 2))
    tables = [jnp.asarray(t) for t in dft_tables(SECTORS * sector, sector)]
    tiles = fields * rows * 2
    f32, bf16 = jnp.float32, jnp.bfloat16
    dma = pltpu.SemaphoreType.DMA
    hbm = pl.BlockSpec(memory_space=pltpu.HBM)
    vmem = pl.BlockSpec(memory_space=pltpu.VMEM)
    out = pl.pallas_call(
        functools.partial(kernel, lat_count, fields, rows),
        out_shape=jax.ShapeDtypeStruct((fields, rows, levels, sector), f32),
        in_specs=[hbm] * 9,
        out_specs=vmem,
        scratch_shapes=[
            pltpu.VMEM((fields, rows, levels, sector), f32),
            pltpu.VMEM((rows, levels, sector), f32),
            pltpu.VMEM((rows, levels, sector), f32),
            pltpu.VMEM((fields, rows, levels, LANES), f32),
            pltpu.VMEM((rows, levels, LANES), f32),
            pltpu.VMEM((rows, levels, LANES), f32),
            pltpu.VMEM((2, fields + 1, levels, LANES), f32),
            pltpu.VMEM((2, fields + 1, levels, LANES), f32),
            pltpu.VMEM((2, levels, LANES), f32),
            pltpu.VMEM((2, levels, LANES), f32),
            pltpu.VMEM((levels, LANES), f32),
            pltpu.VMEM((6, 256, 256), bf16),
            pltpu.VMEM((6, 256, 256), bf16),
            pltpu.VMEM((6, 256, 256), bf16),
            pltpu.VMEM((6, 256, 256), bf16),
            pltpu.VMEM((8, 256), f32),
            pltpu.SMEM((rows,), jnp.int32),
            pltpu.VMEM((16, LANES), f32),
            pltpu.VMEM((16, LANES), f32),
            pltpu.VMEM((tiles, 8, LANES), f32),
            pltpu.VMEM((42, 8, LANES), f32),
            pltpu.VMEM((SECTORS, 4, 8, LANES), f32),
            pltpu.VMEM((SECTORS, 4, 8, LANES), f32),
            pltpu.VMEM((tiles, 8, LANES), f32),
            dma((3,)), dma((6,)), dma((4,)), dma((4,)), dma, dma, dma, dma((2,)), dma((6,)), pltpu.SemaphoreType.REGULAR((SECTORS,)),
            pltpu.SemaphoreType.REGULAR,
            dma((2,)), dma((2,)), dma((2,)), dma((2,)),
        ],
        compiler_params=pltpu.CompilerParams(
            collective_id=0, has_side_effects=True, vmem_limit_bytes=60 * 1024 * 1024
        ),
    )(q, u, v, cutoff, *tables)
    return jnp.transpose(out, (0, 2, 1, 3))


def solution(mesh):
    in_specs = (P(None, None, "lat", "lon"), P(None, "lat", "lon"), P(None, "lat", "lon"), P("lat"))
    out_specs = P(None, None, "lat", "lon")
    return jax.shard_map(
        functools.partial(body, mesh.shape["lat"]),
        mesh=mesh, in_specs=in_specs, out_specs=out_specs, check_vma=False,
    )
```

```python
import functools
import math

import jax
import jax.numpy as jnp
import ml_dtypes
import numpy as np
from jax import lax
from jax.experimental import pallas as pl
from jax.experimental.pallas import tpu as pltpu
from jax.sharding import PartitionSpec as P

MESH = pl.DeviceIdType.MESH
POLAR_ROWS = 96
SECTORS = 12
LANES = 128
STRIDE = 16
OFFSETS = (1, 11, 2, 10, 3, 9, 4, 8, 5, 7, 6)


def slab_order(fields, rows):
    order = [(f, r) for r in range(1, rows - 1) for f in range(fields)]
    return order + [(f, r) for r in (0, rows - 1) for f in range(fields)]


def split_bf16(table):
    high = table.astype(ml_dtypes.bfloat16)
    low = (table - high.astype(np.float64)).astype(ml_dtypes.bfloat16)
    return high, low


@functools.lru_cache(maxsize=None)
def dft_tables(circle, sector):
    forward = np.zeros((6, 256, 256))
    inverse = np.zeros((6, 256, 256))
    waves = np.zeros((8, 256))
    m = np.arange(sector)

    def put(block, column, k, part, weight, real_half):
        phase = 2.0 * math.pi * ((m * k) % circle) / circle
        cos, sin = np.cos(phase), np.sin(phase)
        waves[block, column] = min(k, circle - k)
        if real_half is not None:
            base = 128 * real_half
            row = cos if part == 0 else -sin
            forward[block, base : base + sector, column] = row
            inverse[block, column, base : base + sector] = weight * row / circle
            return
        if part == 0:
            forward[block, :sector, column] = cos
            forward[block, 128 : 128 + sector, column] = sin
            inverse[block, column, :sector] = weight * cos / circle
            inverse[block, column, 128 : 128 + sector] = weight * sin / circle
        else:
            forward[block, :sector, column] = -sin
            forward[block, 128 : 128 + sector, column] = cos
            inverse[block, column, :sector] = -weight * sin / circle
            inverse[block, column, 128 : 128 + sector] = weight * cos / circle

    half = sector // 2
    for q in range(half + 1):
        put(0, q, SECTORS * q, 0, 1.0 if q in (0, half) else 2.0, 0)
    for q in range(1, half):
        put(0, half + q, SECTORS * q, 1, 2.0, 0)
    for q in range(half):
        put(0, 128 + q, 6 + SECTORS * q, 0, 2.0, 1)
        put(0, 128 + half + q, 6 + SECTORS * q, 1, 2.0, 1)
    for r in range(1, 6):
        for q in range(sector):
            put(r, q, r + SECTORS * q, 0, 2.0, None)
            put(r, 128 + q, r + SECTORS * q, 1, 2.0, None)
    return split_bf16(forward) + split_bf16(inverse) + (waves.astype(np.float32),)


def combine(terms):
    groups = {}
    for coefficient, array in terms:
        size = round(abs(coefficient), 6)
        if size < 1e-6:
            continue
        groups.setdefault(size, []).append((coefficient, array))
    total = None
    for size in sorted(groups, reverse=True):
        part = None
        for coefficient, array in groups[size]:
            if part is None:
                part = array if coefficient > 0 else -array
            else:
                part = part + array if coefficient > 0 else part - array
        if size != 1.0:
            part = part * abs(groups[size][0][0])
        total = part if total is None else total + part
    return total


def cos12(i):
    return math.cos(2.0 * math.pi * (i % 12) / 12)


def sin12(i):
    return math.sin(2.0 * math.pi * (i % 12) / 12)


def sector_dft(x):
    sums = [None] + [x[j] + x[12 - j] for j in range(1, 6)]
    differences = [None] + [x[j] - x[12 - j] for j in range(1, 6)]
    real, imag = [], []
    for r in range(7):
        terms = [(1.0, x[0]), (1.0 if r % 2 == 0 else -1.0, x[6])]
        terms += [(cos12(j * r), sums[j]) for j in range(1, 6)]
        real.append(combine(terms))
        if 0 < r < 6:
            imag.append(combine([(-sin12(j * r), differences[j]) for j in range(1, 6)]))
        else:
            imag.append(None)
    return [(real[0], real[6])] + [(real[r], imag[r]) for r in range(1, 6)]


def sector_inverse(w):
    out = [None] * 12
    for j in range(7):
        terms = [(1.0, w[0][0]), (1.0 if j % 2 == 0 else -1.0, w[0][1])]
        terms += [(cos12(j * r), w[r][0]) for r in range(1, 6)]
        even = combine(terms)
        if j in (0, 6):
            out[j] = even
            continue
        odd = combine([(sin12(j * r), w[r][1]) for r in range(1, 6)])
        out[j] = even - odd
        out[12 - j] = even + odd
    return out


def split_dot(x, high, low):
    x_high = x.astype(jnp.bfloat16)
    x_low = (x - x_high.astype(jnp.float32)).astype(jnp.bfloat16)
    dot = functools.partial(jnp.dot, preferred_element_type=jnp.float32)
    count = x.shape[0]
    both = dot(jnp.concatenate([x_high, x_low], axis=0), high)
    return both[:count] + (both[count:] + dot(x_high, low))


def kernel(
    lat_count, fields, rows,
    q_hbm, u_hbm, v_hbm, cut_hbm, fh_hbm, fl_hbm, ih_hbm, il_hbm, waves_hbm,
    out_ref,
    q_in, u_in, v_in, q_pad, u_pad, v_pad, edge_out, edge_in, side_out, side_in, kept,
    fh, fl, ih, il, waves_ref, cut_ref, cut_out, cut_rows, stepped, relay, land, done, result,
    load_sem, table_sem, halo_send, halo_recv, kept_recv, cut_send, cut_recv, relay_send, relay_recv, hello, far_hello,
    go_send, go_recv, back_send, back_recv,
):
    lat, lon = lax.axis_index("lat"), lax.axis_index("lon")
    chip, core = lon // 2, lax.rem(lon, 2)
    tiles = 2 * fields * rows
    low_edge, high_edge = lat == 0, lat == lat_count - 1
    caps = -(-POLAR_ROWS // rows)
    in_north, in_south = lat < caps, lat >= lat_count - caps
    main = jnp.logical_or(in_north, in_south)
    helper = jnp.logical_or(
        jnp.logical_and(lat >= STRIDE, lat < STRIDE + caps),
        jnp.logical_and(lat >= lat_count - STRIDE - caps, lat < lat_count - STRIDE),
    )
    mate = jnp.where(jnp.logical_or(in_north, lat >= lat_count // 2), STRIDE, -STRIDE)
    mate = lat + jnp.where(in_south, -STRIDE, mate)
    team = jnp.where(main, lat, mate)
    across = lax.rem(lon + 6, SECTORS)
    north = (jnp.where(low_edge, 0, lat - 1), jnp.where(low_edge, across, lon))
    south = (jnp.where(high_edge, lat, lat + 1), jnp.where(high_edge, across, lon))
    west = (lat, lax.rem(lon + SECTORS - 1, SECTORS))
    east = (lat, lax.rem(lon + 1, SECTORS))
    first = jnp.where(low_edge, 1, 0)
    rank = lax.rem(lon + SECTORS - first, SECTORS)
    eager = lat >= 0
    inwards = jnp.where(chip < 3, 2 * chip, 11 - 2 * chip)
    slot = jnp.where(eager, chip, inwards)
    starts = (
        jnp.where(main, 24 + 2 * lon, 4 * slot + 2 * core),
        jnp.where(main, 66 + 2 * lon, 48 + 3 * inwards + 2 * core),
    )
    order = slab_order(fields, rows)
    half = STRIDE // 2
    place_in_run = lax.rem(lat, STRIDE)
    far_north = jnp.logical_and(lax.rem(place_in_run, half) == 0, jnp.logical_not(low_edge))
    far_south = jnp.logical_and(lax.rem(place_in_run, half) == half - 1, jnp.logical_not(high_edge))
    upper = place_in_run >= half
    north_late = jnp.logical_or(
        jnp.logical_and(far_north, jnp.logical_not(upper)), jnp.logical_and(lat == 1, lon == 0)
    )
    south_late = jnp.logical_and(far_south, jnp.logical_not(upper))
    late_for_north = jnp.logical_and(far_north, upper)
    late_for_south = jnp.logical_or(
        jnp.logical_and(far_south, upper), jnp.logical_and(low_edge, lon == 0)
    )

    def ranked(t):
        return lax.rem(t + first, SECTORS)

    def turned(offset):
        return lax.rem(lon + offset, SECTORS)

    def greet(target):
        pl.semaphore_signal(barrier, inc=1, device_id=target, device_id_type=MESH)

    def waiter(ref, sem):
        return pltpu.make_async_copy(ref, ref, sem)

    def send(source, target, send_sem, recv_sem, device):
        pltpu.make_async_remote_copy(
            src_ref=source, dst_ref=target, send_sem=send_sem, recv_sem=recv_sem,
            device_id=device, device_id_type=MESH,
        ).start()

    loads = [
        pltpu.make_async_copy(q_hbm, q_in, load_sem.at[0]),
        pltpu.make_async_copy(u_hbm, u_in, load_sem.at[1]),
        pltpu.make_async_copy(v_hbm, v_in, load_sem.at[2]),
    ]
    for load in loads:
        load.start()
    tables = [
        pltpu.make_async_copy(source, target, table_sem.at[i])
        for i, (source, target) in enumerate(
            ((cut_hbm, cut_ref), (waves_hbm, waves_ref), (fh_hbm, fh), (fl_hbm, fl), (ih_hbm, ih), (il_hbm, il))
        )
    ]

    barrier = pltpu.get_barrier_semaphore()
    for target, pole, late in ((north, low_edge, late_for_north), (south, high_edge, late_for_south)):
        @pl.when(jnp.logical_not(jnp.logical_or(pole, late)))
        def _():
            greet(target)

    team_member = jnp.logical_or(main, helper)

    @pl.when(team_member)
    def _():
        for t in range(SECTORS):
            @pl.when(jnp.logical_or(t > rank, jnp.logical_and(t < rank, jnp.logical_not(eager))))
            def _():
                greet((lat, ranked(t)))

    @pl.when(jnp.logical_not(team_member))
    def _():
        greet(west)
        greet(east)

    @pl.when(helper)
    def _():
        greet((mate, lon))

    seen = jnp.where(eager, rank, SECTORS - 1)
    greeted = jnp.where(main, seen + 1, jnp.where(helper, seen, 2))
    for pole, late in ((low_edge, north_late), (high_edge, south_late)):
        greeted += jnp.where(jnp.logical_or(pole, late), 0, 1)
    pl.semaphore_wait(barrier, greeted)

    for target, late in ((north, late_for_north), (south, late_for_south)):
        @pl.when(late)
        def _():
            pl.semaphore_signal(far_hello, inc=1, device_id=target, device_id_type=MESH)

    @pl.when(team_member)
    def _():
        for t in range(SECTORS - 1):
            @pl.when(jnp.logical_and(t < rank, eager))
            def _():
                pl.semaphore_signal(
                    hello.at[rank], inc=1, device_id=(lat, ranked(t)), device_id_type=MESH
                )

    for load in loads:
        load.wait()

    @pl.when(team_member)
    def _():
        for table in tables:
            table.start()

    sector = q_in.shape[-1]
    lane = lax.broadcasted_iota(jnp.int32, (16, LANES), 1)
    for f in range(fields):
        for r in range(rows):
            q_pad[f, r, :, pl.ds(0, sector)] = q_in[f, r]
    for r in range(rows):
        u_pad[r, :, pl.ds(0, sector)] = u_in[r]
        v_pad[r, :, pl.ds(0, sector)] = v_in[r]
    for side, row in ((0, 0), (1, rows - 1)):
        for f in range(fields):
            edge_out[side, f] = q_pad[f, row]
        edge_out[side, fields] = v_pad[row]

    def edge_copy(side, slot, target):
        return pltpu.make_async_remote_copy(
            src_ref=edge_out.at[side],
            dst_ref=edge_in.at[slot],
            send_sem=halo_send.at[side],
            recv_sem=halo_recv.at[slot],
            device_id=target,
            device_id_type=MESH,
        )

    to_north = edge_copy(0, jnp.where(low_edge, 0, 1), north)
    to_south = edge_copy(1, jnp.where(high_edge, 1, 0), south)
    to_west = pltpu.make_async_remote_copy(
        src_ref=side_out.at[0], dst_ref=side_in.at[1], send_sem=halo_send.at[2],
        recv_sem=halo_recv.at[2], device_id=west, device_id_type=MESH,
    )
    to_east = pltpu.make_async_remote_copy(
        src_ref=side_out.at[1], dst_ref=side_in.at[0], send_sem=halo_send.at[3],
        recv_sem=halo_recv.at[3], device_id=east, device_id_type=MESH,
    )
    known = rank >= SECTORS // 2
    for copy, pole, late in ((to_north, low_edge, north_late), (to_south, high_edge, south_late)):
        @pl.when(jnp.where(pole, known, jnp.logical_not(late)))
        def _():
            copy.start()

    east_pack = jnp.zeros((16, LANES), jnp.float32)
    west_pack = jnp.zeros((16, LANES), jnp.float32)
    for f in range(fields + 1):
        for r in range(rows):
            s = f * rows + r
            x = q_pad[f, r] if f < fields else u_pad[r]
            west_pack = jnp.where(lane == s, pltpu.roll(x, s, 1), west_pack)
            east_pack = jnp.where(
                lane == s, pltpu.roll(x, (s - (sector - 1)) % LANES, 1), east_pack
            )
    side_out[0] = west_pack
    side_out[1] = east_pack

    @pl.when(jnp.logical_not(team_member))
    def _():
        to_west.start()
        to_east.start()

    keeps = jnp.logical_and(low_edge, main)
    to_keeper = pltpu.make_async_remote_copy(
        src_ref=side_out.at[1], dst_ref=kept, send_sem=halo_send.at[3],
        recv_sem=kept_recv, device_id=(lat, 1), device_id_type=MESH,
    )
    from_keeper = pltpu.make_async_remote_copy(
        src_ref=kept, dst_ref=side_in.at[0], send_sem=halo_send.at[2],
        recv_sem=halo_recv.at[3], device_id=(lat, 0), device_id_type=MESH,
    )

    @pl.when(main)
    def _():
        to_kept = jnp.logical_and(keeps, lon == SECTORS - 1)

        @pl.when(jnp.logical_and(rank < SECTORS - 1, jnp.logical_not(to_kept)))
        def _():
            pl.semaphore_wait(hello.at[rank + 1], 1)

        @pl.when(jnp.logical_not(to_kept))
        def _():
            to_east.start()

        @pl.when(to_kept)
        def _():
            to_keeper.start()

        @pl.when(jnp.logical_and(keeps, lon == 1))
        def _():
            pl.semaphore_wait(hello.at[SECTORS - 1], 1)
            to_keeper.wait_recv()
            from_keeper.start()

    def edges_arrive():
        for copy, late in ((to_north, north_late), (to_south, south_late)):
            @pl.when(late)
            def _():
                pl.semaphore_wait(far_hello, 1)
                copy.start()

        edge_copy(0, 0, north).wait_recv()
        edge_copy(1, 1, south).wait_recv()

    ghosts = set()
    flip_north = jnp.where(low_edge, -1.0, 1.0)
    flip_south = jnp.where(high_edge, -1.0, 1.0)

    def set_ghosts(slabs, both):
        from_west = side_in[0]
        wanted = []
        for p in slabs:
            f, r = order[p]
            if (fields, r) not in ghosts:
                wanted.append((fields, r))
                ghosts.add((fields, r))
            wanted.append((f, r))
        for f, r in wanted:
            s = f * rows + r
            pad = q_pad.at[f] if f < fields else u_pad
            x = pad[r]
            if both:
                x = jnp.where(lane == sector, pltpu.roll(side_in[1], (sector - s) % LANES, 1), x)
            pad[r] = jnp.where(lane == LANES - 1, pltpu.roll(from_west, (LANES - 1 - s) % LANES, 1), x)

    def step(slabs, winds, whole=False):
        for p in slabs:
            f, r = order[p]
            if r not in winds:
                u = u_pad[r]
                v = v_pad[r]
                v_next = v_pad[r + 1] if r < rows - 1 else edge_in[1, fields] * flip_south
                v_previous = v_pad[r - 1] if r > 0 else edge_in[0, fields] * flip_north
                speeds = (
                    0.5 * (u + pltpu.roll(u, LANES - 1, 1)), 0.5 * (pltpu.roll(u, 1, 1) + u),
                    0.5 * (v + v_next), 0.5 * (v_previous + v),
                )
                winds[r] = [(jnp.maximum(x, 0.0), jnp.minimum(x, 0.0)) for x in speeds]
            (e_plus, e_minus), (w_plus, w_minus), (s_plus, s_minus), (n_plus, n_minus) = winds[r]
            q = q_pad[f, r]
            q_next = q_pad[f, r + 1] if r < rows - 1 else edge_in[1, f]
            q_previous = q_pad[f, r - 1] if r > 0 else edge_in[0, f]
            east_flux = e_plus * q + e_minus * pltpu.roll(q, LANES - 1, 1)
            west_flux = w_plus * pltpu.roll(q, 1, 1) + w_minus * q
            south_flux = s_plus * q + s_minus * q_next
            north_flux = n_plus * q_previous + n_minus * q
            rest = 0.0
            if not whole:
                east_flux = jnp.where(lane < sector - 1, east_flux, 0.0)
                rest = jnp.where(lane == LANES - 1, pltpu.roll(west_flux, LANES - 1, 1), 0.0)
            new = q - (east_flux - west_flux) - (south_flux - north_flux)
            new = jnp.where(lane < sector, new, rest)
            stepped[2 * p] = new[:8]
            stepped[2 * p + 1] = new[8:]

    def hand_out(source):
        for p, (f, r) in enumerate(order):
            out_ref[f, r] = source[pl.ds(2 * p, 2)].reshape(16, LANES)[:, :sector]

    @pl.when(main)
    def _():
        tables[0].wait()
        for r in range(rows):
            limit = jnp.full((1, LANES), cut_ref[r], jnp.int32).astype(jnp.float32)
            cut_out[pl.ds(r, 1)] = limit
            cut_rows[pl.ds(r, 1)] = limit
        cut_out[pl.ds(rows, 16 - rows)] = jnp.zeros((16 - rows, LANES), jnp.float32)
        send(cut_out, cut_rows, cut_send, cut_recv, (mate, lon))

    @pl.when(helper)
    def _():
        for phase in range(2):
            for group in range(3):
                count = (8, 6)[phase]
                if phase == 1 and group == 0:
                    waiter(stepped.at[pl.ds(0, 22)], go_send.at[0]).wait()
                chunk = relay.at[pl.ds(24 * phase + count * group, count)]
                waiter(chunk, relay_recv.at[3 * phase + group]).wait()
                for place, c in ((0, 0), (0, 1), (1, 0), (1, 1)):
                    to = 2 * (5 - group if place else group) + c
                    if phase == 0:
                        to = jnp.where(eager, 2 * (2 * group + place) + c, to)
                    n = 2 - phase * c
                    at = 24 * phase + count * group + count // 2 * place + 2 * c

                    if phase == 0:
                        @pl.when(jnp.logical_and(to > rank, eager))
                        def _():
                            pl.semaphore_wait(hello.at[to], 1)

                    @pl.when(lon != to)
                    def _():
                        send(
                            relay.at[pl.ds(at, n)], land.at[lon, pl.ds(2 * phase, n)],
                            go_send.at[phase], go_recv.at[phase], (lat, to),
                        )

                    @pl.when(lon == to)
                    def _():
                        land[lon, pl.ds(2 * phase, n)] = relay[pl.ds(at, n)]

        to_west.start()
        to_east.start()

    @pl.when(main)
    def _():
        winds = {}
        ghosts.clear()
        to_east.wait_recv()

        def for_helper(phase):
            for group in range(3):
                count = (8, 6)[phase]
                at = 48 * phase + count * group
                step(range(at // 2, (at + count) // 2), winds)
                send(
                    stepped.at[pl.ds(at, count)], relay.at[pl.ds(24 * phase + count * group, count)],
                    relay_send.at[phase], relay_recv.at[3 * phase + group], (mate, lon),
                )

        def for_line(phase):
            at = (24, 66)[phase]
            for t, offset in enumerate((0,) + OFFSETS):
                to = turned(offset)
                if phase == 0:
                    to = jnp.where(eager, ranked(t), to)
                    waits = t > rank + 1
                    if t == SECTORS - 1:
                        waits = jnp.logical_and(waits, jnp.logical_not(jnp.logical_and(keeps, lon == 1)))
                        waits = jnp.logical_or(waits, jnp.logical_and(keeps, lon == SECTORS - 1))

                    @pl.when(jnp.logical_and(waits, eager))
                    def _():
                        pl.semaphore_wait(hello.at[t], 1)

                    for copy, pole in ((to_north, low_edge), (to_south, high_edge)):
                        @pl.when(jnp.logical_and(pole, jnp.logical_and(to == across, jnp.logical_not(known))))
                        def _():
                            copy.start()

                @pl.when(to != lon)
                def _():
                    send(
                        stepped.at[pl.ds(at + 2 * to, 2)], land.at[lon, pl.ds(2 * phase, 2)],
                        go_send.at[phase], go_recv.at[phase], (lat, to),
                    )
            land[lon, pl.ds(2 * phase, 2)] = stepped[pl.ds(at + 2 * lon, 2)]

        set_ghosts(range(24), False)
        for_helper(0)
        step(range(12, 24), winds)
        for_line(0)
        set_ghosts(range(24, 45), False)
        waiter(stepped.at[pl.ds(0, 24)], relay_send.at[0]).wait()
        for_helper(1)
        step(range(33, 35), winds)
        edges_arrive()
        step(range(35, 45), winds)
        waiter(stepped.at[pl.ds(0, 22)], go_send.at[0]).wait()
        for_line(1)

    @pl.when(helper)
    def _():
        waiter(cut_rows, cut_recv).wait()
        tables[0].wait()

    @pl.when(jnp.logical_or(main, helper))
    def _():
        short = jnp.logical_and(helper, core == 1)
        for table in tables[1:]:
            table.wait()
        for phase in range(2):
            for n in range(1, 3) if phase else (2,):
                @pl.when(short == (n == 1) if phase else core >= 0)
                def _():
                    waiter(land.at[pl.ds(0, 11), pl.ds(0, n)], go_recv.at[phase]).wait()
            x = [land[j, pl.ds(2 * phase, 2)].reshape(16, LANES) for j in range(SECTORS)]
            x = [
                jnp.where(lane < sector, x[j], 0.0)
                - jnp.where(lane == sector - 1, pltpu.roll(x[(j + 1) % SECTORS], sector, 1), 0.0)
                for j in range(SECTORS)
            ]
            limits = []
            for i in range(2):
                p = (starts[phase] + i) // 2
                row = 1 + p // fields
                row = jnp.where(p < fields * (rows - 1), jnp.where(row < rows - 1, row, 0), rows - 1)
                limit = jnp.broadcast_to(cut_rows[pl.ds(row, 1)], (8, LANES))
                limits.append(jnp.concatenate([limit, limit], axis=1))
            limits = jnp.concatenate(limits, axis=0)
            w = []
            for block, (a, b) in enumerate(sector_dft(x)):
                z = split_dot(jnp.concatenate([a, b], axis=1), fh[block], fl[block])
                wave = jnp.broadcast_to(waves_ref[pl.ds(block, 1)], (16, 256))
                z = jnp.where(wave <= limits, z, 0.0)
                y = split_dot(z, ih[block], il[block])
                w.append((y[:, :LANES], y[:, LANES:]))
            for j, y in enumerate(sector_inverse(w)):
                done[j, pl.ds(2 * phase, 2)] = y.reshape(2, 8, LANES)
            for n in range(1, 3) if phase else (2,):
                @pl.when(short == (n == 1) if phase else core >= 0)
                def _():
                    def back(to):
                        send(
                            done.at[to, pl.ds(2 * phase, n)], result.at[pl.ds(starts[phase], n)],
                            back_send.at[phase], back_recv.at[phase], (team, to),
                        )

                    for t in range(SECTORS):
                        to = lax.rem(t + jnp.where(team == 0, 1, 0), SECTORS)

                        @pl.when(jnp.logical_or(helper, to != lon))
                        def _():
                            back(to)

            @pl.when(main)
            def _():
                result[pl.ds(starts[phase], 2)] = done[lon, pl.ds(2 * phase, 2)]

    @pl.when(main)
    def _():
        waiter(result.at[pl.ds(0, 46)], back_recv.at[0]).wait()
        waiter(result.at[pl.ds(0, 40)], back_recv.at[1]).wait()
        hand_out(result)
        waiter(stepped.at[pl.ds(0, 22)], go_send.at[1]).wait()
        for phase in range(2):
            waiter(stepped.at[pl.ds(0, 22)], back_send.at[phase]).wait()
        waiter(stepped.at[pl.ds(0, 18)], relay_send.at[1]).wait()
        waiter(cut_out, cut_send).wait()

    @pl.when(helper)
    def _():
        waiter(stepped.at[pl.ds(0, 24)], back_send.at[0]).wait()
        for c in range(2):
            @pl.when(core == c)
            def _():
                waiter(stepped.at[pl.ds(0, 16 + c)], go_send.at[1]).wait()
                waiter(stepped.at[pl.ds(0, 24 - 12 * c)], back_send.at[1]).wait()

    @pl.when(jnp.logical_not(main))
    def _():
        ghosts.clear()
        to_west.wait_recv()
        to_east.wait_recv()
        set_ghosts(range(len(order)), True)
        edges_arrive()
        step(range(len(order)), {}, True)
        hand_out(stepped)

    for copy in (to_north, to_south, to_east):
        copy.wait_send()

    @pl.when(jnp.logical_or(jnp.logical_not(main), jnp.logical_and(keeps, lon == 1)))
    def _():
        to_west.wait_send()


def body(lat_count, tracers, zonal_wind, meridional_wind, cutoff):
    fields, levels, rows, sector = tracers.shape
    q = jnp.transpose(tracers, (0, 2, 1, 3))
    u = jnp.transpose(zonal_wind, (1, 0, 2))
    v = jnp.transpose(meridional_wind, (1, 0, 2))
    tables = [jnp.asarray(t) for t in dft_tables(SECTORS * sector, sector)]
    tiles = fields * rows * 2
    f32, bf16 = jnp.float32, jnp.bfloat16
    dma = pltpu.SemaphoreType.DMA
    hbm = pl.BlockSpec(memory_space=pltpu.HBM)
    vmem = pl.BlockSpec(memory_space=pltpu.VMEM)
    out = pl.pallas_call(
        functools.partial(kernel, lat_count, fields, rows),
        out_shape=jax.ShapeDtypeStruct((fields, rows, levels, sector), f32),
        in_specs=[hbm] * 9,
        out_specs=vmem,
        scratch_shapes=[
            pltpu.VMEM((fields, rows, levels, sector), f32),
            pltpu.VMEM((rows, levels, sector), f32),
            pltpu.VMEM((rows, levels, sector), f32),
            pltpu.VMEM((fields, rows, levels, LANES), f32),
            pltpu.VMEM((rows, levels, LANES), f32),
            pltpu.VMEM((rows, levels, LANES), f32),
            pltpu.VMEM((2, fields + 1, levels, LANES), f32),
            pltpu.VMEM((2, fields + 1, levels, LANES), f32),
            pltpu.VMEM((2, levels, LANES), f32),
            pltpu.VMEM((2, levels, LANES), f32),
            pltpu.VMEM((levels, LANES), f32),
            pltpu.VMEM((6, 256, 256), bf16),
            pltpu.VMEM((6, 256, 256), bf16),
            pltpu.VMEM((6, 256, 256), bf16),
            pltpu.VMEM((6, 256, 256), bf16),
            pltpu.VMEM((8, 256), f32),
            pltpu.SMEM((rows,), jnp.int32),
            pltpu.VMEM((16, LANES), f32),
            pltpu.VMEM((16, LANES), f32),
            pltpu.VMEM((tiles, 8, LANES), f32),
            pltpu.VMEM((42, 8, LANES), f32),
            pltpu.VMEM((SECTORS, 4, 8, LANES), f32),
            pltpu.VMEM((SECTORS, 4, 8, LANES), f32),
            pltpu.VMEM((tiles, 8, LANES), f32),
            dma((3,)), dma((6,)), dma((4,)), dma((4,)), dma, dma, dma, dma((2,)), dma((6,)), pltpu.SemaphoreType.REGULAR((SECTORS,)),
            pltpu.SemaphoreType.REGULAR,
            dma((2,)), dma((2,)), dma((2,)), dma((2,)),
        ],
        compiler_params=pltpu.CompilerParams(
            collective_id=0, has_side_effects=True, vmem_limit_bytes=60 * 1024 * 1024
        ),
    )(q, u, v, cutoff, *tables)
    return jnp.transpose(out, (0, 2, 1, 3))


def solution(mesh):
    in_specs = (P(None, None, "lat", "lon"), P(None, "lat", "lon"), P(None, "lat", "lon"), P("lat"))
    out_specs = P(None, None, "lat", "lon")
    return jax.shard_map(
        functools.partial(body, mesh.shape["lat"]),
        mesh=mesh, in_specs=in_specs, out_specs=out_specs, check_vma=False,
    )
```

```python
import functools
import math

import jax
import jax.numpy as jnp
import ml_dtypes
import numpy as np
from jax import lax
from jax.experimental import pallas as pl
from jax.experimental.pallas import tpu as pltpu
from jax.sharding import PartitionSpec as P

MESH = pl.DeviceIdType.MESH
POLAR_ROWS = 96
SECTORS = 12
LANES = 128
STRIDE = 16
OFFSETS = (1, 11, 2, 10, 3, 9, 4, 8, 5, 7, 6)


def slab_order(fields, rows):
    order = [(f, r) for r in range(1, rows - 1) for f in range(fields)]
    return order + [(f, r) for r in (0, rows - 1) for f in range(fields)]


def split_bf16(table):
    high = table.astype(ml_dtypes.bfloat16)
    low = (table - high.astype(np.float64)).astype(ml_dtypes.bfloat16)
    return high, low


@functools.lru_cache(maxsize=None)
def dft_tables(circle, sector):
    forward = np.zeros((6, 256, 256))
    inverse = np.zeros((6, 256, 256))
    waves = np.zeros((8, 256))
    m = np.arange(sector)

    def put(block, column, k, part, weight, real_half):
        phase = 2.0 * math.pi * ((m * k) % circle) / circle
        cos, sin = np.cos(phase), np.sin(phase)
        waves[block, column] = min(k, circle - k)
        if real_half is not None:
            base = 128 * real_half
            row = cos if part == 0 else -sin
            forward[block, base : base + sector, column] = row
            inverse[block, column, base : base + sector] = weight * row / circle
            return
        if part == 0:
            forward[block, :sector, column] = cos
            forward[block, 128 : 128 + sector, column] = sin
            inverse[block, column, :sector] = weight * cos / circle
            inverse[block, column, 128 : 128 + sector] = weight * sin / circle
        else:
            forward[block, :sector, column] = -sin
            forward[block, 128 : 128 + sector, column] = cos
            inverse[block, column, :sector] = -weight * sin / circle
            inverse[block, column, 128 : 128 + sector] = weight * cos / circle

    half = sector // 2
    for q in range(half + 1):
        put(0, q, SECTORS * q, 0, 1.0 if q in (0, half) else 2.0, 0)
    for q in range(1, half):
        put(0, half + q, SECTORS * q, 1, 2.0, 0)
    for q in range(half):
        put(0, 128 + q, 6 + SECTORS * q, 0, 2.0, 1)
        put(0, 128 + half + q, 6 + SECTORS * q, 1, 2.0, 1)
    for r in range(1, 6):
        for q in range(sector):
            put(r, q, r + SECTORS * q, 0, 2.0, None)
            put(r, 128 + q, r + SECTORS * q, 1, 2.0, None)
    return split_bf16(forward) + split_bf16(inverse) + (waves.astype(np.float32),)


def combine(terms):
    groups = {}
    for coefficient, array in terms:
        size = round(abs(coefficient), 6)
        if size < 1e-6:
            continue
        groups.setdefault(size, []).append((coefficient, array))
    total = None
    for size in sorted(groups, reverse=True):
        part = None
        for coefficient, array in groups[size]:
            if part is None:
                part = array if coefficient > 0 else -array
            else:
                part = part + array if coefficient > 0 else part - array
        if size != 1.0:
            part = part * abs(groups[size][0][0])
        total = part if total is None else total + part
    return total


def cos12(i):
    return math.cos(2.0 * math.pi * (i % 12) / 12)


def sin12(i):
    return math.sin(2.0 * math.pi * (i % 12) / 12)


def sector_dft(x):
    sums = [None] + [x[j] + x[12 - j] for j in range(1, 6)]
    differences = [None] + [x[j] - x[12 - j] for j in range(1, 6)]
    real, imag = [], []
    for r in range(7):
        terms = [(1.0, x[0]), (1.0 if r % 2 == 0 else -1.0, x[6])]
        terms += [(cos12(j * r), sums[j]) for j in range(1, 6)]
        real.append(combine(terms))
        if 0 < r < 6:
            imag.append(combine([(-sin12(j * r), differences[j]) for j in range(1, 6)]))
        else:
            imag.append(None)
    return [(real[0], real[6])] + [(real[r], imag[r]) for r in range(1, 6)]


def sector_inverse(w):
    out = [None] * 12
    for j in range(7):
        terms = [(1.0, w[0][0]), (1.0 if j % 2 == 0 else -1.0, w[0][1])]
        terms += [(cos12(j * r), w[r][0]) for r in range(1, 6)]
        even = combine(terms)
        if j in (0, 6):
            out[j] = even
            continue
        odd = combine([(sin12(j * r), w[r][1]) for r in range(1, 6)])
        out[j] = even - odd
        out[12 - j] = even + odd
    return out


def split_dot(x, high, low):
    x_high = x.astype(jnp.bfloat16)
    x_low = (x - x_high.astype(jnp.float32)).astype(jnp.bfloat16)
    dot = functools.partial(jnp.dot, preferred_element_type=jnp.float32)
    count = x.shape[0]
    both = dot(jnp.concatenate([x_high, x_low], axis=0), high)
    return both[:count] + (both[count:] + dot(x_high, low))


def kernel(
    lat_count, fields, rows,
    q_hbm, u_hbm, v_hbm, cut_hbm, fh_hbm, fl_hbm, ih_hbm, il_hbm, waves_hbm,
    out_ref,
    q_in, u_in, v_in, q_pad, u_pad, v_pad, edge_out, edge_in, side_out, side_in, kept,
    fh, fl, ih, il, waves_ref, cut_ref, cut_out, cut_rows, stepped, relay, land, done, result,
    load_sem, table_sem, halo_send, halo_recv, kept_recv, cut_send, cut_recv, relay_send, relay_recv, hello, far_hello,
    go_send, go_recv, back_send, back_recv,
):
    lat, lon = lax.axis_index("lat"), lax.axis_index("lon")
    chip, core = lon // 2, lax.rem(lon, 2)
    tiles = 2 * fields * rows
    low_edge, high_edge = lat == 0, lat == lat_count - 1
    caps = -(-POLAR_ROWS // rows)
    in_north, in_south = lat < caps, lat >= lat_count - caps
    main = jnp.logical_or(in_north, in_south)
    helper = jnp.logical_or(
        jnp.logical_and(lat >= STRIDE, lat < STRIDE + caps),
        jnp.logical_and(lat >= lat_count - STRIDE - caps, lat < lat_count - STRIDE),
    )
    mate = jnp.where(jnp.logical_or(in_north, lat >= lat_count // 2), STRIDE, -STRIDE)
    mate = lat + jnp.where(in_south, -STRIDE, mate)
    team = jnp.where(main, lat, mate)
    across = lax.rem(lon + 6, SECTORS)
    north = (jnp.where(low_edge, 0, lat - 1), jnp.where(low_edge, across, lon))
    south = (jnp.where(high_edge, lat, lat + 1), jnp.where(high_edge, across, lon))
    west = (lat, lax.rem(lon + SECTORS - 1, SECTORS))
    east = (lat, lax.rem(lon + 1, SECTORS))
    first = jnp.where(low_edge, 1, 0)
    rank = lax.rem(lon + SECTORS - first, SECTORS)
    eager = lat >= 0
    inwards = jnp.where(chip < 3, 2 * chip, 11 - 2 * chip)
    slot = jnp.where(eager, chip, inwards)
    starts = (
        jnp.where(main, 24 + 2 * lon, 4 * slot + 2 * core),
        jnp.where(main, 66 + 2 * lon, 48 + 3 * inwards + 2 * core),
    )
    order = slab_order(fields, rows)
    half = STRIDE // 2
    place_in_run = lax.rem(lat, STRIDE)
    far_north = jnp.logical_and(lax.rem(place_in_run, half) == 0, jnp.logical_not(low_edge))
    far_south = jnp.logical_and(lax.rem(place_in_run, half) == half - 1, jnp.logical_not(high_edge))
    upper = place_in_run >= half
    north_late = jnp.logical_or(
        jnp.logical_and(far_north, jnp.logical_not(upper)), jnp.logical_and(lat == 1, lon == 0)
    )
    south_late = jnp.logical_and(far_south, jnp.logical_not(upper))
    late_for_north = jnp.logical_and(far_north, upper)
    late_for_south = jnp.logical_or(
        jnp.logical_and(far_south, upper), jnp.logical_and(low_edge, lon == 0)
    )

    def ranked(t):
        return lax.rem(t + first, SECTORS)

    def turned(offset):
        return lax.rem(lon + offset, SECTORS)

    def greet(target):
        pl.semaphore_signal(barrier, inc=1, device_id=target, device_id_type=MESH)

    def waiter(ref, sem):
        return pltpu.make_async_copy(ref, ref, sem)

    def send(source, target, send_sem, recv_sem, device):
        pltpu.make_async_remote_copy(
            src_ref=source, dst_ref=target, send_sem=send_sem, recv_sem=recv_sem,
            device_id=device, device_id_type=MESH,
        ).start()

    loads = [
        pltpu.make_async_copy(q_hbm, q_in, load_sem.at[0]),
        pltpu.make_async_copy(u_hbm, u_in, load_sem.at[1]),
        pltpu.make_async_copy(v_hbm, v_in, load_sem.at[2]),
    ]
    for load in loads:
        load.start()
    tables = [
        pltpu.make_async_copy(source, target, table_sem.at[i])
        for i, (source, target) in enumerate(
            ((cut_hbm, cut_ref), (waves_hbm, waves_ref), (fh_hbm, fh), (fl_hbm, fl), (ih_hbm, ih), (il_hbm, il))
        )
    ]

    barrier = pltpu.get_barrier_semaphore()
    for target, pole, late in ((north, low_edge, late_for_north), (south, high_edge, late_for_south)):
        @pl.when(jnp.logical_not(jnp.logical_or(pole, late)))
        def _():
            greet(target)

    team_member = jnp.logical_or(main, helper)

    @pl.when(team_member)
    def _():
        for t in range(SECTORS):
            @pl.when(jnp.logical_or(t > rank, jnp.logical_and(t < rank, jnp.logical_not(eager))))
            def _():
                greet((lat, ranked(t)))

    @pl.when(jnp.logical_not(team_member))
    def _():
        greet(west)
        greet(east)

    @pl.when(helper)
    def _():
        greet((mate, lon))

    seen = jnp.where(eager, rank, SECTORS - 1)
    greeted = jnp.where(main, seen + 1, jnp.where(helper, seen, 2))
    for pole, late in ((low_edge, north_late), (high_edge, south_late)):
        greeted += jnp.where(jnp.logical_or(pole, late), 0, 1)
    pl.semaphore_wait(barrier, greeted)

    for target, late in ((north, late_for_north), (south, late_for_south)):
        @pl.when(late)
        def _():
            pl.semaphore_signal(far_hello, inc=1, device_id=target, device_id_type=MESH)

    @pl.when(team_member)
    def _():
        for t in range(SECTORS - 1):
            @pl.when(jnp.logical_and(t < rank, eager))
            def _():
                pl.semaphore_signal(
                    hello.at[rank], inc=1, device_id=(lat, ranked(t)), device_id_type=MESH
                )

    for load in loads:
        load.wait()

    @pl.when(team_member)
    def _():
        for table in tables:
            table.start()

    sector = q_in.shape[-1]
    lane = lax.broadcasted_iota(jnp.int32, (16, LANES), 1)
    for f in range(fields):
        for r in range(rows):
            q_pad[f, r, :, pl.ds(0, sector)] = q_in[f, r]
    for r in range(rows):
        u_pad[r, :, pl.ds(0, sector)] = u_in[r]
        v_pad[r, :, pl.ds(0, sector)] = v_in[r]
    for side, row in ((0, 0), (1, rows - 1)):
        for f in range(fields):
            edge_out[side, f] = q_pad[f, row]
        edge_out[side, fields] = v_pad[row]

    def edge_copy(side, slot, target):
        return pltpu.make_async_remote_copy(
            src_ref=edge_out.at[side],
            dst_ref=edge_in.at[slot],
            send_sem=halo_send.at[side],
            recv_sem=halo_recv.at[slot],
            device_id=target,
            device_id_type=MESH,
        )

    to_north = edge_copy(0, jnp.where(low_edge, 0, 1), north)
    to_south = edge_copy(1, jnp.where(high_edge, 1, 0), south)
    to_west = pltpu.make_async_remote_copy(
        src_ref=side_out.at[0], dst_ref=side_in.at[1], send_sem=halo_send.at[2],
        recv_sem=halo_recv.at[2], device_id=west, device_id_type=MESH,
    )
    to_east = pltpu.make_async_remote_copy(
        src_ref=side_out.at[1], dst_ref=side_in.at[0], send_sem=halo_send.at[3],
        recv_sem=halo_recv.at[3], device_id=east, device_id_type=MESH,
    )
    known = rank >= SECTORS // 2
    for copy, pole, late in ((to_north, low_edge, north_late), (to_south, high_edge, south_late)):
        @pl.when(jnp.where(pole, known, jnp.logical_not(late)))
        def _():
            copy.start()

    east_pack = jnp.zeros((16, LANES), jnp.float32)
    west_pack = jnp.zeros((16, LANES), jnp.float32)
    for f in range(fields + 1):
        for r in range(rows):
            s = f * rows + r
            x = q_pad[f, r] if f < fields else u_pad[r]
            west_pack = jnp.where(lane == s, pltpu.roll(x, s, 1), west_pack)
            east_pack = jnp.where(
                lane == s, pltpu.roll(x, (s - (sector - 1)) % LANES, 1), east_pack
            )
    side_out[0] = west_pack
    side_out[1] = east_pack

    @pl.when(jnp.logical_not(team_member))
    def _():
        to_west.start()
        to_east.start()

    keeps = jnp.logical_and(low_edge, main)
    to_keeper = pltpu.make_async_remote_copy(
        src_ref=side_out.at[1], dst_ref=kept, send_sem=halo_send.at[3],
        recv_sem=kept_recv, device_id=(lat, 1), device_id_type=MESH,
    )
    from_keeper = pltpu.make_async_remote_copy(
        src_ref=kept, dst_ref=side_in.at[0], send_sem=halo_send.at[2],
        recv_sem=halo_recv.at[3], device_id=(lat, 0), device_id_type=MESH,
    )

    @pl.when(main)
    def _():
        to_kept = jnp.logical_and(keeps, lon == SECTORS - 1)

        @pl.when(jnp.logical_and(rank < SECTORS - 1, jnp.logical_not(to_kept)))
        def _():
            pl.semaphore_wait(hello.at[rank + 1], 1)

        @pl.when(jnp.logical_not(to_kept))
        def _():
            to_east.start()

        @pl.when(to_kept)
        def _():
            to_keeper.start()

        @pl.when(jnp.logical_and(keeps, lon == 1))
        def _():
            pl.semaphore_wait(hello.at[SECTORS - 1], 1)
            to_keeper.wait_recv()
            from_keeper.start()

    def edges_arrive():
        for copy, late in ((to_north, north_late), (to_south, south_late)):
            @pl.when(late)
            def _():
                pl.semaphore_wait(far_hello, 1)
                copy.start()

        edge_copy(0, 0, north).wait_recv()
        edge_copy(1, 1, south).wait_recv()

    ghosts = set()
    flip_north = jnp.where(low_edge, -1.0, 1.0)
    flip_south = jnp.where(high_edge, -1.0, 1.0)

    def set_ghosts(slabs, both):
        from_west = side_in[0]
        wanted = []
        for p in slabs:
            f, r = order[p]
            if (fields, r) not in ghosts:
                wanted.append((fields, r))
                ghosts.add((fields, r))
            wanted.append((f, r))
        for f, r in wanted:
            s = f * rows + r
            pad = q_pad.at[f] if f < fields else u_pad
            x = pad[r]
            if both:
                x = jnp.where(lane == sector, pltpu.roll(side_in[1], (sector - s) % LANES, 1), x)
            pad[r] = jnp.where(lane == LANES - 1, pltpu.roll(from_west, (LANES - 1 - s) % LANES, 1), x)

    def step(slabs, winds, whole=False):
        for p in slabs:
            f, r = order[p]
            if r not in winds:
                u = u_pad[r]
                v = v_pad[r]
                v_next = v_pad[r + 1] if r < rows - 1 else edge_in[1, fields] * flip_south
                v_previous = v_pad[r - 1] if r > 0 else edge_in[0, fields] * flip_north
                speeds = (
                    0.5 * (u + pltpu.roll(u, LANES - 1, 1)), 0.5 * (pltpu.roll(u, 1, 1) + u),
                    0.5 * (v + v_next), 0.5 * (v_previous + v),
                )
                winds[r] = [(jnp.maximum(x, 0.0), jnp.minimum(x, 0.0)) for x in speeds]
            (e_plus, e_minus), (w_plus, w_minus), (s_plus, s_minus), (n_plus, n_minus) = winds[r]
            q = q_pad[f, r]
            q_next = q_pad[f, r + 1] if r < rows - 1 else edge_in[1, f]
            q_previous = q_pad[f, r - 1] if r > 0 else edge_in[0, f]
            east_flux = e_plus * q + e_minus * pltpu.roll(q, LANES - 1, 1)
            west_flux = w_plus * pltpu.roll(q, 1, 1) + w_minus * q
            south_flux = s_plus * q + s_minus * q_next
            north_flux = n_plus * q_previous + n_minus * q
            rest = 0.0
            if not whole:
                east_flux = jnp.where(lane < sector - 1, east_flux, 0.0)
                rest = jnp.where(lane == LANES - 1, pltpu.roll(west_flux, LANES - 1, 1), 0.0)
            new = q - (east_flux - west_flux) - (south_flux - north_flux)
            new = jnp.where(lane < sector, new, rest)
            stepped[2 * p] = new[:8]
            stepped[2 * p + 1] = new[8:]

    def hand_out(source, places):
        for p in places:
            f, r = order[p]
            out_ref[f, r] = source[pl.ds(2 * p, 2)].reshape(16, LANES)[:, :sector]

    @pl.when(main)
    def _():
        tables[0].wait()
        for r in range(rows):
            limit = jnp.full((1, LANES), cut_ref[r], jnp.int32).astype(jnp.float32)
            cut_out[pl.ds(r, 1)] = limit
            cut_rows[pl.ds(r, 1)] = limit
        cut_out[pl.ds(rows, 16 - rows)] = jnp.zeros((16 - rows, LANES), jnp.float32)
        send(cut_out, cut_rows, cut_send, cut_recv, (mate, lon))

    @pl.when(helper)
    def _():
        for phase in range(2):
            for group in range(3):
                count = (8, 6)[phase]
                if phase == 1 and group == 0:
                    waiter(stepped.at[pl.ds(0, 22)], go_send.at[0]).wait()
                chunk = relay.at[pl.ds(24 * phase + count * group, count)]
                waiter(chunk, relay_recv.at[3 * phase + group]).wait()
                for place, c in ((0, 0), (0, 1), (1, 0), (1, 1)):
                    to = 2 * (5 - group if place else group) + c
                    if phase == 0:
                        to = jnp.where(eager, 2 * (2 * group + place) + c, to)
                    n = 2 - phase * c
                    at = 24 * phase + count * group + count // 2 * place + 2 * c

                    if phase == 0:
                        @pl.when(jnp.logical_and(to > rank, eager))
                        def _():
                            pl.semaphore_wait(hello.at[to], 1)

                    @pl.when(lon != to)
                    def _():
                        send(
                            relay.at[pl.ds(at, n)], land.at[lon, pl.ds(2 * phase, n)],
                            go_send.at[phase], go_recv.at[phase], (lat, to),
                        )

                    @pl.when(lon == to)
                    def _():
                        land[lon, pl.ds(2 * phase, n)] = relay[pl.ds(at, n)]

        to_west.start()
        to_east.start()

    @pl.when(main)
    def _():
        winds = {}
        ghosts.clear()
        to_east.wait_recv()

        def for_helper(phase):
            for group in range(3):
                count = (8, 6)[phase]
                at = 48 * phase + count * group
                step(range(at // 2, (at + count) // 2), winds)
                send(
                    stepped.at[pl.ds(at, count)], relay.at[pl.ds(24 * phase + count * group, count)],
                    relay_send.at[phase], relay_recv.at[3 * phase + group], (mate, lon),
                )

        def for_line(phase):
            at = (24, 66)[phase]
            for t, offset in enumerate((0,) + OFFSETS):
                to = turned(offset)
                if phase == 0:
                    to = jnp.where(eager, ranked(t), to)
                    waits = t > rank + 1
                    if t == SECTORS - 1:
                        waits = jnp.logical_and(waits, jnp.logical_not(jnp.logical_and(keeps, lon == 1)))
                        waits = jnp.logical_or(waits, jnp.logical_and(keeps, lon == SECTORS - 1))

                    @pl.when(jnp.logical_and(waits, eager))
                    def _():
                        pl.semaphore_wait(hello.at[t], 1)

                    for copy, pole in ((to_north, low_edge), (to_south, high_edge)):
                        @pl.when(jnp.logical_and(pole, jnp.logical_and(to == across, jnp.logical_not(known))))
                        def _():
                            copy.start()

                @pl.when(to != lon)
                def _():
                    send(
                        stepped.at[pl.ds(at + 2 * to, 2)], land.at[lon, pl.ds(2 * phase, 2)],
                        go_send.at[phase], go_recv.at[phase], (lat, to),
                    )
            land[lon, pl.ds(2 * phase, 2)] = stepped[pl.ds(at + 2 * lon, 2)]

        set_ghosts(range(24), False)
        for_helper(0)
        step(range(12, 24), winds)
        for_line(0)
        set_ghosts(range(24, 45), False)
        waiter(stepped.at[pl.ds(0, 24)], relay_send.at[0]).wait()
        for_helper(1)
        step(range(33, 35), winds)
        edges_arrive()
        step(range(35, 45), winds)
        waiter(stepped.at[pl.ds(0, 22)], go_send.at[0]).wait()
        for_line(1)

    @pl.when(helper)
    def _():
        waiter(cut_rows, cut_recv).wait()
        tables[0].wait()

    @pl.when(jnp.logical_or(main, helper))
    def _():
        short = jnp.logical_and(helper, core == 1)
        for table in tables[1:]:
            table.wait()
        for phase in range(2):
            for n in range(1, 3) if phase else (2,):
                @pl.when(short == (n == 1) if phase else core >= 0)
                def _():
                    waiter(land.at[pl.ds(0, 11), pl.ds(0, n)], go_recv.at[phase]).wait()
            x = [land[j, pl.ds(2 * phase, 2)].reshape(16, LANES) for j in range(SECTORS)]
            x = [
                jnp.where(lane < sector, x[j], 0.0)
                - jnp.where(lane == sector - 1, pltpu.roll(x[(j + 1) % SECTORS], sector, 1), 0.0)
                for j in range(SECTORS)
            ]
            limits = []
            for i in range(2):
                p = (starts[phase] + i) // 2
                row = 1 + p // fields
                row = jnp.where(p < fields * (rows - 1), jnp.where(row < rows - 1, row, 0), rows - 1)
                limit = jnp.broadcast_to(cut_rows[pl.ds(row, 1)], (8, LANES))
                limits.append(jnp.concatenate([limit, limit], axis=1))
            limits = jnp.concatenate(limits, axis=0)
            w = []
            for block, (a, b) in enumerate(sector_dft(x)):
                z = split_dot(jnp.concatenate([a, b], axis=1), fh[block], fl[block])
                wave = jnp.broadcast_to(waves_ref[pl.ds(block, 1)], (16, 256))
                z = jnp.where(wave <= limits, z, 0.0)
                y = split_dot(z, ih[block], il[block])
                w.append((y[:, :LANES], y[:, LANES:]))
            for j, y in enumerate(sector_inverse(w)):
                done[j, pl.ds(2 * phase, 2)] = y.reshape(2, 8, LANES)
            for n in range(1, 3) if phase else (2,):
                @pl.when(short == (n == 1) if phase else core >= 0)
                def _():
                    def back(to):
                        send(
                            done.at[to, pl.ds(2 * phase, n)], result.at[pl.ds(starts[phase], n)],
                            back_send.at[phase], back_recv.at[phase], (team, to),
                        )

                    for t in range(SECTORS):
                        to = lax.rem(t + jnp.where(team == 0, 1, 0), SECTORS)

                        @pl.when(jnp.logical_or(helper, to != lon))
                        def _():
                            back(to)

            @pl.when(main)
            def _():
                result[pl.ds(starts[phase], 2)] = done[lon, pl.ds(2 * phase, 2)]

    @pl.when(main)
    def _():
        waiter(result.at[pl.ds(0, 46)], back_recv.at[0]).wait()
        hand_out(result, range(24))
        waiter(result.at[pl.ds(0, 40)], back_recv.at[1]).wait()
        hand_out(result, range(24, 45))
        waiter(stepped.at[pl.ds(0, 22)], go_send.at[1]).wait()
        for phase in range(2):
            waiter(stepped.at[pl.ds(0, 22)], back_send.at[phase]).wait()
        waiter(stepped.at[pl.ds(0, 18)], relay_send.at[1]).wait()
        waiter(cut_out, cut_send).wait()

    @pl.when(helper)
    def _():
        waiter(stepped.at[pl.ds(0, 24)], back_send.at[0]).wait()
        for c in range(2):
            @pl.when(core == c)
            def _():
                waiter(stepped.at[pl.ds(0, 16 + c)], go_send.at[1]).wait()
                waiter(stepped.at[pl.ds(0, 24 - 12 * c)], back_send.at[1]).wait()

    @pl.when(jnp.logical_not(main))
    def _():
        ghosts.clear()
        to_west.wait_recv()
        to_east.wait_recv()
        set_ghosts(range(len(order)), True)
        edges_arrive()
        step(range(len(order)), {}, True)
        hand_out(stepped, range(len(order)))

    for copy in (to_north, to_south, to_east):
        copy.wait_send()

    @pl.when(jnp.logical_or(jnp.logical_not(main), jnp.logical_and(keeps, lon == 1)))
    def _():
        to_west.wait_send()


def body(lat_count, tracers, zonal_wind, meridional_wind, cutoff):
    fields, levels, rows, sector = tracers.shape
    q = jnp.transpose(tracers, (0, 2, 1, 3))
    u = jnp.transpose(zonal_wind, (1, 0, 2))
    v = jnp.transpose(meridional_wind, (1, 0, 2))
    tables = [jnp.asarray(t) for t in dft_tables(SECTORS * sector, sector)]
    tiles = fields * rows * 2
    f32, bf16 = jnp.float32, jnp.bfloat16
    dma = pltpu.SemaphoreType.DMA
    hbm = pl.BlockSpec(memory_space=pltpu.HBM)
    vmem = pl.BlockSpec(memory_space=pltpu.VMEM)
    out = pl.pallas_call(
        functools.partial(kernel, lat_count, fields, rows),
        out_shape=jax.ShapeDtypeStruct((fields, rows, levels, sector), f32),
        in_specs=[hbm] * 9,
        out_specs=vmem,
        scratch_shapes=[
            pltpu.VMEM((fields, rows, levels, sector), f32),
            pltpu.VMEM((rows, levels, sector), f32),
            pltpu.VMEM((rows, levels, sector), f32),
            pltpu.VMEM((fields, rows, levels, LANES), f32),
            pltpu.VMEM((rows, levels, LANES), f32),
            pltpu.VMEM((rows, levels, LANES), f32),
            pltpu.VMEM((2, fields + 1, levels, LANES), f32),
            pltpu.VMEM((2, fields + 1, levels, LANES), f32),
            pltpu.VMEM((2, levels, LANES), f32),
            pltpu.VMEM((2, levels, LANES), f32),
            pltpu.VMEM((levels, LANES), f32),
            pltpu.VMEM((6, 256, 256), bf16),
            pltpu.VMEM((6, 256, 256), bf16),
            pltpu.VMEM((6, 256, 256), bf16),
            pltpu.VMEM((6, 256, 256), bf16),
            pltpu.VMEM((8, 256), f32),
            pltpu.SMEM((rows,), jnp.int32),
            pltpu.VMEM((16, LANES), f32),
            pltpu.VMEM((16, LANES), f32),
            pltpu.VMEM((tiles, 8, LANES), f32),
            pltpu.VMEM((42, 8, LANES), f32),
            pltpu.VMEM((SECTORS, 4, 8, LANES), f32),
            pltpu.VMEM((SECTORS, 4, 8, LANES), f32),
            pltpu.VMEM((tiles, 8, LANES), f32),
            dma((3,)), dma((6,)), dma((4,)), dma((4,)), dma, dma, dma, dma((2,)), dma((6,)), pltpu.SemaphoreType.REGULAR((SECTORS,)),
            pltpu.SemaphoreType.REGULAR,
            dma((2,)), dma((2,)), dma((2,)), dma((2,)),
        ],
        compiler_params=pltpu.CompilerParams(
            collective_id=0, has_side_effects=True, vmem_limit_bytes=60 * 1024 * 1024
        ),
    )(q, u, v, cutoff, *tables)
    return jnp.transpose(out, (0, 2, 1, 3))


def solution(mesh):
    in_specs = (P(None, None, "lat", "lon"), P(None, "lat", "lon"), P(None, "lat", "lon"), P("lat"))
    out_specs = P(None, None, "lat", "lon")
    return jax.shard_map(
        functools.partial(body, mesh.shape["lat"]),
        mesh=mesh, in_specs=in_specs, out_specs=out_specs, check_vma=False,
    )
```
